32 devices in a mesh: dp: 16 (over z, x, core), tensor: 2 (over y).
Axes of the slice: x: 2, y: 2, z: 4, core: 2. Of those that a mesh axis runs over, the one named last changes fastest.
Arguments:
- block_in: bfloat16 [32768, 1024], P(('dp', 'tensor')), may hold values from -6 to 6
- ln1_scale: bfloat16 [1024], replicated, may hold values from 0.5 to 1.5
- ln1_shift: bfloat16 [1024], replicated, may hold values from -0.5 to 0.5
- qkv_weight: bfloat16 [1024, 3, 1024], P(None, None, 'tensor'), may hold values from -0.1875 to 0.1875
- qkv_bias: bfloat16 [3, 1024], P(None, 'tensor'), may hold values from -0.5 to 0.5
- out_weight: bfloat16 [1024, 1024], P('tensor'), may hold values from -1.5 to 1.5
- out_bias: bfloat16 [1024], replicated, may hold values from -1.5 to 1.5
- ln2_scale: bfloat16 [1024], replicated, may hold values from 0.5 to 1.5
- ln2_shift: bfloat16 [1024], replicated, may hold values from -0.5 to 0.5
- up_weight: bfloat16 [1024, 4096], P(None, 'tensor'), may hold values from -0.1875 to 0.1875
- up_bias: bfloat16 [4096], P('tensor'), may hold values from -1.5 to 1.5
- down_weight: bfloat16 [4096, 1024], P('tensor'), may hold values from -0.09375 to 0.09375
- down_bias: bfloat16 [1024], replicated, may hold values from -1.5 to 1.5
- out_grad: bfloat16 [32768, 1024], P(('dp', 'tensor')), may hold values from -6 to 6
Outputs:
- block_out: bfloat16 [32768, 1024], P(('dp', 'tensor'))
- in_grad: bfloat16 [32768, 1024], P(('dp', 'tensor'))
- ln1_scale_grad: float32 [1024], P('tensor')
- ln1_shift_grad: float32 [1024], P('tensor')
- qkv_weight_grad: float32 [1024, 3, 1024], P(None, None, 'tensor')
- qkv_bias_grad: float32 [3, 1024], P(None, 'tensor')
- out_weight_grad: float32 [1024, 1024], P('tensor')
- out_bias_grad: float32 [1024], P('tensor')
- ln2_scale_grad: float32 [1024], P('tensor')
- ln2_shift_grad: float32 [1024], P('tensor')
- up_weight_grad: float32 [1024, 4096], P(None, 'tensor')
- up_bias_grad: float32 [4096], P('tensor')
- down_weight_grad: float32 [4096, 1024], P('tensor')
- down_bias_grad: float32 [1024], P('tensor')
The draws below stay inside these ranges and needn't reach their ends.
All inputs are finite; a program needn't handle non-finite values.
Results may differ from the reference program's by a relative error of at most 0.02.
Values may be sent and summed in bfloat16 or wider, within the bound.
A program may use at most 320 MiB of HBM per device.

```python
import math
import jax
import jax.numpy as jnp
import numpy as np
from jax import lax

D = 1024
HEADS = 16
HD = 64
FF = 4096
GH = 16
GW = 16
CLIPS_DEV = 1
SEQ = 2048
TOK_GROUP = 2048
TOKENS = 32768
N_DP = 16


def block_levels(key, shape, pieces, smallest, top_value):
    def one(position, parts):
        steps = jax.random.uniform(jax.random.fold_in(jax.random.fold_in(key, 6), position), (parts,), jnp.float32, smallest / len(pieces), top_value / len(pieces))
        return jnp.repeat(jnp.exp(steps), shape[position] // parts).reshape((-1,) + (1,) * (len(shape) - position - 1))

    loudness = one(*pieces[0])
    for cut in pieces[1:]:
        loudness = loudness * one(*cut)
    return loudness


def normal_values(own_key, shape, deviation, most, split=(), held_as=jnp.bfloat16):
    gain = block_levels(own_key, shape, split, -0.22, 0.18) if split else 1.0
    array = jax.random.normal(own_key, shape, jnp.float32) * deviation * gain
    return jnp.minimum(jnp.maximum(array, -most), most).astype(held_as)


def setup_inputs(seed: int = 0) -> dict:
    arg_keys = jax.random.split(jax.random.key(seed), 15)
    return {
        "block_in": normal_values(arg_keys[0], (TOKENS, D), 1.0, 6.0, ((0, 32),)),
        "ln1_scale": jnp.clip(1.0 + 0.1 * jax.random.normal(arg_keys[1], (D,), jnp.float32), 0.5, 1.5).astype(jnp.bfloat16),
        "ln1_shift": normal_values(arg_keys[2], (D,), 0.1, 0.5),
        "qkv_weight": normal_values(arg_keys[3], (D, 3, D), D ** -0.5, 0.1875, ((2, 2),)),
        "qkv_bias": normal_values(arg_keys[4], (3, D), 0.1, 0.5, ((1, 2),)),
        "out_weight": normal_values(arg_keys[5], (D, D), 16 ** -0.5, 1.5, ((0, 2),)),
        "out_bias": normal_values(arg_keys[6], (D,), 0.3, 1.5),
        "ln2_scale": jnp.clip(1.0 + 0.1 * jax.random.normal(arg_keys[7], (D,), jnp.float32), 0.5, 1.5).astype(jnp.bfloat16),
        "ln2_shift": normal_values(arg_keys[8], (D,), 0.1, 0.5),
        "up_weight": normal_values(arg_keys[9], (D, FF), D ** -0.5, 0.1875, ((1, 2),)),
        "up_bias": normal_values(arg_keys[10], (FF,), 0.3, 1.5, ((0, 2),)),
        "down_weight": normal_values(arg_keys[11], (FF, D), FF ** -0.5, 0.09375, ((0, 2),)),
        "down_bias": normal_values(arg_keys[12], (D,), 0.3, 1.5),
        "out_grad": normal_values(arg_keys[13], (TOKENS, D), 1.0, 6.0, ((0, 32),)),
    }


@jax.custom_vjp
def low(v):
    return lax.optimization_barrier(v.astype(jnp.bfloat16)).astype(jnp.float32)

@jax.custom_vjp
def low_back(v):
    return v

def low_keep(v):
    return (low(v), None)

def low_pass(kept, grad):
    return (grad,)

def back_keep(v):
    return (v, None)

def back_low(kept, grad):
    return (low(grad),)
low.defvjp(low_keep, low_pass)
low_back.defvjp(back_keep, back_low)
epsilon = 1e-06
highest = lax.Precision.HIGHEST

def rotary_tables():
    rot_dims = 2 * (HD // 3 // 2)
    half_dims = rot_dims // 2
    index = jnp.arange(SEQ, dtype=jnp.int32)
    places = (index // (GH * GW), index // GW % GH, index % GW)
    freqs = jnp.float32(10000.0) ** (-jnp.arange(half_dims, dtype=jnp.float32) / jnp.float32(half_dims))
    cos_parts = []
    sin_parts = []
    for which in range(3):
        angle = places[which].astype(jnp.float32)[:, None] * freqs[None, :]
        cos_parts = cos_parts + [jnp.cos(angle), jnp.cos(angle)]
        sin_parts = sin_parts + [-jnp.sin(angle), jnp.sin(angle)]
    remain = HD - 3 * rot_dims
    cos_parts.append(jnp.ones((SEQ, remain), jnp.float32))
    sin_parts.append(jnp.zeros((SEQ, remain), jnp.float32))
    return (jnp.concatenate(cos_parts, 1), jnp.concatenate(sin_parts, 1))

def partner_order():
    rot_dims = 2 * (HD // 3 // 2)
    half_dims = rot_dims // 2
    order = np.arange(HD)
    for which in range(3):
        first = which * rot_dims
        order[first:first + half_dims] = np.arange(first + half_dims, first + rot_dims)
        order[first + half_dims:first + rot_dims] = np.arange(first, first + half_dims)
    return order

def rotate(values, cos_table, sin_table):
    partner = jnp.take(values, partner_order(), axis=-1)
    return values * cos_table[:, None, :] + partner * sin_table[:, None, :]

def layer_norm(values, scale_vec, shift_vec):
    centred = values - lax.optimization_barrier(jnp.mean(values, axis=-1, keepdims=True))
    variance = lax.optimization_barrier(jnp.mean(centred * centred, axis=-1, keepdims=True))
    return centred * lax.rsqrt(variance + epsilon) * scale_vec + shift_vec

def attend_block(query_blk, key_rows, value_rows):
    scale_factor = 1.0 / math.sqrt(HD)
    scores = low_back(jnp.einsum('qhd,khd->hqk', query_blk, key_rows, precision=highest) * scale_factor)
    shares = jax.nn.softmax(scores, axis=-1)
    return jnp.einsum('hqk,khd->qhd', low(shares), value_rows, precision=highest)

def clip_attention(clip_parts):
    clip_q, clip_k, clip_v = clip_parts
    block_rows = min(512, SEQ)
    blocks_q = clip_q.reshape(SEQ // block_rows, block_rows, HEADS, HD)
    checked = jax.checkpoint(attend_block)
    outputs = lax.map(lambda query_blk: checked(query_blk, clip_k, clip_v), blocks_q)
    return outputs.reshape(SEQ, HEADS, HD)

def forward(x_rows, ln1_s, ln1_b, w_qkv, b_qkv, w_out, b_out, ln2_s, ln2_b, w_up, b_up, w_down, b_down):
    cos_table, sin_table = rotary_tables()
    normed1 = low(layer_norm(x_rows, ln1_s, ln1_b))
    qkv_rows = jnp.dot(normed1, w_qkv.reshape(D, 3 * D), precision=highest) + b_qkv.reshape(3 * D)
    qkv_rows = low_back(qkv_rows).reshape(CLIPS_DEV, SEQ, 3, HEADS, HD)
    queries = low(rotate(qkv_rows[:, :, 0], cos_table, sin_table))
    key_rows = low(rotate(qkv_rows[:, :, 1], cos_table, sin_table))
    value_rows = low(qkv_rows[:, :, 2])
    attended = lax.map(clip_attention, (queries, key_rows, value_rows))
    attended = low_back(low(attended.reshape(TOK_GROUP, D)))
    branch_one = low_back(jnp.dot(attended, w_out, precision=highest) + b_out)
    resid = x_rows + branch_one
    normed2 = low(layer_norm(resid, ln2_s, ln2_b))
    hidden = low_back(jnp.dot(normed2, w_up, precision=highest) + b_up)
    acted = low(jax.nn.gelu(hidden, approximate=False))
    branch_two = low_back(jnp.dot(acted, w_down, precision=highest) + b_down)
    return resid + branch_two

def reference(block_in, ln1_scale, ln1_shift, qkv_weight, qkv_bias, out_weight, out_bias, ln2_scale, ln2_shift, up_weight, up_bias, down_weight, down_bias, out_grad):
    params = tuple((item.astype(jnp.float32) for item in (ln1_scale, ln1_shift, qkv_weight, qkv_bias, out_weight, out_bias, ln2_scale, ln2_shift, up_weight, up_bias, down_weight, down_bias)))
    rows_in = block_in.astype(jnp.float32).reshape(N_DP, TOK_GROUP, D)
    grads_in = out_grad.astype(jnp.float32).reshape(N_DP, TOK_GROUP, D)

    def group_step(totals, pair):
        x_rows, cot_rows = pair
        result, pullback = jax.vjp(forward, x_rows, *params)
        cotangents = pullback(cot_rows)
        new_totals = tuple((total + part for total, part in zip(totals, cotangents[1:])))
        return (new_totals, (result, cotangents[0]))
    zeros = tuple((jnp.zeros(item.shape, jnp.float32) for item in params))
    totals, (results, input_grads) = lax.scan(group_step, zeros, (rows_in, grads_in))
    block_out = results.reshape(TOKENS, D).astype(jnp.bfloat16)
    in_grad = input_grads.reshape(TOKENS, D).astype(jnp.bfloat16)
    return (block_out, in_grad, totals[0], totals[1], totals[2], totals[3], totals[4], totals[5], totals[6], totals[7], totals[8], totals[9], totals[10], totals[11])
```

```python
import functools
import math

import jax
import jax.numpy as jnp
import numpy as np
from jax import lax
from jax.experimental import pallas as pl
from jax.experimental.pallas import tpu as pltpu
from jax.sharding import PartitionSpec as P

HD = 64
GH = 16
GW = 16
SEQ = 2048
EPS = 1e-06
LANES = 128
ROT = 2 * (HD // 3 // 2)
HALF_ROT = ROT // 2
LOG2E = math.log2(math.e)
SCALE = 1.0 / math.sqrt(HD)
BF = jnp.bfloat16
F32 = jnp.float32
VMEM_BYTES = 56 << 20


def dot_nt(left, right):
    return lax.dot_general(left, right, (((1,), (1,)), ((), ())), preferred_element_type=F32)


def dot_nn(left, right):
    return lax.dot_general(left, right, (((1,), (0,)), ((), ())), preferred_element_type=F32)


def dot_tn(left, right):
    return lax.dot_general(left, right, (((0,), (0,)), ((), ())), preferred_element_type=F32)


def call(kernel, flops, moved, exps=0, **kw):
    return pl.pallas_call(
        kernel,
        compiler_params=pltpu.CompilerParams(vmem_limit_bytes=VMEM_BYTES),
        cost_estimate=pl.CostEstimate(flops=flops, bytes_accessed=moved, transcendentals=exps),
        **kw,
    )


def rotary_tables(first, count):
    lane = np.arange(LANES) % HD
    axis = lane // ROT
    inside = lane % ROT
    freq = np.float32(10000.0) ** (
        -(inside % HALF_ROT).astype(np.float32) / np.float32(HALF_ROT)
    )
    turned = axis < 3
    early = turned & (inside < HALF_ROT)
    late = turned & (inside >= HALF_ROT)
    index = first + jnp.arange(count, dtype=jnp.int32)[:, None]
    places = (index // (GH * GW), index // GW % GH, index % GW)
    place = jnp.where(axis == 0, places[0], jnp.where(axis == 1, places[1], places[2]))
    angle = place.astype(F32) * freq.astype(np.float32)[None, :]
    cos = jnp.where(turned, jnp.cos(angle), 1.0)
    sin = jnp.sin(angle)
    return cos, jnp.where(early, -sin, 0.0), jnp.where(late, sin, 0.0)


def turn(x, cos, sin_a, sin_b):
    return (
        x * cos
        + pltpu.roll(x, LANES - HALF_ROT, 1) * sin_a
        + pltpu.roll(x, HALF_ROT, 1) * sin_b
    )


def turn_back(g, cos, sin_a, sin_b):
    return (
        g * cos
        + pltpu.roll(g * sin_b, LANES - HALF_ROT, 1)
        + pltpu.roll(g * sin_a, HALF_ROT, 1)
    )


def qkv_kernel(n_ref, w_ref, b_ref, c_ref, sa_ref, sb_ref, q_ref, kv_ref, *, q_steps):
    step = pl.program_id(0)
    rows = dot_nn(n_ref[...], w_ref[...]) + b_ref[...]
    wide = rows.shape[1]

    def turned():
        tables = (c_ref[...], sa_ref[...], sb_ref[...])
        parts = [
            turn(rows[:, at : at + LANES], *tables).astype(BF) for at in range(0, wide, LANES)
        ]
        return jnp.concatenate(parts, axis=1)

    @pl.when(step < q_steps)
    def _():
        q_ref[...] = turned()

    @pl.when((step >= q_steps) & (step < 2 * q_steps))
    def _():
        kv_ref[...] = turned()

    @pl.when(step >= 2 * q_steps)
    def _():
        kv_ref[...] = rows.astype(BF)


def qkv_rows(normed, weight, bias, tables):
    tokens, width = normed.shape
    cols = weight.shape[1] // 3
    tile = 256 if cols % 256 == 0 else LANES
    q_steps = cols // tile
    whole = lambda n: (0, 0)
    return call(
        functools.partial(qkv_kernel, q_steps=q_steps),
        2 * tokens * width * 3 * cols,
        2 * (tokens * width + width * 3 * cols + tokens * 3 * cols),
        grid=(3 * q_steps,),
        in_specs=[
            pl.BlockSpec((tokens, width), whole),
            pl.BlockSpec((width, tile), lambda n: (0, n)),
            pl.BlockSpec((1, tile), lambda n: (0, n)),
        ]
        + [pl.BlockSpec((tokens, LANES), whole)] * 3,
        out_specs=[
            pl.BlockSpec((tokens, tile), lambda n: (0, jnp.minimum(n, q_steps - 1))),
            pl.BlockSpec((tokens, tile), lambda n: (0, jnp.maximum(n - q_steps, 0))),
        ],
        out_shape=[
            jax.ShapeDtypeStruct((tokens, cols), BF),
            jax.ShapeDtypeStruct((tokens, 2 * cols), BF),
        ],
    )(normed, weight, bias, *tables)


def attend_kernel(*refs, sources, rows_at):
    q_ref = refs[0]
    k_refs = refs[1 : 1 + sources]
    v_refs = refs[1 + sources : 1 + 2 * sources]
    o_ref, lse_ref = refs[1 + 2 * sources :]
    lane = lax.broadcasted_iota(jnp.int32, (1, LANES), 1)

    def body(i, carry):
        rows = pl.ds(pl.multiple_of(i * rows_at, rows_at), rows_at)
        q = q_ref[rows, :]
        outs, logs = [], []
        for head in range(2):
            mine = (lane // HD) == head
            q_head = jnp.where(mine, q, jnp.zeros_like(q))
            scores = [dot_nt(q_head, k[...]) for k in k_refs]
            peak = functools.reduce(
                jnp.maximum, [jnp.max(s, axis=1, keepdims=True) for s in scores]
            )
            weights = [jnp.exp2((s - peak) * (SCALE * LOG2E)) for s in scores]
            total = sum(jnp.sum(w, axis=1, keepdims=True) for w in weights)
            out = sum(dot_nn(w.astype(BF), v[...]) for w, v in zip(weights, v_refs))
            outs.append(out / total)
            logs.append(peak * (SCALE * LOG2E) + jnp.log2(total))
        first = lane < HD
        o_ref[rows, :] = jnp.where(first, outs[0], outs[1]).astype(BF)
        logs_t = jnp.where(first, logs[0], logs[1]).T
        lse_ref[0, 0:1, rows] = logs_t[0:1]
        lse_ref[0, 1:2, rows] = logs_t[HD : HD + 1]
        return carry

    steps = q_ref.shape[0] // rows_at
    lax.fori_loop(0, steps, body, 0, unroll=2 if steps % 2 == 0 else 1)


def attend(q, kvs):
    tokens, cols = q.shape
    pairs = cols // LANES
    keys = sum(kv.shape[0] for kv in kvs)
    q_spec = pl.BlockSpec((tokens, LANES), lambda i: (0, i))
    k_specs = [pl.BlockSpec((kv.shape[0], LANES), lambda i: (0, i)) for kv in kvs]
    v_specs = [pl.BlockSpec((kv.shape[0], LANES), lambda i: (0, pairs + i)) for kv in kvs]
    return call(
        functools.partial(attend_kernel, sources=len(kvs), rows_at=256),
        4 * 4 * tokens * keys * cols,
        2 * (2 * tokens * cols + 2 * keys * cols),
        tokens * keys * 2 * pairs,
        grid=(pairs,),
        in_specs=[q_spec] + k_specs + v_specs,
        out_specs=[q_spec, pl.BlockSpec((1, 2, tokens), lambda i: (i, 0, 0))],
        out_shape=[
            jax.ShapeDtypeStruct((tokens, cols), BF),
            jax.ShapeDtypeStruct((pairs, 2, tokens), F32),
        ],
    )(q, *kvs, *kvs)


def attend_back_kernel(*refs, sources, keys_at, queries_at):
    q_ref, do_ref, o_ref, lse_ref, c_ref, sa_ref, sb_ref = refs[:7]
    at = 7
    k_refs = refs[at : at + sources]
    v_refs = refs[at + sources : at + 2 * sources]
    at += 2 * sources
    dq_ref = refs[at]
    dk_refs = refs[at + 1 : at + 1 + sources]
    dv_refs = refs[at + 1 + sources : at + 1 + 2 * sources]
    dq_acc, centre = refs[at + 1 + 2 * sources :]
    lane = lax.broadcasted_iota(jnp.int32, (1, LANES), 1)
    tokens = q_ref.shape[0]
    product = (do_ref[...].astype(F32) * o_ref[...].astype(F32)).T
    for head in range(2):
        centre[head : head + 1, :] = jnp.sum(
            product[head * HD : head * HD + HD], axis=0, keepdims=True
        )
    dq_acc[...] = jnp.zeros_like(dq_acc)
    for k_ref, v_ref, dk_ref, dv_ref in zip(k_refs, v_refs, dk_refs, dv_refs):

        def body(j, carry):
            rows = pl.ds(pl.multiple_of(j * keys_at, keys_at), keys_at)
            k, v = k_ref[rows, :], v_ref[rows, :]
            k_t = k.astype(F32).T.astype(BF)
            dv = jnp.zeros((keys_at, LANES), F32)
            dk = jnp.zeros((keys_at, LANES), F32)
            for head in range(2):
                mine = (lane // HD) == head
                for first in range(0, tokens, queries_at):
                    cut = slice(first, first + queries_at)
                    q, do = q_ref[cut, :], do_ref[cut, :]
                    q_head = jnp.where(mine, q, jnp.zeros_like(q))
                    do_head = jnp.where(mine, do, jnp.zeros_like(do))
                    scores = dot_nt(k, q_head)
                    share_grad = dot_nt(v, do_head)
                    shares = jnp.exp2(
                        scores * (SCALE * LOG2E) - lse_ref[0, head : head + 1, cut]
                    )
                    score_grad = (
                        shares * (share_grad - centre[head : head + 1, cut])
                    ).astype(BF)
                    dv += dot_nn(shares.astype(BF), do_head)
                    dk += dot_nn(score_grad, q_head)
                    part = slice(head * HD, head * HD + HD)
                    dq_acc[part, cut] += dot_nn(k_t[part], score_grad)
            dv_ref[rows, :] = dv.astype(BF)
            dk_ref[rows, :] = (dk * SCALE).astype(BF)
            return carry

        lax.fori_loop(0, k_ref.shape[0] // keys_at, body, 0)
    dq = (dq_acc[...] * SCALE).T
    dq_ref[...] = turn_back(dq, c_ref[...], sa_ref[...], sb_ref[...]).astype(BF)


def attend_back(q, out_grad, out, lse, kvs, tables):
    tokens, cols = q.shape
    pairs = cols // LANES
    keys = sum(kv.shape[0] for kv in kvs)
    q_spec = pl.BlockSpec((tokens, LANES), lambda i: (0, i))
    k_specs = [pl.BlockSpec((kv.shape[0], LANES), lambda i: (0, i)) for kv in kvs]
    v_specs = [pl.BlockSpec((kv.shape[0], LANES), lambda i: (0, pairs + i)) for kv in kvs]
    table = pl.BlockSpec((tokens, LANES), lambda i: (0, 0))
    piece = min(512, tokens)
    outs = call(
        functools.partial(
            attend_back_kernel, sources=len(kvs), keys_at=512, queries_at=piece
        ),
        10 * 4 * tokens * keys * cols,
        2 * (4 * tokens * cols + 4 * keys * cols),
        tokens * keys * 2 * pairs,
        grid=(pairs,),
        in_specs=[q_spec, q_spec, q_spec]
        + [pl.BlockSpec((1, 2, tokens), lambda i: (i, 0, 0))]
        + [table] * 3
        + k_specs
        + v_specs,
        out_specs=[q_spec] + k_specs + k_specs,
        out_shape=[jax.ShapeDtypeStruct((tokens, cols), BF)]
        + [jax.ShapeDtypeStruct((kv.shape[0], cols), BF) for kv in kvs] * 2,
        scratch_shapes=[pltpu.VMEM((LANES, tokens), F32), pltpu.VMEM((2, tokens), F32)],
    )(q, out_grad, out, lse, *tables, *kvs, *kvs)
    n = len(kvs)
    return outs[0], outs[1 : 1 + n], outs[1 + n :]


def key_sum_kernel(own_ref, got_ref, c_ref, sa_ref, sb_ref, dk_ref):
    total = own_ref[...].astype(F32) + got_ref[...].astype(F32)
    dk_ref[...] = turn_back(total, c_ref[...], sa_ref[...], sb_ref[...]).astype(BF)


def key_sum(own, got, tables):
    tokens, cols = own.shape
    spec = pl.BlockSpec((tokens, LANES), lambda i: (0, i))
    table = pl.BlockSpec((tokens, LANES), lambda i: (0, 0))
    return call(
        key_sum_kernel,
        12 * tokens * cols,
        6 * tokens * cols,
        grid=(cols // LANES,),
        in_specs=[spec, spec] + [table] * 3,
        out_specs=spec,
        out_shape=jax.ShapeDtypeStruct((tokens, cols), BF),
    )(own, got, *tables)


def gelu_parts(hidden):
    size = jnp.abs(hidden)
    bell = jnp.exp2(hidden * hidden * (-0.5 * LOG2E))
    t = 1.0 / (1.0 + (0.3275911 / math.sqrt(2.0)) * size)
    poly = 0.5 * 1.061405429
    for factor in (-1.453152027, 1.421413741, -0.284496736, 0.254829592):
        poly = poly * t + 0.5 * factor
    tail = poly * t * bell
    cdf = jnp.where(hidden >= 0.0, 1.0 - tail, tail)
    return hidden * cdf, cdf + hidden * bell * (1.0 / math.sqrt(2.0 * math.pi))


def up_kernel(n_ref, w_ref, b_ref, acted_ref, slope_ref):
    hidden = dot_nn(n_ref[...], w_ref[...]) + b_ref[...]
    acted, slope = gelu_parts(hidden)
    acted_ref[...] = acted.astype(BF)
    slope_ref[...] = slope.astype(BF)


def up_rows(normed, weight, bias):
    tokens, width = normed.shape
    cols = weight.shape[1]
    tile = 256
    out = pl.BlockSpec((tokens, tile), lambda n: (0, n))
    return call(
        up_kernel,
        2 * tokens * width * cols,
        2 * (tokens * width + width * cols + 2 * tokens * cols),
        tokens * cols,
        grid=(cols // tile,),
        in_specs=[
            pl.BlockSpec((tokens, width), lambda n: (0, 0)),
            pl.BlockSpec((width, tile), lambda n: (0, n)),
            pl.BlockSpec((1, tile), lambda n: (0, n)),
        ],
        out_specs=[out, out],
        out_shape=[jax.ShapeDtypeStruct((tokens, cols), BF)] * 2,
    )(normed, weight, bias)


def hidden_grad_kernel(g_ref, w_ref, slope_ref, hg_ref, sum_ref):
    grad = dot_nt(g_ref[...], w_ref[...]) * slope_ref[...].astype(F32)
    low = grad.astype(BF)
    hg_ref[...] = low
    sum_ref[...] = jnp.sum(low.astype(F32), axis=0, keepdims=True)


def hidden_grads(grad, down, slope):
    tokens, width = grad.shape
    cols = down.shape[0]
    tile = 256
    out = pl.BlockSpec((tokens, tile), lambda n: (0, n))
    return call(
        hidden_grad_kernel,
        2 * tokens * width * cols,
        2 * (tokens * width + width * cols + 2 * tokens * cols),
        grid=(cols // tile,),
        in_specs=[
            pl.BlockSpec((tokens, width), lambda n: (0, 0)),
            pl.BlockSpec((tile, width), lambda n: (n, 0)),
            out,
        ],
        out_specs=[out, pl.BlockSpec((1, tile), lambda n: (0, n))],
        out_shape=[
            jax.ShapeDtypeStruct((tokens, cols), BF),
            jax.ShapeDtypeStruct((1, cols), F32),
        ],
    )(grad, down, slope)


def norm_parts(values, gain, shift):
    centred = values - jnp.mean(values, axis=-1, keepdims=True)
    inv_dev = lax.rsqrt(jnp.mean(centred * centred, axis=-1, keepdims=True) + EPS)
    normal = centred * inv_dev
    return (normal * gain + shift).astype(BF), normal, inv_dev


def norm_back(upstream, normal, inv_dev, gain):
    scaled = upstream * gain
    mean_first = jnp.mean(scaled, axis=-1, keepdims=True)
    mean_second = jnp.mean(scaled * normal, axis=-1, keepdims=True)
    back = inv_dev * (scaled - mean_first - normal * mean_second)
    return back, jnp.sum(upstream * normal, 0), jnp.sum(upstream, 0)


class Paired:
    def __init__(self, n_dp):
        self.n_dp = n_dp
        self.me_dp = lax.axis_index("dp")
        self.me_y = lax.axis_index("tensor")
        self.core = self.me_dp % 2
        self.first = self.core * (SEQ // 2)

    def move(self, x, to):
        pairs = []
        for dp in range(self.n_dp):
            for y in range(2):
                a, b = to(dp, y)
                if (a, b) != (dp, y):
                    pairs.append((dp * 2 + y, a * 2 + b))
        return lax.ppermute(x, ("dp", "tensor"), pairs)

    def swap_rows(self, rows):
        got = self.move(rows, lambda dp, y: (dp - dp % 2 + y, dp % 2))
        return jnp.where(self.core == self.me_y, rows, got)

    def over_y(self, x):
        return self.move(x, lambda dp, y: (dp, 1 - y))

    def over_core(self, x):
        return self.move(x, lambda dp, y: (dp ^ 1, y))

    def over_chip(self, x, bit):
        return self.move(x, lambda dp, y: (dp ^ (2 << bit), y))

    def other_half(self, own):
        rows = own.shape[0] // self.n_dp
        piece = lax.dynamic_slice_in_dim(own, self.me_dp * rows, rows, 0)
        return lax.all_gather(self.over_y(piece), "dp", axis=0, tiled=True)

    def weights(self, own):
        return [own, self.other_half(own)]

    def biases(self, own):
        return [own, self.over_y(own)]

    def keys(self, kv):
        return [kv, self.over_core(kv)]

    def keys_back(self, grads):
        return grads[0], self.over_core(grads[1])

    def reduce(self, own, other):
        rows, cols = own.shape
        chips = self.n_dp // 2
        piece = rows // self.n_dp

        def split(x, axis, bit):
            take = lambda b: lax.dynamic_index_in_dim(x, b, axis, keepdims=False)
            return take(bit), take(1 - bit)

        kept = []
        for half in (own, other):
            keep, send = split(half.reshape(chips, 2, piece, cols), 1, self.core)
            kept.append(keep + self.over_core(send))
        total = kept[0] + self.over_y(kept[1])
        chip = self.me_dp // 2
        for level in range(chips.bit_length() - 1):
            left = total.shape[0] // 2
            keep, send = split(total.reshape(left, 2, piece, cols), 1, (chip >> level) & 1)
            total = keep + self.over_chip(send, level)
        total = total.reshape(piece, cols)
        return lax.all_gather(total, "dp", axis=0, tiled=True).astype(F32)

    def reduce_vectors(self, both, own, other):
        k, width = both.shape
        both = both.reshape(k, 2, width // 2)
        take = lambda b: lax.dynamic_index_in_dim(both, b, 1, keepdims=False).reshape(-1)
        mine = jnp.concatenate([take(self.me_y), own]).reshape(-1, LANES)
        theirs = jnp.concatenate([take(1 - self.me_y), other]).reshape(-1, LANES)
        total = mine + self.over_y(theirs)
        total = total + self.over_core(total)
        for level in range((self.n_dp // 2).bit_length() - 1):
            total = total + self.over_chip(total, level)
        total = total.reshape(-1)
        return total[: k * width // 2].reshape(k, width // 2), total[k * width // 2 :]


class Spread:
    def __init__(self, tokens):
        self.first = lax.axis_index("tensor") * tokens

    def swap_rows(self, rows):
        return rows

    def keys(self, kv):
        return [lax.all_gather(kv, "tensor", axis=0, tiled=True)]

    def keys_back(self, grads):
        return lax.psum_scatter(grads[0], "tensor", scatter_dimension=0, tiled=True), None


def block_step(
    move,
    block_in,
    ln1_scale,
    ln1_shift,
    qkv_ws,
    qkv_bs,
    out_ws,
    out_bias,
    ln2_scale,
    ln2_shift,
    up_ws,
    up_bs,
    down_ws,
    down_bias,
    out_grad,
):
    f32 = lambda v: v.astype(F32)
    tokens = block_in.shape[0]
    tables = rotary_tables(move.first, tokens)
    ln1_gain, ln2_gain = f32(ln1_scale), f32(ln2_scale)
    block_in = move.swap_rows(block_in)
    x_rows = f32(block_in)
    normed1, normal1, inv_one = norm_parts(x_rows, ln1_gain, f32(ln1_shift))
    queries, keys, outs, logs = [], [], [], []
    for weight, bias in zip(qkv_ws, qkv_bs):
        q, kv = qkv_rows(normed1, weight, f32(bias)[None, :], tables)
        queries.append(q)
        keys.append(move.keys(kv))
    for q, kvs in zip(queries, keys):
        out, log = attend(q, kvs)
        outs.append(out)
        logs.append(log)
    grad_low = move.swap_rows(out_grad)
    grad_rows = f32(grad_low)
    branch_one = sum(dot_nn(o, w) for o, w in zip(outs, out_ws)) + f32(out_bias)
    resid = x_rows + branch_one
    normed2, normal2, inv_two = norm_parts(resid, ln2_gain, f32(ln2_shift))
    acts, slopes = [], []
    for weight, bias in zip(up_ws, up_bs):
        acted, slope = up_rows(normed2, weight, f32(bias)[None, :])
        acts.append(acted)
        slopes.append(slope)
    branch_two = sum(dot_nn(a, w) for a, w in zip(acts, down_ws)) + f32(down_bias)
    block_out = move.swap_rows((resid + branch_two).astype(BF))
    down_bias_grad = jnp.sum(grad_rows, 0)
    down_grads = [dot_tn(a, grad_low).astype(BF) for a in acts]
    hidden_gs, up_b_grads = [], []
    for down, slope in zip(down_ws, slopes):
        hg, total = hidden_grads(grad_low, down, slope)
        hidden_gs.append(hg)
        up_b_grads.append(total[0])
    up_grads = [dot_tn(normed2, hg).astype(BF) for hg in hidden_gs]
    normed2_grad = sum(dot_nt(hg, w) for hg, w in zip(hidden_gs, up_ws))
    resid_part, ln2_scale_grad, ln2_shift_grad = norm_back(normed2_grad, normal2, inv_two, ln2_gain)
    resid_grad = grad_rows + resid_part
    branch_grad = resid_grad.astype(BF)
    out_bias_grad = jnp.sum(branch_grad, 0, dtype=F32)
    out_w_grads = [dot_tn(o, branch_grad).astype(BF) for o in outs]
    qkv_w_grads, qkv_b_grads = [], []
    normed1_grad = 0.0
    for q, kvs, out, log, out_w, qkv_w in zip(queries, keys, outs, logs, out_ws, qkv_ws):
        out_g = dot_nt(branch_grad, out_w).astype(BF)
        dq, dks, dvs = attend_back(q, out_g, out, log, kvs, tables)
        dk_own, dk_got = move.keys_back(dks)
        dv_own, dv_got = move.keys_back(dvs)
        if dk_got is None:
            dk_got, dv_got = jnp.zeros_like(dk_own), jnp.zeros_like(dv_own)
        dk = key_sum(dk_own, dk_got, tables)
        dv = dv_own + dv_got
        qkv_g = jnp.concatenate([dq, dk, dv], axis=1)
        qkv_w_grads.append(dot_tn(normed1, qkv_g).astype(BF))
        qkv_b_grads.append(jnp.sum(qkv_g, 0, dtype=F32))
        normed1_grad = normed1_grad + dot_nt(qkv_g, qkv_w)
    input_part, ln1_scale_grad, ln1_shift_grad = norm_back(normed1_grad, normal1, inv_one, ln1_gain)
    in_grad = move.swap_rows((resid_grad + input_part).astype(BF))
    vectors = [
        ln1_scale_grad,
        ln1_shift_grad,
        out_bias_grad,
        ln2_scale_grad,
        ln2_shift_grad,
        down_bias_grad,
    ]
    return (
        block_out,
        in_grad,
        vectors,
        (qkv_w_grads, out_w_grads, up_grads, down_grads),
        (qkv_b_grads, up_b_grads),
    )


def paired_device(n_dp, *args):
    (block_in, ln1_scale, ln1_shift, qkv_weight, qkv_bias, out_weight, out_bias) = args[:7]
    (ln2_scale, ln2_shift, up_weight, up_bias, down_weight, down_bias, out_grad) = args[7:]
    move = Paired(n_dp)
    width, _, part = qkv_weight.shape
    qkv_flat = qkv_weight.reshape(width, 3 * part)
    out = block_step(
        move,
        block_in,
        ln1_scale,
        ln1_shift,
        move.weights(qkv_flat),
        move.biases(qkv_bias.reshape(3 * part)),
        move.weights(out_weight),
        out_bias,
        ln2_scale,
        ln2_shift,
        move.weights(up_weight),
        move.biases(up_bias),
        move.weights(down_weight),
        down_bias,
        out_grad,
    )
    block_out, in_grad, vectors, weight_grads, (qkv_b, up_b) = out
    qkv_g, out_g, up_g, down_g = (move.reduce(*pair) for pair in weight_grads)
    vec, flat = move.reduce_vectors(
        jnp.stack(vectors),
        jnp.concatenate([qkv_b[0], up_b[0]]),
        jnp.concatenate([qkv_b[1], up_b[1]]),
    )
    return (
        block_out,
        in_grad,
        vec[0],
        vec[1],
        qkv_g.reshape(width, 3, part),
        flat[: 3 * part].reshape(3, part),
        out_g,
        vec[2],
        vec[3],
        vec[4],
        up_g,
        flat[3 * part :],
        down_g,
        vec[5],
    )


def spread_device(*args):
    (block_in, ln1_scale, ln1_shift, qkv_weight, qkv_bias, out_weight, out_bias) = args[:7]
    (ln2_scale, ln2_shift, up_weight, up_bias, down_weight, down_bias, out_grad) = args[7:]
    gather = lambda w, axis: lax.all_gather(w, "tensor", axis=axis, tiled=True)
    scatter = lambda g, axis: lax.psum(
        lax.psum_scatter(g, "tensor", scatter_dimension=axis, tiled=True), "dp"
    ).astype(F32)
    width = qkv_weight.shape[0]
    qkv_all = gather(qkv_weight, 2)
    full = qkv_all.shape[2]
    out = block_step(
        Spread(block_in.shape[0]),
        block_in,
        ln1_scale,
        ln1_shift,
        [qkv_all.reshape(width, 3 * full)],
        [gather(qkv_bias, 1).reshape(3 * full)],
        [gather(out_weight, 0)],
        out_bias,
        ln2_scale,
        ln2_shift,
        [gather(up_weight, 1)],
        [gather(up_bias, 0)],
        [gather(down_weight, 0)],
        down_bias,
        out_grad,
    )
    block_out, in_grad, vectors, weight_grads, (qkv_b, up_b) = out
    ((qkv_g,), (out_g,), (up_g,), (down_g,)) = weight_grads
    vec = scatter(jnp.stack(vectors), 1)
    return (
        block_out,
        in_grad,
        vec[0],
        vec[1],
        scatter(qkv_g.reshape(width, 3, full), 2),
        scatter(qkv_b[0].reshape(3, full), 1),
        scatter(out_g, 0),
        vec[2],
        vec[3],
        vec[4],
        scatter(up_g, 1),
        scatter(up_b[0], 0),
        scatter(down_g, 0),
        vec[5],
    )


def solution(mesh):
    n_dp, n_tensor = mesh.shape["dp"], mesh.shape["tensor"]
    rows = P(("dp", "tensor"), None)
    vector = P("tensor")
    placed = (
        rows,
        P(),
        P(),
        P(None, None, "tensor"),
        P(None, "tensor"),
        P("tensor", None),
        P(),
        P(),
        P(),
        P(None, "tensor"),
        vector,
        P("tensor", None),
        P(),
        rows,
    )
    paired = n_tensor == 2 and n_dp & (n_dp - 1) == 0
    return jax.shard_map(
        functools.partial(paired_device, n_dp) if paired else spread_device,
        mesh=mesh,
        in_specs=placed,
        out_specs=(
            rows,
            rows,
            vector,
            vector,
            P(None, None, "tensor"),
            P(None, "tensor"),
            P("tensor", None),
            vector,
            vector,
            vector,
            P(None, "tensor"),
            vector,
            P("tensor", None),
            vector,
        ),
        check_vma=False,
    )
```

```python
import functools
import math

import jax
import jax.numpy as jnp
import numpy as np
from jax import lax
from jax.experimental import pallas as pl
from jax.experimental.pallas import tpu as pltpu
from jax.sharding import PartitionSpec as P

HD = 64
GH = 16
GW = 16
SEQ = 2048
EPS = 1e-06
LANES = 128
ROT = 2 * (HD // 3 // 2)
HALF_ROT = ROT // 2
LOG2E = math.log2(math.e)
SCALE = 1.0 / math.sqrt(HD)
BF = jnp.bfloat16
F32 = jnp.float32
VMEM_BYTES = 56 << 20


def dot_nt(left, right):
    return lax.dot_general(left, right, (((1,), (1,)), ((), ())), preferred_element_type=F32)


def dot_nn(left, right):
    return lax.dot_general(left, right, (((1,), (0,)), ((), ())), preferred_element_type=F32)


def dot_tn(left, right):
    return lax.dot_general(left, right, (((0,), (0,)), ((), ())), preferred_element_type=F32)


def call(kernel, flops, moved, exps=0, **kw):
    return pl.pallas_call(
        kernel,
        compiler_params=pltpu.CompilerParams(vmem_limit_bytes=VMEM_BYTES),
        cost_estimate=pl.CostEstimate(flops=flops, bytes_accessed=moved, transcendentals=exps),
        **kw,
    )


def rotary_tables(first, count):
    lane = np.arange(LANES) % HD
    axis = lane // ROT
    inside = lane % ROT
    freq = np.float32(10000.0) ** (
        -(inside % HALF_ROT).astype(np.float32) / np.float32(HALF_ROT)
    )
    turned = axis < 3
    early = turned & (inside < HALF_ROT)
    late = turned & (inside >= HALF_ROT)
    index = first + jnp.arange(count, dtype=jnp.int32)[:, None]
    places = (index // (GH * GW), index // GW % GH, index % GW)
    place = jnp.where(axis == 0, places[0], jnp.where(axis == 1, places[1], places[2]))
    angle = place.astype(F32) * freq.astype(np.float32)[None, :]
    cos = jnp.where(turned, jnp.cos(angle), 1.0)
    sin = jnp.sin(angle)
    return cos, jnp.where(early, -sin, 0.0), jnp.where(late, sin, 0.0)


def turn(x, cos, sin_a, sin_b):
    return (
        x * cos
        + pltpu.roll(x, LANES - HALF_ROT, 1) * sin_a
        + pltpu.roll(x, HALF_ROT, 1) * sin_b
    )


def turn_back(g, cos, sin_a, sin_b):
    return (
        g * cos
        + pltpu.roll(g * sin_b, LANES - HALF_ROT, 1)
        + pltpu.roll(g * sin_a, HALF_ROT, 1)
    )


def qkv_kernel(n_ref, w_ref, b_ref, c_ref, sa_ref, sb_ref, q_ref, kv_ref, *, q_steps):
    step = pl.program_id(0)
    rows = dot_nn(n_ref[...], w_ref[...]) + b_ref[...]
    wide = rows.shape[1]

    def turned():
        tables = (c_ref[...], sa_ref[...], sb_ref[...])
        parts = [
            turn(rows[:, at : at + LANES], *tables).astype(BF) for at in range(0, wide, LANES)
        ]
        return jnp.concatenate(parts, axis=1)

    @pl.when(step < q_steps)
    def _():
        q_ref[...] = turned()

    @pl.when((step >= q_steps) & (step < 2 * q_steps))
    def _():
        kv_ref[...] = turned()

    @pl.when(step >= 2 * q_steps)
    def _():
        kv_ref[...] = rows.astype(BF)


def qkv_rows(normed, weight, bias, tables):
    tokens, width = normed.shape
    cols = weight.shape[1] // 3
    tile = 256 if cols % 256 == 0 else LANES
    q_steps = cols // tile
    whole = lambda n: (0, 0)
    return call(
        functools.partial(qkv_kernel, q_steps=q_steps),
        2 * tokens * width * 3 * cols,
        2 * (tokens * width + width * 3 * cols + tokens * 3 * cols),
        grid=(3 * q_steps,),
        in_specs=[
            pl.BlockSpec((tokens, width), whole),
            pl.BlockSpec((width, tile), lambda n: (0, n)),
            pl.BlockSpec((1, tile), lambda n: (0, n)),
        ]
        + [pl.BlockSpec((tokens, LANES), whole)] * 3,
        out_specs=[
            pl.BlockSpec((tokens, tile), lambda n: (0, jnp.minimum(n, q_steps - 1))),
            pl.BlockSpec((tokens, tile), lambda n: (0, jnp.maximum(n - q_steps, 0))),
        ],
        out_shape=[
            jax.ShapeDtypeStruct((tokens, cols), BF),
            jax.ShapeDtypeStruct((tokens, 2 * cols), BF),
        ],
    )(normed, weight, bias, *tables)


def attend_kernel(*refs, sources, rows_at):
    q_ref = refs[0]
    k_refs = refs[1 : 1 + sources]
    v_refs = refs[1 + sources : 1 + 2 * sources]
    o_ref, lse_ref = refs[1 + 2 * sources :]
    lane = lax.broadcasted_iota(jnp.int32, (1, LANES), 1)

    def body(i, carry):
        rows = pl.ds(pl.multiple_of(i * rows_at, rows_at), rows_at)
        q = q_ref[rows, :]
        outs, logs = [], []
        for head in range(2):
            mine = (lane // HD) == head
            q_head = jnp.where(mine, q, jnp.zeros_like(q))
            scores = [dot_nt(q_head, k[...]) for k in k_refs]
            peak = functools.reduce(
                jnp.maximum, [jnp.max(s, axis=1, keepdims=True) for s in scores]
            )
            weights = [jnp.exp2((s - peak) * (SCALE * LOG2E)) for s in scores]
            total = sum(jnp.sum(w, axis=1, keepdims=True) for w in weights)
            out = sum(dot_nn(w.astype(BF), v[...]) for w, v in zip(weights, v_refs))
            outs.append(out / total)
            logs.append(peak * (SCALE * LOG2E) + jnp.log2(total))
        first = lane < HD
        o_ref[rows, :] = jnp.where(first, outs[0], outs[1]).astype(BF)
        logs_t = jnp.where(first, logs[0], logs[1]).T
        lse_ref[0, 0:1, rows] = logs_t[0:1]
        lse_ref[0, 1:2, rows] = logs_t[HD : HD + 1]
        return carry

    steps = q_ref.shape[0] // rows_at
    lax.fori_loop(0, steps, body, 0, unroll=2 if steps % 2 == 0 else 1)


def attend(q, kvs):
    tokens, cols = q.shape
    pairs = cols // LANES
    keys = sum(kv.shape[0] for kv in kvs)
    q_spec = pl.BlockSpec((tokens, LANES), lambda i: (0, i))
    k_specs = [pl.BlockSpec((kv.shape[0], LANES), lambda i: (0, i)) for kv in kvs]
    v_specs = [pl.BlockSpec((kv.shape[0], LANES), lambda i: (0, pairs + i)) for kv in kvs]
    return call(
        functools.partial(attend_kernel, sources=len(kvs), rows_at=256),
        4 * 4 * tokens * keys * cols,
        2 * (2 * tokens * cols + 2 * keys * cols),
        tokens * keys * 2 * pairs,
        grid=(pairs,),
        in_specs=[q_spec] + k_specs + v_specs,
        out_specs=[q_spec, pl.BlockSpec((1, 2, tokens), lambda i: (i, 0, 0))],
        out_shape=[
            jax.ShapeDtypeStruct((tokens, cols), BF),
            jax.ShapeDtypeStruct((pairs, 2, tokens), F32),
        ],
    )(q, *kvs, *kvs)


def attend_back_kernel(*refs, sources, keys_at, queries_at):
    q_ref, do_ref, o_ref, lse_ref, c_ref, sa_ref, sb_ref = refs[:7]
    at = 7
    k_refs = refs[at : at + sources]
    v_refs = refs[at + sources : at + 2 * sources]
    at += 2 * sources
    dq_ref = refs[at]
    dk_refs = refs[at + 1 : at + 1 + sources]
    dv_refs = refs[at + 1 + sources : at + 1 + 2 * sources]
    dq_acc, centre = refs[at + 1 + 2 * sources :]
    lane = lax.broadcasted_iota(jnp.int32, (1, LANES), 1)
    tokens = q_ref.shape[0]
    product = (do_ref[...].astype(F32) * o_ref[...].astype(F32)).T
    for head in range(2):
        centre[head : head + 1, :] = jnp.sum(
            product[head * HD : head * HD + HD], axis=0, keepdims=True
        )
    dq_acc[...] = jnp.zeros_like(dq_acc)
    for k_ref, v_ref, dk_ref, dv_ref in zip(k_refs, v_refs, dk_refs, dv_refs):

        def body(j, carry):
            rows = pl.ds(pl.multiple_of(j * keys_at, keys_at), keys_at)
            k, v = k_ref[rows, :], v_ref[rows, :]
            k_t = k.astype(F32).T.astype(BF)
            dv = jnp.zeros((keys_at, LANES), F32)
            dk = jnp.zeros((keys_at, LANES), F32)
            for head in range(2):
                mine = (lane // HD) == head
                for first in range(0, tokens, queries_at):
                    cut = slice(first, first + queries_at)
                    q, do = q_ref[cut, :], do_ref[cut, :]
                    q_head = jnp.where(mine, q, jnp.zeros_like(q))
                    do_head = jnp.where(mine, do, jnp.zeros_like(do))
                    scores = dot_nt(k, q_head)
                    share_grad = dot_nt(v, do_head)
                    shares = jnp.exp2(
                        scores * (SCALE * LOG2E) - lse_ref[0, head : head + 1, cut]
                    )
                    score_grad = (
                        shares * (share_grad - centre[head : head + 1, cut])
                    ).astype(BF)
                    dv += dot_nn(shares.astype(BF), do_head)
                    dk += dot_nn(score_grad, q_head)
                    part = slice(head * HD, head * HD + HD)
                    dq_acc[part, cut] += dot_nn(k_t[part], score_grad)
            dv_ref[rows, :] = dv.astype(BF)
            dk_ref[rows, :] = (dk * SCALE).astype(BF)
            return carry

        lax.fori_loop(0, k_ref.shape[0] // keys_at, body, 0)
    dq = (dq_acc[...] * SCALE).T
    dq_ref[...] = turn_back(dq, c_ref[...], sa_ref[...], sb_ref[...]).astype(BF)


def attend_back(q, out_grad, out, lse, kvs, tables, skip=0, pairs=None):
    tokens, cols = q.shape
    all_pairs = cols // LANES
    pairs = pairs or all_pairs
    cols = pairs * LANES
    keys = sum(kv.shape[0] for kv in kvs)
    q_spec = pl.BlockSpec((tokens, LANES), lambda i: (0, skip + i))
    k_specs = [pl.BlockSpec((kv.shape[0], LANES), lambda i: (0, skip + i)) for kv in kvs]
    v_specs = [
        pl.BlockSpec((kv.shape[0], LANES), lambda i: (0, all_pairs + skip + i)) for kv in kvs
    ]
    dq_spec = pl.BlockSpec((tokens, LANES), lambda i: (0, i))
    dk_specs = [pl.BlockSpec((kv.shape[0], LANES), lambda i: (0, i)) for kv in kvs]
    table = pl.BlockSpec((tokens, LANES), lambda i: (0, 0))
    piece = min(512, tokens)
    outs = call(
        functools.partial(
            attend_back_kernel, sources=len(kvs), keys_at=512, queries_at=piece
        ),
        10 * 4 * tokens * keys * cols,
        2 * (4 * tokens * cols + 4 * keys * cols),
        tokens * keys * 2 * pairs,
        grid=(pairs,),
        in_specs=[q_spec, q_spec, q_spec]
        + [pl.BlockSpec((1, 2, tokens), lambda i: (skip + i, 0, 0))]
        + [table] * 3
        + k_specs
        + v_specs,
        out_specs=[dq_spec] + dk_specs + dk_specs,
        out_shape=[jax.ShapeDtypeStruct((tokens, cols), BF)]
        + [jax.ShapeDtypeStruct((kv.shape[0], cols), BF) for kv in kvs] * 2,
        scratch_shapes=[pltpu.VMEM((LANES, tokens), F32), pltpu.VMEM((2, tokens), F32)],
    )(q, out_grad, out, lse, *tables, *kvs, *kvs)
    n = len(kvs)
    return outs[0], outs[1 : 1 + n], outs[1 + n :]


def key_sum_kernel(own_ref, got_ref, c_ref, sa_ref, sb_ref, dk_ref):
    total = own_ref[...].astype(F32) + got_ref[...].astype(F32)
    dk_ref[...] = turn_back(total, c_ref[...], sa_ref[...], sb_ref[...]).astype(BF)


def key_sum(own, got, tables):
    tokens, cols = own.shape
    spec = pl.BlockSpec((tokens, LANES), lambda i: (0, i))
    table = pl.BlockSpec((tokens, LANES), lambda i: (0, 0))
    return call(
        key_sum_kernel,
        12 * tokens * cols,
        6 * tokens * cols,
        grid=(cols // LANES,),
        in_specs=[spec, spec] + [table] * 3,
        out_specs=spec,
        out_shape=jax.ShapeDtypeStruct((tokens, cols), BF),
    )(own, got, *tables)


def gelu_parts(hidden):
    size = jnp.abs(hidden)
    bell = jnp.exp2(hidden * hidden * (-0.5 * LOG2E))
    t = 1.0 / (1.0 + (0.3275911 / math.sqrt(2.0)) * size)
    poly = 0.5 * 1.061405429
    for factor in (-1.453152027, 1.421413741, -0.284496736, 0.254829592):
        poly = poly * t + 0.5 * factor
    tail = poly * t * bell
    cdf = jnp.where(hidden >= 0.0, 1.0 - tail, tail)
    return hidden * cdf, cdf + hidden * bell * (1.0 / math.sqrt(2.0 * math.pi))


def up_kernel(n_ref, w_ref, b_ref, acted_ref, slope_ref):
    hidden = dot_nn(n_ref[...], w_ref[...]) + b_ref[...]
    acted, slope = gelu_parts(hidden)
    acted_ref[...] = acted.astype(BF)
    slope_ref[...] = slope.astype(BF)


def up_rows(normed, weight, bias):
    tokens, width = normed.shape
    cols = weight.shape[1]
    tile = 256
    out = pl.BlockSpec((tokens, tile), lambda n: (0, n))
    return call(
        up_kernel,
        2 * tokens * width * cols,
        2 * (tokens * width + width * cols + 2 * tokens * cols),
        tokens * cols,
        grid=(cols // tile,),
        in_specs=[
            pl.BlockSpec((tokens, width), lambda n: (0, 0)),
            pl.BlockSpec((width, tile), lambda n: (0, n)),
            pl.BlockSpec((1, tile), lambda n: (0, n)),
        ],
        out_specs=[out, out],
        out_shape=[jax.ShapeDtypeStruct((tokens, cols), BF)] * 2,
    )(normed, weight, bias)


def hidden_grad_kernel(g_ref, w_ref, slope_ref, hg_ref, sum_ref):
    grad = dot_nt(g_ref[...], w_ref[...]) * slope_ref[...].astype(F32)
    low = grad.astype(BF)
    hg_ref[...] = low
    sum_ref[...] = jnp.sum(low.astype(F32), axis=0, keepdims=True)


def hidden_grads(grad, down, slope):
    tokens, width = grad.shape
    cols = down.shape[0]
    tile = 256
    out = pl.BlockSpec((tokens, tile), lambda n: (0, n))
    return call(
        hidden_grad_kernel,
        2 * tokens * width * cols,
        2 * (tokens * width + width * cols + 2 * tokens * cols),
        grid=(cols // tile,),
        in_specs=[
            pl.BlockSpec((tokens, width), lambda n: (0, 0)),
            pl.BlockSpec((tile, width), lambda n: (n, 0)),
            out,
        ],
        out_specs=[out, pl.BlockSpec((1, tile), lambda n: (0, n))],
        out_shape=[
            jax.ShapeDtypeStruct((tokens, cols), BF),
            jax.ShapeDtypeStruct((1, cols), F32),
        ],
    )(grad, down, slope)


def norm_parts(values, gain, shift):
    centred = values - jnp.mean(values, axis=-1, keepdims=True)
    inv_dev = lax.rsqrt(jnp.mean(centred * centred, axis=-1, keepdims=True) + EPS)
    normal = centred * inv_dev
    return (normal * gain + shift).astype(BF), normal, inv_dev


def norm_back(upstream, normal, inv_dev, gain):
    scaled = upstream * gain
    mean_first = jnp.mean(scaled, axis=-1, keepdims=True)
    mean_second = jnp.mean(scaled * normal, axis=-1, keepdims=True)
    back = inv_dev * (scaled - mean_first - normal * mean_second)
    return back, jnp.sum(upstream * normal, 0), jnp.sum(upstream, 0)


def pick(x, index):
    return lax.dynamic_index_in_dim(x, index, 1, keepdims=False)


def tie(*trees):
    leaves, form = jax.tree.flatten(trees)
    return jax.tree.unflatten(form, lax.optimization_barrier(tuple(leaves)))


class Paired:
    def __init__(self, n_dp):
        self.n_dp = n_dp
        self.me_dp = lax.axis_index("dp")
        self.me_y = lax.axis_index("tensor")
        self.core = self.me_dp % 2
        self.first = self.core * (SEQ // 2)

    def move(self, x, to):
        pairs = []
        for dp in range(self.n_dp):
            for y in range(2):
                a, b = to(dp, y)
                if (a, b) != (dp, y):
                    pairs.append((dp * 2 + y, a * 2 + b))
        return lax.ppermute(x, ("dp", "tensor"), pairs)

    def swap_rows(self, rows):
        got = self.move(rows, lambda dp, y: (dp - dp % 2 + y, dp % 2))
        return jnp.where(self.core == self.me_y, rows, got)

    def over_y(self, x):
        return self.move(x, lambda dp, y: (dp, 1 - y))

    def over_core(self, x):
        return self.move(x, lambda dp, y: (dp ^ 1, y))

    def over_chip(self, x, bit):
        return self.move(x, lambda dp, y: (dp ^ (2 << bit), y))

    def piece(self, own):
        rows = own.shape[0] // self.n_dp
        return lax.dynamic_slice_in_dim(own, self.me_dp * rows, rows, 0)

    def spread(self, got):
        return lax.all_gather(got, "dp", axis=0, tiled=True)

    def biases(self, own):
        return [own, self.over_y(own)]

    def keys(self, kv):
        return [kv, self.over_core(kv)]

    def keys_back(self, grads):
        return grads[0], self.over_core(grads[1])

    def core_split(self, half):
        rows, cols = half.shape
        blocks = half.reshape(self.n_dp // 2, 2, rows // self.n_dp, cols)
        return pick(blocks, self.core), pick(blocks, 1 - self.core)

    def chip_split(self, blocks, level):
        bit = (self.me_dp >> (level + 1)) & 1
        left = blocks.shape[0] // 2
        blocks = blocks.reshape(left, 2, *blocks.shape[1:])
        return pick(blocks, bit), pick(blocks, 1 - bit)

    def gather(self, block):
        return lax.all_gather(block[0], "dp", axis=0, tiled=True)

    def reduce_vectors(self, both, own, other):
        k, width = both.shape
        both = both.reshape(k, 2, width // 2)
        take = lambda b: lax.dynamic_index_in_dim(both, b, 1, keepdims=False).reshape(-1)
        mine = jnp.concatenate([take(self.me_y), own]).reshape(-1, LANES)
        theirs = jnp.concatenate([take(1 - self.me_y), other]).reshape(-1, LANES)
        total = mine + self.over_y(theirs)
        total = total + self.over_core(total)
        for level in range((self.n_dp // 2).bit_length() - 1):
            total = total + self.over_chip(total, level)
        total = total.reshape(-1)
        return total[: k * width // 2].reshape(k, width // 2), total[k * width // 2 :]


class Spread:
    def __init__(self, tokens):
        self.first = lax.axis_index("tensor") * tokens

    def swap_rows(self, rows):
        return rows

    def keys(self, kv):
        return [lax.all_gather(kv, "tensor", axis=0, tiled=True)]

    def keys_back(self, grads):
        return lax.psum_scatter(grads[0], "tensor", scatter_dimension=0, tiled=True), None


def block_step(
    move,
    block_in,
    ln1_scale,
    ln1_shift,
    qkv_ws,
    qkv_bs,
    out_ws,
    out_bias,
    ln2_scale,
    ln2_shift,
    up_ws,
    up_bs,
    down_ws,
    down_bias,
    out_grad,
):
    f32 = lambda v: v.astype(F32)
    tokens = block_in.shape[0]
    tables = rotary_tables(move.first, tokens)
    ln1_gain, ln2_gain = f32(ln1_scale), f32(ln2_scale)
    block_in = move.swap_rows(block_in)
    x_rows = f32(block_in)
    normed1, normal1, inv_one = norm_parts(x_rows, ln1_gain, f32(ln1_shift))
    queries, keys, outs, logs = [], [], [], []
    for weight, bias in zip(qkv_ws, qkv_bs):
        q, kv = qkv_rows(normed1, weight, f32(bias)[None, :], tables)
        queries.append(q)
        keys.append(move.keys(kv))
    for q, kvs in zip(queries, keys):
        out, log = attend(q, kvs)
        outs.append(out)
        logs.append(log)
    grad_low = move.swap_rows(out_grad)
    grad_rows = f32(grad_low)
    branch_one = sum(dot_nn(o, w) for o, w in zip(outs, out_ws)) + f32(out_bias)
    resid = x_rows + branch_one
    normed2, normal2, inv_two = norm_parts(resid, ln2_gain, f32(ln2_shift))
    acts, slopes = [], []
    for weight, bias in zip(up_ws, up_bs):
        acted, slope = up_rows(normed2, weight, f32(bias)[None, :])
        acts.append(acted)
        slopes.append(slope)
    branch_two = sum(dot_nn(a, w) for a, w in zip(acts, down_ws)) + f32(down_bias)
    block_out = move.swap_rows((resid + branch_two).astype(BF))
    down_bias_grad = jnp.sum(grad_rows, 0)
    down_grads = [dot_tn(a, grad_low).astype(BF) for a in acts]
    hidden_gs, up_b_grads = [], []
    for down, slope in zip(down_ws, slopes):
        hg, total = hidden_grads(grad_low, down, slope)
        hidden_gs.append(hg)
        up_b_grads.append(total[0])
    up_grads = [dot_tn(normed2, hg).astype(BF) for hg in hidden_gs]
    normed2_grad = sum(dot_nt(hg, w) for hg, w in zip(hidden_gs, up_ws))
    resid_part, ln2_scale_grad, ln2_shift_grad = norm_back(normed2_grad, normal2, inv_two, ln2_gain)
    resid_grad = grad_rows + resid_part
    branch_grad = resid_grad.astype(BF)
    out_bias_grad = jnp.sum(branch_grad, 0, dtype=F32)
    out_w_grads = [dot_tn(o, branch_grad).astype(BF) for o in outs]
    qkv_w_grads, qkv_b_grads = [], []
    normed1_grad = 0.0
    for q, kvs, out, log, out_w, qkv_w in zip(queries, keys, outs, logs, out_ws, qkv_ws):
        out_g = dot_nt(branch_grad, out_w).astype(BF)
        dq, dks, dvs = attend_back(q, out_g, out, log, kvs, tables)
        dk_own, dk_got = move.keys_back(dks)
        dv_own, dv_got = move.keys_back(dvs)
        if dk_got is None:
            dk_got, dv_got = jnp.zeros_like(dk_own), jnp.zeros_like(dv_own)
        dk = key_sum(dk_own, dk_got, tables)
        dv = dv_own + dv_got
        qkv_g = jnp.concatenate([dq, dk, dv], axis=1)
        qkv_w_grads.append(dot_tn(normed1, qkv_g).astype(BF))
        qkv_b_grads.append(jnp.sum(qkv_g, 0, dtype=F32))
        normed1_grad = normed1_grad + dot_nt(qkv_g, qkv_w)
    input_part, ln1_scale_grad, ln1_shift_grad = norm_back(normed1_grad, normal1, inv_one, ln1_gain)
    in_grad = move.swap_rows((resid_grad + input_part).astype(BF))
    vectors = [
        ln1_scale_grad,
        ln1_shift_grad,
        out_bias_grad,
        ln2_scale_grad,
        ln2_shift_grad,
        down_bias_grad,
    ]
    return (
        block_out,
        in_grad,
        vectors,
        (qkv_w_grads, out_w_grads, up_grads, down_grads),
        (qkv_b_grads, up_b_grads),
    )


def paired_device(n_dp, *args):
    (block_in, ln1_scale, ln1_shift, qkv_weight, qkv_bias, out_weight, out_bias) = args[:7]
    (ln2_scale, ln2_shift, up_weight, up_bias, down_weight, down_bias, out_grad) = args[7:]
    move = Paired(n_dp)
    f32 = lambda v: v.astype(F32)
    width, _, part = qkv_weight.shape
    tokens = block_in.shape[0]
    pairs = part // LANES
    levels = (n_dp // 2).bit_length() - 1
    ln1_gain, ln2_gain = f32(ln1_scale), f32(ln2_scale)

    block_in = move.swap_rows(block_in)
    qkv_own = qkv_weight.reshape(width, 3 * part)
    qkv_got = move.over_y(move.piece(qkv_own))
    qkv_bs = move.biases(qkv_bias.reshape(3 * part))
    tables = rotary_tables(move.first, tokens)
    x_rows = f32(block_in)
    normed1, normal1, inv_one = norm_parts(x_rows, ln1_gain, f32(ln1_shift))
    qkv_got, normed1 = tie(qkv_got, normed1)
    qkv_ws = [qkv_own, move.spread(qkv_got)]
    q_own, kv_own = qkv_rows(normed1, qkv_own, f32(qkv_bs[0])[None, :], tables)
    rest = [move.piece(w) for w in (out_weight, up_weight, down_weight)]
    rest, up_bias, kv_own = tie(rest, up_bias, kv_own)
    kvs_own = move.keys(kv_own)
    rest = [move.over_y(w) for w in rest]
    up_bs = move.biases(up_bias)
    q_oth, kv_oth = qkv_rows(normed1, qkv_ws[1], f32(qkv_bs[1])[None, :], tables)
    kvs_own, rest, kv_oth, q_own = tie(kvs_own, rest, kv_oth, q_own)
    out_ws, up_ws, down_ws = (
        [w, move.spread(got)] for w, got in zip((out_weight, up_weight, down_weight), rest)
    )
    kvs_oth = move.keys(kv_oth)
    out_own, log_own = attend(q_own, kvs_own)
    out_own, kvs_oth, q_oth, out_grad = tie(out_own, kvs_oth, q_oth, out_grad)
    grad_low = move.swap_rows(out_grad)
    out_oth, log_oth = attend(q_oth, kvs_oth)
    out_oth, grad_low = tie(out_oth, grad_low)
    grad_rows = f32(grad_low)
    outs = [out_own, out_oth]

    branch_one = sum(dot_nn(o, w) for o, w in zip(outs, out_ws)) + f32(out_bias)
    resid = x_rows + branch_one
    normed2, normal2, inv_two = norm_parts(resid, ln2_gain, f32(ln2_shift))
    acts, slopes = [], []
    for weight, bias in zip(up_ws, up_bs):
        acted, slope = up_rows(normed2, weight, f32(bias)[None, :])
        acts.append(acted)
        slopes.append(slope)
    branch_two = sum(dot_nn(a, w) for a, w in zip(acts, down_ws)) + f32(down_bias)
    block_out = (resid + branch_two).astype(BF)
    block_out, acts = tie(block_out, acts)
    block_out = move.swap_rows(block_out)
    down_bias_grad = jnp.sum(grad_rows, 0)
    down_grads = [dot_tn(a, grad_low).astype(BF) for a in acts]
    down_keep, down_send = zip(*[move.core_split(g) for g in down_grads])

    down_keep, down_send, acts, grad_low = tie(down_keep, down_send, acts, grad_low)
    down_got = [move.over_core(x) for x in down_send]
    hidden_gs, up_b_grads = [], []
    for down, slope in zip(down_ws, slopes):
        hg, total = hidden_grads(grad_low, down, slope)
        hidden_gs.append(hg)
        up_b_grads.append(total[0])
    down_got, hidden_gs, block_out = tie(down_got, hidden_gs, block_out)
    down_send = down_keep[1] + down_got[1]
    down_keep = down_keep[0] + down_got[0]

    down_send, hidden_gs = tie(down_send, hidden_gs)
    down_got = move.over_y(down_send)
    up_grads = [dot_tn(normed2, hg).astype(BF) for hg in hidden_gs]
    up_keep, up_send = zip(*[move.core_split(g) for g in up_grads])
    up_keep, up_send, hidden_gs = tie(up_keep, up_send, hidden_gs)
    up_got = [move.over_core(x) for x in up_send]
    normed2_grad = sum(dot_nt(hg, w) for hg, w in zip(hidden_gs, up_ws))
    resid_part, ln2_scale_grad, ln2_shift_grad = norm_back(normed2_grad, normal2, inv_two, ln2_gain)
    resid_grad = grad_rows + resid_part
    branch_grad = resid_grad.astype(BF)
    out_bias_grad = jnp.sum(branch_grad, 0, dtype=F32)
    out_w_grads = [dot_tn(o, branch_grad).astype(BF) for o in outs]
    out_gs = [dot_nt(branch_grad, w).astype(BF) for w in out_ws]
    up_got, down_got, out_gs, out_w_grads = tie(up_got, down_got, out_gs, out_w_grads)
    up_send = up_keep[1] + up_got[1]
    up_keep = up_keep[0] + up_got[0]
    down = down_keep + down_got

    def step(total, level):
        keep, send = move.chip_split(total, level)
        return keep, send

    def back(which, skip):
        q, kvs, log = ((q_own, kvs_own, log_own), (q_oth, kvs_oth, log_oth))[which]
        return q, out_gs[which], outs[which], log, kvs

    half = pairs // 2
    down_keep, down_send = step(down, 0)
    ins, up_send, down_send = tie(back(1, 0), up_send, down_send)
    up_got = move.over_y(up_send)
    down_got = move.over_chip(down_send, 0)
    first = attend_back(*ins, tables, 0, half)
    first, down_got = tie(first, down_got)
    down_keep, down_send = step(down_keep + down_got, 1)
    ins, down_send, first = tie(back(1, half), down_send, first)
    down_got = move.over_chip(down_send, 1)
    first_got = [move.over_core(x[1]) for x in first[1:]]
    second = attend_back(*ins, tables, half, half)
    second, down_got, up_got, first_got = tie(second, down_got, up_got, first_got)
    down_keep, down_send = step(down_keep + down_got, 2)
    up_keep, up_send = step(up_keep + up_got, 0)
    second, down_send, up_send = tie(second, down_send, up_send)
    second_got = [move.over_core(x[1]) for x in second[1:]]
    down_got = move.over_chip(down_send, 2)
    up_got = move.over_chip(up_send, 0)

    def finish(parts, gots):
        dk = [key_sum(p[1][0], g[0], tables) for p, g in zip(parts, gots)]
        dv = [p[2][0] + g[1] for p, g in zip(parts, gots)]
        return jnp.concatenate([p[0] for p in parts] + dk + dv, axis=1)

    third = attend_back(*back(0, 0), tables, 0, half)
    third, second_got, down_got, up_got = tie(third, second_got, down_got, up_got)
    down_block = down_keep + down_got
    up_keep, up_send = step(up_keep + up_got, 1)
    qkv_g_oth = finish((first, second), (first_got, second_got))
    qkv_w_oth = dot_tn(normed1, qkv_g_oth).astype(BF)
    ins, down_block, up_send, third, qkv_w_oth = tie(
        back(0, half), down_block, up_send, third, qkv_w_oth
    )
    third_got = [move.over_core(x[1]) for x in third[1:]]
    down_all = move.gather(down_block)
    up_got = move.over_chip(up_send, 1)
    oth_keep, oth_send = zip(*[move.core_split(g) for g in (qkv_w_oth, out_w_grads[1])])
    oth_got = [move.over_core(x) for x in oth_send]
    fourth = attend_back(*ins, tables, half, half)
    fourth, third_got, up_got, oth_got = tie(fourth, third_got, up_got, oth_got)
    up_keep, up_send = step(up_keep + up_got, 2)
    oth_send = [k + g for k, g in zip(oth_keep, oth_got)]
    fourth, up_send, oth_send = tie(fourth, up_send, oth_send)
    fourth_got = [move.over_core(x[1]) for x in fourth[1:]]
    up_got = move.over_chip(up_send, 2)
    oth_got = [move.over_y(x) for x in oth_send]
    normed1_grad = dot_nt(qkv_g_oth, qkv_ws[1])
    fourth_got, normed1_grad = tie(fourth_got, normed1_grad)
    qkv_g_own = finish((third, fourth), (third_got, fourth_got))
    qkv_w_own = dot_tn(normed1, qkv_g_own).astype(BF)
    qkv_w_own, qkv_g_own, up_got, down_all = tie(qkv_w_own, qkv_g_own, up_got, down_all)
    up_all = move.gather(up_keep + up_got)
    own_keep, own_send = zip(*[move.core_split(g) for g in (qkv_w_own, out_w_grads[0])])
    own_got = [move.over_core(x) for x in own_send]
    normed1_grad = normed1_grad + dot_nt(qkv_g_own, qkv_ws[0])
    input_part, ln1_scale_grad, ln1_shift_grad = norm_back(normed1_grad, normal1, inv_one, ln1_gain)
    in_grad = (resid_grad + input_part).astype(BF)
    own_got, in_grad, oth_got = tie(own_got, in_grad, oth_got)
    in_grad = move.swap_rows(in_grad)
    totals = [k + g + h for k, g, h in zip(own_keep, own_got, oth_got)]
    for level in range(levels):
        keeps, sends = zip(*[step(t, level) for t in totals])
        totals = [k + move.over_chip(s, level) for k, s in zip(keeps, sends)]
    qkv_g, out_g = (move.gather(t) for t in totals)
    qkv_b = [jnp.sum(g, 0, dtype=F32) for g in (qkv_g_own, qkv_g_oth)]
    vec, flat = move.reduce_vectors(
        jnp.stack(
            [
                ln1_scale_grad,
                ln1_shift_grad,
                out_bias_grad,
                ln2_scale_grad,
                ln2_shift_grad,
                down_bias_grad,
            ]
        ),
        jnp.concatenate([qkv_b[0], up_b_grads[0]]),
        jnp.concatenate([qkv_b[1], up_b_grads[1]]),
    )
    return (
        block_out,
        in_grad,
        vec[0],
        vec[1],
        f32(qkv_g).reshape(width, 3, part),
        flat[: 3 * part].reshape(3, part),
        f32(out_g),
        vec[2],
        vec[3],
        vec[4],
        f32(up_all),
        flat[3 * part :],
        f32(down_all),
        vec[5],
    )


def spread_device(*args):
    (block_in, ln1_scale, ln1_shift, qkv_weight, qkv_bias, out_weight, out_bias) = args[:7]
    (ln2_scale, ln2_shift, up_weight, up_bias, down_weight, down_bias, out_grad) = args[7:]
    gather = lambda w, axis: lax.all_gather(w, "tensor", axis=axis, tiled=True)
    scatter = lambda g, axis: lax.psum(
        lax.psum_scatter(g, "tensor", scatter_dimension=axis, tiled=True), "dp"
    ).astype(F32)
    width = qkv_weight.shape[0]
    qkv_all = gather(qkv_weight, 2)
    full = qkv_all.shape[2]
    out = block_step(
        Spread(block_in.shape[0]),
        block_in,
        ln1_scale,
        ln1_shift,
        [qkv_all.reshape(width, 3 * full)],
        [gather(qkv_bias, 1).reshape(3 * full)],
        [gather(out_weight, 0)],
        out_bias,
        ln2_scale,
        ln2_shift,
        [gather(up_weight, 1)],
        [gather(up_bias, 0)],
        [gather(down_weight, 0)],
        down_bias,
        out_grad,
    )
    block_out, in_grad, vectors, weight_grads, (qkv_b, up_b) = out
    ((qkv_g,), (out_g,), (up_g,), (down_g,)) = weight_grads
    vec = scatter(jnp.stack(vectors), 1)
    return (
        block_out,
        in_grad,
        vec[0],
        vec[1],
        scatter(qkv_g.reshape(width, 3, full), 2),
        scatter(qkv_b[0].reshape(3, full), 1),
        scatter(out_g, 0),
        vec[2],
        vec[3],
        vec[4],
        scatter(up_g, 1),
        scatter(up_b[0], 0),
        scatter(down_g, 0),
        vec[5],
    )


def solution(mesh):
    n_dp, n_tensor = mesh.shape["dp"], mesh.shape["tensor"]
    rows = P(("dp", "tensor"), None)
    vector = P("tensor")
    placed = (
        rows,
        P(),
        P(),
        P(None, None, "tensor"),
        P(None, "tensor"),
        P("tensor", None),
        P(),
        P(),
        P(),
        P(None, "tensor"),
        vector,
        P("tensor", None),
        P(),
        rows,
    )
    paired = n_tensor == 2 and n_dp & (n_dp - 1) == 0
    return jax.shard_map(
        functools.partial(paired_device, n_dp) if paired else spread_device,
        mesh=mesh,
        in_specs=placed,
        out_specs=(
            rows,
            rows,
            vector,
            vector,
            P(None, None, "tensor"),
            P(None, "tensor"),
            P("tensor", None),
            vector,
            vector,
            vector,
            P(None, "tensor"),
            vector,
            P("tensor", None),
            vector,
        ),
        check_vma=False,
    )
```

```python
import functools
import math

import jax
import jax.numpy as jnp
import numpy as np
from jax import lax
from jax.experimental import pallas as pl
from jax.experimental.pallas import tpu as pltpu
from jax.sharding import PartitionSpec as P

HD = 64
GH = 16
GW = 16
SEQ = 2048
EPS = 1e-06
LANES = 128
ROT = 2 * (HD // 3 // 2)
HALF_ROT = ROT // 2
LOG2E = math.log2(math.e)
SCALE = 1.0 / math.sqrt(HD)
BF = jnp.bfloat16
F32 = jnp.float32
VMEM_BYTES = 56 << 20


def dot_nt(left, right):
    return lax.dot_general(left, right, (((1,), (1,)), ((), ())), preferred_element_type=F32)


def dot_nn(left, right):
    return lax.dot_general(left, right, (((1,), (0,)), ((), ())), preferred_element_type=F32)


def dot_tn(left, right):
    return lax.dot_general(left, right, (((0,), (0,)), ((), ())), preferred_element_type=F32)


def call(kernel, flops, moved, exps=0, **kw):
    return pl.pallas_call(
        kernel,
        compiler_params=pltpu.CompilerParams(vmem_limit_bytes=VMEM_BYTES),
        cost_estimate=pl.CostEstimate(flops=flops, bytes_accessed=moved, transcendentals=exps),
        **kw,
    )


def rotary_tables(first, count):
    lane = np.arange(LANES) % HD
    axis = lane // ROT
    inside = lane % ROT
    freq = np.float32(10000.0) ** (
        -(inside % HALF_ROT).astype(np.float32) / np.float32(HALF_ROT)
    )
    turned = axis < 3
    early = turned & (inside < HALF_ROT)
    late = turned & (inside >= HALF_ROT)
    index = first + jnp.arange(count, dtype=jnp.int32)[:, None]
    places = (index // (GH * GW), index // GW % GH, index % GW)
    place = jnp.where(axis == 0, places[0], jnp.where(axis == 1, places[1], places[2]))
    angle = place.astype(F32) * freq.astype(np.float32)[None, :]
    cos = jnp.where(turned, jnp.cos(angle), 1.0)
    sin = jnp.sin(angle)
    return cos, jnp.where(early, -sin, 0.0), jnp.where(late, sin, 0.0)


def turn(x, cos, sin_a, sin_b):
    return (
        x * cos
        + pltpu.roll(x, LANES - HALF_ROT, 1) * sin_a
        + pltpu.roll(x, HALF_ROT, 1) * sin_b
    )


def turn_back(g, cos, sin_a, sin_b):
    return (
        g * cos
        + pltpu.roll(g * sin_b, LANES - HALF_ROT, 1)
        + pltpu.roll(g * sin_a, HALF_ROT, 1)
    )


def qkv_kernel(n_ref, w_ref, b_ref, c_ref, sa_ref, sb_ref, q_ref, kv_ref, *, q_steps):
    step = pl.program_id(0)
    rows = dot_nn(n_ref[...], w_ref[...]) + b_ref[...]
    wide = rows.shape[1]

    def turned():
        tables = (c_ref[...], sa_ref[...], sb_ref[...])
        parts = [
            turn(rows[:, at : at + LANES], *tables).astype(BF) for at in range(0, wide, LANES)
        ]
        return jnp.concatenate(parts, axis=1)

    @pl.when(step < q_steps)
    def _():
        q_ref[...] = turned()

    @pl.when((step >= q_steps) & (step < 2 * q_steps))
    def _():
        kv_ref[...] = turned()

    @pl.when(step >= 2 * q_steps)
    def _():
        kv_ref[...] = rows.astype(BF)


def qkv_rows(normed, weight, bias, tables):
    tokens, width = normed.shape
    cols = weight.shape[1] // 3
    tile = 256 if cols % 256 == 0 else LANES
    q_steps = cols // tile
    whole = lambda n: (0, 0)
    return call(
        functools.partial(qkv_kernel, q_steps=q_steps),
        2 * tokens * width * 3 * cols,
        2 * (tokens * width + width * 3 * cols + tokens * 3 * cols),
        grid=(3 * q_steps,),
        in_specs=[
            pl.BlockSpec((tokens, width), whole),
            pl.BlockSpec((width, tile), lambda n: (0, n)),
            pl.BlockSpec((1, tile), lambda n: (0, n)),
        ]
        + [pl.BlockSpec((tokens, LANES), whole)] * 3,
        out_specs=[
            pl.BlockSpec((tokens, tile), lambda n: (0, jnp.minimum(n, q_steps - 1))),
            pl.BlockSpec((tokens, tile), lambda n: (0, jnp.maximum(n - q_steps, 0))),
        ],
        out_shape=[
            jax.ShapeDtypeStruct((tokens, cols), BF),
            jax.ShapeDtypeStruct((tokens, 2 * cols), BF),
        ],
    )(normed, weight, bias, *tables)


def attend_kernel(*refs, sources, rows_at):
    q_ref = refs[0]
    k_refs = refs[1 : 1 + sources]
    v_refs = refs[1 + sources : 1 + 2 * sources]
    o_ref, lse_ref = refs[1 + 2 * sources :]
    lane = lax.broadcasted_iota(jnp.int32, (1, LANES), 1)

    def body(i, carry):
        rows = pl.ds(pl.multiple_of(i * rows_at, rows_at), rows_at)
        q = q_ref[rows, :]
        outs, logs = [], []
        for head in range(2):
            mine = (lane // HD) == head
            q_head = jnp.where(mine, q, jnp.zeros_like(q))
            scores = [dot_nt(q_head, k[...]) for k in k_refs]
            peak = functools.reduce(
                jnp.maximum, [jnp.max(s, axis=1, keepdims=True) for s in scores]
            )
            weights = [jnp.exp2((s - peak) * (SCALE * LOG2E)) for s in scores]
            total = sum(jnp.sum(w, axis=1, keepdims=True) for w in weights)
            out = sum(dot_nn(w.astype(BF), v[...]) for w, v in zip(weights, v_refs))
            outs.append(out / total)
            logs.append(peak * (SCALE * LOG2E) + jnp.log2(total))
        first = lane < HD
        o_ref[rows, :] = jnp.where(first, outs[0], outs[1]).astype(BF)
        logs_t = jnp.where(first, logs[0], logs[1]).T
        lse_ref[0, 0:1, rows] = logs_t[0:1]
        lse_ref[0, 1:2, rows] = logs_t[HD : HD + 1]
        return carry

    steps = q_ref.shape[0] // rows_at
    lax.fori_loop(0, steps, body, 0, unroll=2 if steps % 2 == 0 else 1)


def attend(q, kvs):
    tokens, cols = q.shape
    pairs = cols // LANES
    keys = sum(kv.shape[0] for kv in kvs)
    q_spec = pl.BlockSpec((tokens, LANES), lambda i: (0, i))
    k_specs = [pl.BlockSpec((kv.shape[0], LANES), lambda i: (0, i)) for kv in kvs]
    v_specs = [pl.BlockSpec((kv.shape[0], LANES), lambda i: (0, pairs + i)) for kv in kvs]
    return call(
        functools.partial(attend_kernel, sources=len(kvs), rows_at=256),
        4 * 4 * tokens * keys * cols,
        2 * (2 * tokens * cols + 2 * keys * cols),
        tokens * keys * 2 * pairs,
        grid=(pairs,),
        in_specs=[q_spec] + k_specs + v_specs,
        out_specs=[q_spec, pl.BlockSpec((1, 2, tokens), lambda i: (i, 0, 0))],
        out_shape=[
            jax.ShapeDtypeStruct((tokens, cols), BF),
            jax.ShapeDtypeStruct((pairs, 2, tokens), F32),
        ],
    )(q, *kvs, *kvs)


def attend_back_kernel(*refs, sources, keys_at, queries_at):
    q_ref, do_ref, o_ref, lse_ref, c_ref, sa_ref, sb_ref = refs[:7]
    at = 7
    k_refs = refs[at : at + sources]
    v_refs = refs[at + sources : at + 2 * sources]
    at += 2 * sources
    dq_ref = refs[at]
    dk_refs = refs[at + 1 : at + 1 + sources]
    dv_refs = refs[at + 1 + sources : at + 1 + 2 * sources]
    dq_acc, centre = refs[at + 1 + 2 * sources :]
    lane = lax.broadcasted_iota(jnp.int32, (1, LANES), 1)
    tokens = q_ref.shape[0]
    product = (do_ref[...].astype(F32) * o_ref[...].astype(F32)).T
    for head in range(2):
        centre[head : head + 1, :] = jnp.sum(
            product[head * HD : head * HD + HD], axis=0, keepdims=True
        )
    dq_acc[...] = jnp.zeros_like(dq_acc)
    for k_ref, v_ref, dk_ref, dv_ref in zip(k_refs, v_refs, dk_refs, dv_refs):

        def body(j, carry):
            rows = pl.ds(pl.multiple_of(j * keys_at, keys_at), keys_at)
            k, v = k_ref[rows, :], v_ref[rows, :]
            k_t = k.astype(F32).T.astype(BF)
            dv = jnp.zeros((keys_at, LANES), F32)
            dk = jnp.zeros((keys_at, LANES), F32)
            for head in range(2):
                mine = (lane // HD) == head
                for first in range(0, tokens, queries_at):
                    cut = slice(first, first + queries_at)
                    q, do = q_ref[cut, :], do_ref[cut, :]
                    q_head = jnp.where(mine, q, jnp.zeros_like(q))
                    do_head = jnp.where(mine, do, jnp.zeros_like(do))
                    scores = dot_nt(k, q_head)
                    share_grad = dot_nt(v, do_head)
                    shares = jnp.exp2(
                        scores * (SCALE * LOG2E) - lse_ref[0, head : head + 1, cut]
                    )
                    score_grad = (
                        shares * (share_grad - centre[head : head + 1, cut])
                    ).astype(BF)
                    dv += dot_nn(shares.astype(BF), do_head)
                    dk += dot_nn(score_grad, q_head)
                    part = slice(head * HD, head * HD + HD)
                    dq_acc[part, cut] += dot_nn(k_t[part], score_grad)
            dv_ref[rows, :] = dv.astype(BF)
            dk_ref[rows, :] = (dk * SCALE).astype(BF)
            return carry

        lax.fori_loop(0, k_ref.shape[0] // keys_at, body, 0)
    dq = (dq_acc[...] * SCALE).T
    dq_ref[...] = turn_back(dq, c_ref[...], sa_ref[...], sb_ref[...]).astype(BF)


def attend_back(q, out_grad, out, lse, kvs, tables, skip=0, pairs=None):
    tokens, cols = q.shape
    all_pairs = cols // LANES
    pairs = pairs or all_pairs
    cols = pairs * LANES
    keys = sum(kv.shape[0] for kv in kvs)
    q_spec = pl.BlockSpec((tokens, LANES), lambda i: (0, skip + i))
    k_specs = [pl.BlockSpec((kv.shape[0], LANES), lambda i: (0, skip + i)) for kv in kvs]
    v_specs = [
        pl.BlockSpec((kv.shape[0], LANES), lambda i: (0, all_pairs + skip + i)) for kv in kvs
    ]
    dq_spec = pl.BlockSpec((tokens, LANES), lambda i: (0, i))
    dk_specs = [pl.BlockSpec((kv.shape[0], LANES), lambda i: (0, i)) for kv in kvs]
    table = pl.BlockSpec((tokens, LANES), lambda i: (0, 0))
    piece = min(512, tokens)
    outs = call(
        functools.partial(
            attend_back_kernel, sources=len(kvs), keys_at=512, queries_at=piece
        ),
        10 * 4 * tokens * keys * cols,
        2 * (4 * tokens * cols + 4 * keys * cols),
        tokens * keys * 2 * pairs,
        grid=(pairs,),
        in_specs=[q_spec, q_spec, q_spec]
        + [pl.BlockSpec((1, 2, tokens), lambda i: (skip + i, 0, 0))]
        + [table] * 3
        + k_specs
        + v_specs,
        out_specs=[dq_spec] + dk_specs + dk_specs,
        out_shape=[jax.ShapeDtypeStruct((tokens, cols), BF)]
        + [jax.ShapeDtypeStruct((kv.shape[0], cols), BF) for kv in kvs] * 2,
        scratch_shapes=[pltpu.VMEM((LANES, tokens), F32), pltpu.VMEM((2, tokens), F32)],
    )(q, out_grad, out, lse, *tables, *kvs, *kvs)
    n = len(kvs)
    return outs[0], outs[1 : 1 + n], outs[1 + n :]


def key_sum_kernel(own_ref, got_ref, c_ref, sa_ref, sb_ref, dk_ref):
    total = own_ref[...].astype(F32) + got_ref[...].astype(F32)
    dk_ref[...] = turn_back(total, c_ref[...], sa_ref[...], sb_ref[...]).astype(BF)


def key_sum(own, got, tables):
    tokens, cols = own.shape
    spec = pl.BlockSpec((tokens, LANES), lambda i: (0, i))
    table = pl.BlockSpec((tokens, LANES), lambda i: (0, 0))
    return call(
        key_sum_kernel,
        12 * tokens * cols,
        6 * tokens * cols,
        grid=(cols // LANES,),
        in_specs=[spec, spec] + [table] * 3,
        out_specs=spec,
        out_shape=jax.ShapeDtypeStruct((tokens, cols), BF),
    )(own, got, *tables)


def gelu_parts(hidden):
    size = jnp.abs(hidden)
    bell = jnp.exp2(hidden * hidden * (-0.5 * LOG2E))
    t = 1.0 / (1.0 + (0.3275911 / math.sqrt(2.0)) * size)
    poly = 0.5 * 1.061405429
    for factor in (-1.453152027, 1.421413741, -0.284496736, 0.254829592):
        poly = poly * t + 0.5 * factor
    tail = poly * t * bell
    cdf = jnp.where(hidden >= 0.0, 1.0 - tail, tail)
    return hidden * cdf, cdf + hidden * bell * (1.0 / math.sqrt(2.0 * math.pi))


def up_kernel(n_ref, w_ref, b_ref, acted_ref, slope_ref):
    hidden = dot_nn(n_ref[...], w_ref[...]) + b_ref[...]
    acted, slope = gelu_parts(hidden)
    acted_ref[...] = acted.astype(BF)
    slope_ref[...] = slope.astype(BF)


def up_rows(normed, weight, bias):
    tokens, width = normed.shape
    cols = weight.shape[1]
    tile = 256
    out = pl.BlockSpec((tokens, tile), lambda n: (0, n))
    return call(
        up_kernel,
        2 * tokens * width * cols,
        2 * (tokens * width + width * cols + 2 * tokens * cols),
        tokens * cols,
        grid=(cols // tile,),
        in_specs=[
            pl.BlockSpec((tokens, width), lambda n: (0, 0)),
            pl.BlockSpec((width, tile), lambda n: (0, n)),
            pl.BlockSpec((1, tile), lambda n: (0, n)),
        ],
        out_specs=[out, out],
        out_shape=[jax.ShapeDtypeStruct((tokens, cols), BF)] * 2,
    )(normed, weight, bias)


def hidden_grad_kernel(g_ref, w_ref, slope_ref, hg_ref, sum_ref):
    grad = dot_nt(g_ref[...], w_ref[...]) * slope_ref[...].astype(F32)
    low = grad.astype(BF)
    hg_ref[...] = low
    sum_ref[...] = jnp.sum(low.astype(F32), axis=0, keepdims=True)


def hidden_grads(grad, down, slope):
    tokens, width = grad.shape
    cols = down.shape[0]
    tile = 256
    out = pl.BlockSpec((tokens, tile), lambda n: (0, n))
    return call(
        hidden_grad_kernel,
        2 * tokens * width * cols,
        2 * (tokens * width + width * cols + 2 * tokens * cols),
        grid=(cols // tile,),
        in_specs=[
            pl.BlockSpec((tokens, width), lambda n: (0, 0)),
            pl.BlockSpec((tile, width), lambda n: (n, 0)),
            out,
        ],
        out_specs=[out, pl.BlockSpec((1, tile), lambda n: (0, n))],
        out_shape=[
            jax.ShapeDtypeStruct((tokens, cols), BF),
            jax.ShapeDtypeStruct((1, cols), F32),
        ],
    )(grad, down, slope)


def norm_parts(values, gain, shift):
    centred = values - jnp.mean(values, axis=-1, keepdims=True)
    inv_dev = lax.rsqrt(jnp.mean(centred * centred, axis=-1, keepdims=True) + EPS)
    normal = centred * inv_dev
    return (normal * gain + shift).astype(BF), normal, inv_dev


def norm_back(upstream, normal, inv_dev, gain):
    scaled = upstream * gain
    mean_first = jnp.mean(scaled, axis=-1, keepdims=True)
    mean_second = jnp.mean(scaled * normal, axis=-1, keepdims=True)
    back = inv_dev * (scaled - mean_first - normal * mean_second)
    return back, jnp.sum(upstream * normal, 0), jnp.sum(upstream, 0)


def tie(*trees):
    leaves, form = jax.tree.flatten(trees)
    return jax.tree.unflatten(form, lax.optimization_barrier(tuple(leaves)))


def split_kernel(t_ref, own_m, own_f, oth_m, oth_f, got_om, got_of, got_tm, got_tf, ka, kb, sa, sb, *, last):
    total = lambda a, b: (a[...].astype(F32) + b[...].astype(F32)).astype(BF)
    by_y = t_ref[last] == 0
    own_far, oth_me = total(own_f, got_of), total(oth_m, got_tm)
    ka[...] = total(own_m, got_om)
    kb[...] = jnp.where(by_y, own_far, oth_me)
    sa[...] = jnp.where(by_y, oth_me, own_far)
    sb[...] = total(oth_f, got_tf)


def first_split(table, own, oth, got_own, got_oth):
    chips, piece, cols = got_own.shape
    count = chips // 2
    own, oth = (g.reshape(chips, 2, piece, cols) for g in (own, oth))
    whole = lambda far: pl.BlockSpec(
        (None, None, piece, cols), lambda i, t: (t[far * count + i], t[2 * count], 0, 0)
    )
    part = lambda far: pl.BlockSpec((None, piece, cols), lambda i, t: (t[far * count + i], 0, 0))
    out = pl.BlockSpec((None, piece, cols), lambda i, t: (i, 0, 0))
    return pl.pallas_call(
        functools.partial(split_kernel, last=2 * count),
        grid_spec=pltpu.PrefetchScalarGridSpec(
            num_scalar_prefetch=1,
            grid=(count,),
            in_specs=[whole(0), whole(1)] * 2 + [part(0), part(1)] * 2,
            out_specs=[out] * 4,
        ),
        out_shape=[jax.ShapeDtypeStruct((count, piece, cols), BF)] * 4,
        compiler_params=pltpu.CompilerParams(vmem_limit_bytes=VMEM_BYTES),
        cost_estimate=pl.CostEstimate(
            flops=4 * count * piece * cols, bytes_accessed=24 * count * piece * cols, transcendentals=0
        ),
    )(table, own, own, oth, oth, got_own, got_own, got_oth, got_oth)


class Paired:
    def __init__(self, n_dp):
        self.n_dp = n_dp
        self.me_dp = lax.axis_index("dp")
        self.me_y = lax.axis_index("tensor")
        self.core = self.me_dp % 2
        self.first = self.core * (SEQ // 2)

    def move(self, x, to):
        pairs = []
        for dp in range(self.n_dp):
            for y in range(2):
                a, b = to(dp, y)
                if (a, b) != (dp, y):
                    pairs.append((dp * 2 + y, a * 2 + b))
        return lax.ppermute(x, ("dp", "tensor"), pairs)

    def swap_rows(self, rows):
        got = self.move(rows, lambda dp, y: (dp - dp % 2 + y, dp % 2))
        return jnp.where(self.core == self.me_y, rows, got)

    def over_y(self, x):
        return self.move(x, lambda dp, y: (dp, 1 - y))

    def over_core(self, x):
        return self.move(x, lambda dp, y: (dp ^ 1, y))

    def piece(self, own):
        rows = own.shape[0] // self.n_dp
        return lax.dynamic_slice_in_dim(own, self.me_dp * rows, rows, 0)

    def spread(self, got):
        return lax.all_gather(got, "dp", axis=0, tiled=True)

    def core_send(self, half):
        rows, cols = half.shape
        blocks = half.reshape(self.n_dp // 2, 2, rows // self.n_dp, cols)
        return lax.dynamic_index_in_dim(blocks, 1 - self.core, 1, keepdims=False)

    def over_first(self, x):
        return self.move(x, lambda dp, y: (dp ^ 2, y) if dp % 2 else (dp, 1 - y))

    def over_second(self, x):
        return self.move(x, lambda dp, y: (dp, 1 - y) if dp % 2 else (dp ^ 2, y))

    def over_z(self, x, level):
        return self.move(x, lambda dp, y: (dp ^ (4 << level), y))

    def blocks_of(self, x_bit):
        count = self.n_dp // 4
        levels = count.bit_length() - 1
        z = self.me_dp // 4
        places = np.arange(count)
        far = sum(((places >> (levels - 1 - k)) & 1) << k for k in range(levels))
        return (jnp.asarray(far, jnp.int32) ^ z) * 2 + x_bit

    def table(self):
        x = (self.me_dp // 2) % 2
        me, far = self.blocks_of(x), self.blocks_of(1 - x)
        return jnp.concatenate([me, far, jnp.stack([self.core])]).astype(jnp.int32)

    def gather(self, block):
        return lax.all_gather(block[0], "dp", axis=0, tiled=True)

    def reduce_vectors(self, both, own, other):
        k, width = both.shape
        both = both.reshape(k, 2, width // 2)
        take = lambda b: lax.dynamic_index_in_dim(both, b, 1, keepdims=False).reshape(-1)
        mine = jnp.concatenate([take(self.me_y), own]).reshape(-1, LANES)
        theirs = jnp.concatenate([take(1 - self.me_y), other]).reshape(-1, LANES)
        total = mine + self.over_y(theirs)
        total = total + self.over_core(total)
        for level in range((self.n_dp // 2).bit_length() - 1):
            total = total + self.move(total, lambda dp, y: (dp ^ (2 << level), y))
        total = total.reshape(-1)
        return total[: k * width // 2].reshape(k, width // 2), total[k * width // 2 :]


class Spread:
    def __init__(self, tokens):
        self.first = lax.axis_index("tensor") * tokens

    def swap_rows(self, rows):
        return rows

    def keys(self, kv):
        return [lax.all_gather(kv, "tensor", axis=0, tiled=True)]

    def keys_back(self, grads):
        return lax.psum_scatter(grads[0], "tensor", scatter_dimension=0, tiled=True), None


def block_step(
    move,
    block_in,
    ln1_scale,
    ln1_shift,
    qkv_ws,
    qkv_bs,
    out_ws,
    out_bias,
    ln2_scale,
    ln2_shift,
    up_ws,
    up_bs,
    down_ws,
    down_bias,
    out_grad,
):
    f32 = lambda v: v.astype(F32)
    tokens = block_in.shape[0]
    tables = rotary_tables(move.first, tokens)
    ln1_gain, ln2_gain = f32(ln1_scale), f32(ln2_scale)
    block_in = move.swap_rows(block_in)
    x_rows = f32(block_in)
    normed1, normal1, inv_one = norm_parts(x_rows, ln1_gain, f32(ln1_shift))
    queries, keys, outs, logs = [], [], [], []
    for weight, bias in zip(qkv_ws, qkv_bs):
        q, kv = qkv_rows(normed1, weight, f32(bias)[None, :], tables)
        queries.append(q)
        keys.append(move.keys(kv))
    for q, kvs in zip(queries, keys):
        out, log = attend(q, kvs)
        outs.append(out)
        logs.append(log)
    grad_low = move.swap_rows(out_grad)
    grad_rows = f32(grad_low)
    branch_one = sum(dot_nn(o, w) for o, w in zip(outs, out_ws)) + f32(out_bias)
    resid = x_rows + branch_one
    normed2, normal2, inv_two = norm_parts(resid, ln2_gain, f32(ln2_shift))
    acts, slopes = [], []
    for weight, bias in zip(up_ws, up_bs):
        acted, slope = up_rows(normed2, weight, f32(bias)[None, :])
        acts.append(acted)
        slopes.append(slope)
    branch_two = sum(dot_nn(a, w) for a, w in zip(acts, down_ws)) + f32(down_bias)
    block_out = move.swap_rows((resid + branch_two).astype(BF))
    down_bias_grad = jnp.sum(grad_rows, 0)
    down_grads = [dot_tn(a, grad_low).astype(BF) for a in acts]
    hidden_gs, up_b_grads = [], []
    for down, slope in zip(down_ws, slopes):
        hg, total = hidden_grads(grad_low, down, slope)
        hidden_gs.append(hg)
        up_b_grads.append(total[0])
    up_grads = [dot_tn(normed2, hg).astype(BF) for hg in hidden_gs]
    normed2_grad = sum(dot_nt(hg, w) for hg, w in zip(hidden_gs, up_ws))
    resid_part, ln2_scale_grad, ln2_shift_grad = norm_back(normed2_grad, normal2, inv_two, ln2_gain)
    resid_grad = grad_rows + resid_part
    branch_grad = resid_grad.astype(BF)
    out_bias_grad = jnp.sum(branch_grad, 0, dtype=F32)
    out_w_grads = [dot_tn(o, branch_grad).astype(BF) for o in outs]
    qkv_w_grads, qkv_b_grads = [], []
    normed1_grad = 0.0
    for q, kvs, out, log, out_w, qkv_w in zip(queries, keys, outs, logs, out_ws, qkv_ws):
        out_g = dot_nt(branch_grad, out_w).astype(BF)
        dq, dks, dvs = attend_back(q, out_g, out, log, kvs, tables)
        dk_own, dk_got = move.keys_back(dks)
        dv_own, dv_got = move.keys_back(dvs)
        if dk_got is None:
            dk_got, dv_got = jnp.zeros_like(dk_own), jnp.zeros_like(dv_own)
        dk = key_sum(dk_own, dk_got, tables)
        dv = dv_own + dv_got
        qkv_g = jnp.concatenate([dq, dk, dv], axis=1)
        qkv_w_grads.append(dot_tn(normed1, qkv_g).astype(BF))
        qkv_b_grads.append(jnp.sum(qkv_g, 0, dtype=F32))
        normed1_grad = normed1_grad + dot_nt(qkv_g, qkv_w)
    input_part, ln1_scale_grad, ln1_shift_grad = norm_back(normed1_grad, normal1, inv_one, ln1_gain)
    in_grad = move.swap_rows((resid_grad + input_part).astype(BF))
    vectors = [
        ln1_scale_grad,
        ln1_shift_grad,
        out_bias_grad,
        ln2_scale_grad,
        ln2_shift_grad,
        down_bias_grad,
    ]
    return (
        block_out,
        in_grad,
        vectors,
        (qkv_w_grads, out_w_grads, up_grads, down_grads),
        (qkv_b_grads, up_b_grads),
    )


class Reduction:
    def __init__(self, move, table, own, oth):
        self.move, self.table = move, table
        self.grads = own, oth
        self.sends = [move.core_send(g) for g in (own, oth)]
        self.at = 0

    def start(self):
        at = self.at
        if at == 0:
            go = self.move.over_core
        elif at == 1:
            go = self.move.over_first
        elif at == 2:
            go = self.move.over_second
        else:
            go = functools.partial(self.move.over_z, level=at - 3)
        return [go(x) for x in self.sends]

    def take(self, got):
        at, self.at = self.at, self.at + 1
        if at == 0:
            ka, kb, sa, sb = first_split(self.table, *self.grads, *got)
            self.keep, self.sends = (ka, kb), [sa, sb]
        elif at == 1:
            self.sends = [self.keep[1] + got[1]]
            self.keep = self.keep[0] + got[0]
        else:
            total = self.keep + got[0]
            half = total.shape[0] // 2
            if half:
                self.keep, self.sends = total[:half], [total[half:]]
            else:
                self.done = total

    @property
    def last(self):
        return 2 + (self.move.n_dp // 4).bit_length() - 1


def beside(compute, inputs, *steps):
    sends = [s.sends if isinstance(s, Reduction) else s[1] for s in steps]
    inputs, sends = tie(inputs, sends)
    got = []
    for s, x in zip(steps, sends):
        if isinstance(s, Reduction):
            s.sends = x
            got.append(s.start())
        else:
            got.append(s[0](x))
    out = compute(*inputs)
    out, got = tie(out, got)
    moved = []
    for s, x in zip(steps, got):
        if isinstance(s, Reduction):
            s.take(x)
        else:
            moved.append(x)
    return out, moved


def paired_device(n_dp, *args):
    (block_in, ln1_scale, ln1_shift, qkv_weight, qkv_bias, out_weight, out_bias) = args[:7]
    (ln2_scale, ln2_shift, up_weight, up_bias, down_weight, down_bias, out_grad) = args[7:]
    move = Paired(n_dp)
    f32 = lambda v: v.astype(F32)
    width, _, part = qkv_weight.shape
    tokens = block_in.shape[0]
    pairs = part // LANES
    ln1_gain, ln2_gain = f32(ln1_scale), f32(ln2_scale)
    table = move.table()

    small = jnp.concatenate([qkv_bias.reshape(3 * part), up_bias])
    qkv_piece = move.piece(qkv_weight).reshape(width // n_dp, 3 * part)
    qkv_piece, small, block_in = tie(qkv_piece, small, block_in)
    qkv_got = move.over_y(qkv_piece)
    small_got = move.over_y(small)
    block_in = move.swap_rows(block_in)
    qkv_bs = [v[: 3 * part] for v in (small, small_got)]
    up_bs = [v[3 * part :] for v in (small, small_got)]
    tables = rotary_tables(move.first, tokens)
    qkv_own = qkv_weight.reshape(width, 3 * part)
    qkv_oth = move.spread(qkv_got)
    x_rows = f32(block_in)
    normed1, normal1, inv_one = norm_parts(x_rows, ln1_gain, f32(ln1_shift))
    q_own, kv_own = qkv_rows(normed1, qkv_own, f32(qkv_bs[0])[None, :], tables)
    rest = [move.piece(w) for w in (out_weight, up_weight, down_weight)]
    (q_oth, kv_oth), (rest, kv_got) = beside(
        lambda n, w: qkv_rows(n, w, f32(qkv_bs[1])[None, :], tables),
        (normed1, qkv_oth),
        (lambda ws: [move.over_y(w) for w in ws], rest),
        (move.over_core, kv_own),
    )
    kvs_own = [kv_own, kv_got]
    spread = [move.spread(got) for got in rest]
    (out_own, log_own), (kv_got, grad_low) = beside(
        attend, (q_own, kvs_own), (move.over_core, kv_oth), (move.swap_rows, out_grad)
    )
    kvs_oth = [kv_oth, kv_got]
    out_ws, up_ws, down_ws = (
        [w, got] for w, got in zip((out_weight, up_weight, down_weight), spread)
    )
    out_oth, log_oth = attend(q_oth, kvs_oth)
    grad_rows = f32(grad_low)
    outs = [out_own, out_oth]

    branch_one = sum(dot_nn(o, w) for o, w in zip(outs, out_ws)) + f32(out_bias)
    resid = x_rows + branch_one
    normed2, normal2, inv_two = norm_parts(resid, ln2_gain, f32(ln2_shift))
    acts, slopes = [], []
    for weight, bias in zip(up_ws, up_bs):
        acted, slope = up_rows(normed2, weight, f32(bias)[None, :])
        acts.append(acted)
        slopes.append(slope)
    branch_two = sum(dot_nn(a, w) for a, w in zip(acts, down_ws)) + f32(down_bias)
    block_out = (resid + branch_two).astype(BF)
    down_bias_grad = jnp.sum(grad_rows, 0)
    low_product = lambda a, b: dot_tn(a, b).astype(BF)
    down_grads, (block_out,) = beside(
        lambda xs, g: [low_product(a, g) for a in xs],
        (acts, grad_low),
        (move.swap_rows, block_out),
    )
    down = Reduction(move, table, *down_grads)
    (hg_own, up_b_own), _ = beside(hidden_grads, (grad_low, down_ws[0], slopes[0]), down)

    def others(g, hg_own):
        hg_oth, up_b_oth = hidden_grads(g, down_ws[1], slopes[1])
        return hg_oth, up_b_oth, [low_product(normed2, h) for h in (hg_own, hg_oth)]

    (hg_oth, up_b_oth, up_grads), _ = beside(others, (grad_low, hg_own), down)
    hidden_gs = [hg_own, hg_oth]
    up = Reduction(move, table, *up_grads)

    def middle(hidden_gs, grad_rows, normal2):
        normed2_grad = sum(dot_nt(hg, w) for hg, w in zip(hidden_gs, up_ws))
        resid_part, scale_grad, shift_grad = norm_back(normed2_grad, normal2, inv_two, ln2_gain)
        resid_grad = grad_rows + resid_part
        branch_grad = resid_grad.astype(BF)
        bias_grad = jnp.sum(branch_grad, 0, dtype=F32)
        return resid_grad, branch_grad, scale_grad, shift_grad, bias_grad

    (resid_grad, branch_grad, ln2_scale_grad, ln2_shift_grad, out_bias_grad), _ = beside(
        middle, (hidden_gs, grad_rows, normal2), up, down
    )
    (out_w_grads, out_gs), _ = beside(
        lambda xs, g: ([low_product(o, g) for o in xs], [dot_nt(g, w).astype(BF) for w in out_ws]),
        (outs, branch_grad),
        down,
    )
    proj = Reduction(move, table, *out_w_grads)

    def back(which, skip, count):
        q, kvs, log = ((q_own, kvs_own, log_own), (q_oth, kvs_oth, log_oth))[which]
        inputs = q, out_gs[which], outs[which], log, kvs
        return lambda *xs: attend_back(*xs, tables, skip, count), inputs

    def keys_of(x):
        return lambda xs: [move.over_core(g) for g in xs], [x[1][1], x[2][1]]

    def finish(parts, gots):
        dk = [key_sum(p[1][0], g[0], tables) for p, g in zip(parts, gots)]
        dv = [p[2][0] + g[1] for p, g in zip(parts, gots)]
        rows = jnp.concatenate([p[0] for p in parts] + dk + dv, axis=1)
        return rows, low_product(normed1, rows)

    half = pairs // 2
    first, _ = beside(*back(1, 0, half), up, down, proj)
    (down_block, first) = tie(down.done, first)
    down_all = move.gather(down_block)
    second, (first_got,) = beside(*back(1, half, half), keys_of(first), up, proj)
    third, (second_got,) = beside(*back(0, 0, half), keys_of(second), up, proj)
    (rows_oth, w_oth), (third_got,) = beside(
        lambda *x: finish(*x), ((first, second), (first_got, second_got)), keys_of(third), up, proj
    )
    up_block, third, down_all = tie(up.done, third, down_all)
    up_all = move.gather(up_block)
    (rows_a, w_a), (oth_got,) = beside(
        lambda *x: finish(*x), ((third,), (third_got,)), (move.over_core, move.core_send(w_oth)), proj
    )
    out_block, w_a = tie(proj.done, w_a)
    out_all = move.gather(out_block)
    chips = n_dp // 2

    def keep_of(half):
        blocks = half.reshape(chips, 2, half.shape[0] // n_dp, half.shape[1])
        return lax.dynamic_index_in_dim(blocks, move.core, 1, keepdims=False)

    fourth, (oth_got, a_got) = beside(
        *back(0, half, half),
        (move.over_y, keep_of(w_oth) + oth_got),
        (move.over_core, move.core_send(w_a)),
    )

    def columns(x, lo, hi):
        x = x.reshape(*x.shape[:-1], 3, part)
        return x[..., lo * LANES : hi * LANES].reshape(*x.shape[:-2], -1)

    def chip_split(total, level):
        bit = (move.me_dp >> (level + 1)) & 1
        blocks = total.reshape(total.shape[0] // 2, 2, *total.shape[1:])
        take = lambda b: lax.dynamic_index_in_dim(blocks, b, 1, keepdims=False)
        return take(bit), take(1 - bit)

    over_chip = lambda x, level: move.move(x, lambda dp, y: (dp ^ (2 << level), y))
    total_a = keep_of(w_a) + a_got + columns(oth_got, 0, half)
    keep_a, send_a = chip_split(total_a, 0)
    normed1_part, (fourth_got, a_got) = beside(
        lambda a, b: dot_nt(a, qkv_oth), (rows_oth, rows_a), keys_of(fourth), (lambda x: over_chip(x, 0), send_a)
    )
    keep_a, send_a = chip_split(keep_a + a_got, 1)
    (rows_b, w_b), (a_got,) = beside(
        lambda *x: finish(*x), ((fourth,), (fourth_got,)), (lambda x: over_chip(x, 1), send_a)
    )
    keep_a, send_a = chip_split(keep_a + a_got, 2)
    own_cols = lambda lo, hi: columns(qkv_own, lo, hi)

    def last(rows_a, rows_b, part_sum):
        normed1_grad = part_sum + dot_nt(rows_a, own_cols(0, half)) + dot_nt(rows_b, own_cols(half, pairs))
        input_part, scale_grad, shift_grad = norm_back(normed1_grad, normal1, inv_one, ln1_gain)
        return (resid_grad + input_part).astype(BF), scale_grad, shift_grad

    (in_grad, ln1_scale_grad, ln1_shift_grad), (b_got, a_got) = beside(
        last,
        (rows_a, rows_b, normed1_part),
        (move.over_core, move.core_send(w_b)),
        (lambda x: over_chip(x, 2), send_a),
    )
    total_a = keep_a + a_got
    total_b = keep_of(w_b) + b_got + columns(oth_got, half, pairs)
    in_grad = move.swap_rows(in_grad)
    for level in range(chips.bit_length() - 1):
        keep_b, send_b = chip_split(total_b, level)
        total_b = keep_b + over_chip(send_b, level)
    three = lambda x: x.reshape(x.shape[1], 3, -1)
    merged = jnp.concatenate([three(total_a), three(total_b)], axis=2).reshape(1, -1, 3 * part)
    qkv_g = move.gather(merged)
    colsum = lambda g: jnp.sum(g, 0, dtype=F32)
    b_own = jnp.concatenate(
        [colsum(g).reshape(3, -1) for g in (rows_a, rows_b)], axis=1
    ).reshape(-1)
    vec, flat = move.reduce_vectors(
        jnp.stack(
            [
                ln1_scale_grad,
                ln1_shift_grad,
                out_bias_grad,
                ln2_scale_grad,
                ln2_shift_grad,
                down_bias_grad,
            ]
        ),
        jnp.concatenate([b_own, up_b_own[0]]),
        jnp.concatenate([colsum(rows_oth), up_b_oth[0]]),
    )
    return (
        block_out,
        in_grad,
        vec[0],
        vec[1],
        f32(qkv_g).reshape(width, 3, part),
        flat[: 3 * part].reshape(3, part),
        f32(out_all),
        vec[2],
        vec[3],
        vec[4],
        f32(up_all),
        flat[3 * part :],
        f32(down_all),
        vec[5],
    )


def spread_device(*args):
    (block_in, ln1_scale, ln1_shift, qkv_weight, qkv_bias, out_weight, out_bias) = args[:7]
    (ln2_scale, ln2_shift, up_weight, up_bias, down_weight, down_bias, out_grad) = args[7:]
    gather = lambda w, axis: lax.all_gather(w, "tensor", axis=axis, tiled=True)
    scatter = lambda g, axis: lax.psum(
        lax.psum_scatter(g, "tensor", scatter_dimension=axis, tiled=True), "dp"
    ).astype(F32)
    width = qkv_weight.shape[0]
    qkv_all = gather(qkv_weight, 2)
    full = qkv_all.shape[2]
    out = block_step(
        Spread(block_in.shape[0]),
        block_in,
        ln1_scale,
        ln1_shift,
        [qkv_all.reshape(width, 3 * full)],
        [gather(qkv_bias, 1).reshape(3 * full)],
        [gather(out_weight, 0)],
        out_bias,
        ln2_scale,
        ln2_shift,
        [gather(up_weight, 1)],
        [gather(up_bias, 0)],
        [gather(down_weight, 0)],
        down_bias,
        out_grad,
    )
    block_out, in_grad, vectors, weight_grads, (qkv_b, up_b) = out
    ((qkv_g,), (out_g,), (up_g,), (down_g,)) = weight_grads
    vec = scatter(jnp.stack(vectors), 1)
    return (
        block_out,
        in_grad,
        vec[0],
        vec[1],
        scatter(qkv_g.reshape(width, 3, full), 2),
        scatter(qkv_b[0].reshape(3, full), 1),
        scatter(out_g, 0),
        vec[2],
        vec[3],
        vec[4],
        scatter(up_g, 1),
        scatter(up_b[0], 0),
        scatter(down_g, 0),
        vec[5],
    )


def solution(mesh):
    n_dp, n_tensor = mesh.shape["dp"], mesh.shape["tensor"]
    rows = P(("dp", "tensor"), None)
    vector = P("tensor")
    placed = (
        rows,
        P(),
        P(),
        P(None, None, "tensor"),
        P(None, "tensor"),
        P("tensor", None),
        P(),
        P(),
        P(),
        P(None, "tensor"),
        vector,
        P("tensor", None),
        P(),
        rows,
    )
    paired = n_tensor == 2 and n_dp >= 8 and n_dp & (n_dp - 1) == 0
    return jax.shard_map(
        functools.partial(paired_device, n_dp) if paired else spread_device,
        mesh=mesh,
        in_specs=placed,
        out_specs=(
            rows,
            rows,
            vector,
            vector,
            P(None, None, "tensor"),
            P(None, "tensor"),
            P("tensor", None),
            vector,
            vector,
            vector,
            P(None, "tensor"),
            vector,
            P("tensor", None),
            vector,
        ),
        check_vma=False,
    )
```

```python
import functools
import math

import jax
import jax.numpy as jnp
import numpy as np
from jax import lax
from jax.experimental import pallas as pl
from jax.experimental.pallas import tpu as pltpu
from jax.sharding import PartitionSpec as P

HD = 64
GH = 16
GW = 16
SEQ = 2048
EPS = 1e-06
LANES = 128
ROT = 2 * (HD // 3 // 2)
HALF_ROT = ROT // 2
LOG2E = math.log2(math.e)
SCALE = 1.0 / math.sqrt(HD)
BF = jnp.bfloat16
F32 = jnp.float32
VMEM_BYTES = 56 << 20


def dot_nt(left, right):
    return lax.dot_general(left, right, (((1,), (1,)), ((), ())), preferred_element_type=F32)


def dot_nn(left, right):
    return lax.dot_general(left, right, (((1,), (0,)), ((), ())), preferred_element_type=F32)


def dot_tn(left, right):
    return lax.dot_general(left, right, (((0,), (0,)), ((), ())), preferred_element_type=F32)


def call(kernel, flops, moved, exps=0, **kw):
    return pl.pallas_call(
        kernel,
        compiler_params=pltpu.CompilerParams(vmem_limit_bytes=VMEM_BYTES),
        cost_estimate=pl.CostEstimate(flops=flops, bytes_accessed=moved, transcendentals=exps),
        **kw,
    )


def rotary_tables(first, count):
    lane = np.arange(LANES) % HD
    axis = lane // ROT
    inside = lane % ROT
    freq = np.float32(10000.0) ** (
        -(inside % HALF_ROT).astype(np.float32) / np.float32(HALF_ROT)
    )
    turned = axis < 3
    early = turned & (inside < HALF_ROT)
    late = turned & (inside >= HALF_ROT)
    index = first + jnp.arange(count, dtype=jnp.int32)[:, None]
    places = (index // (GH * GW), index // GW % GH, index % GW)
    place = jnp.where(axis == 0, places[0], jnp.where(axis == 1, places[1], places[2]))
    angle = place.astype(F32) * freq.astype(np.float32)[None, :]
    cos = jnp.where(turned, jnp.cos(angle), 1.0)
    sin = jnp.sin(angle)
    return cos, jnp.where(early, -sin, 0.0), jnp.where(late, sin, 0.0)


def turn(x, cos, sin_a, sin_b):
    return (
        x * cos
        + pltpu.roll(x, LANES - HALF_ROT, 1) * sin_a
        + pltpu.roll(x, HALF_ROT, 1) * sin_b
    )


def turn_back(g, cos, sin_a, sin_b):
    return (
        g * cos
        + pltpu.roll(g * sin_b, LANES - HALF_ROT, 1)
        + pltpu.roll(g * sin_a, HALF_ROT, 1)
    )


def norm_kernel(x_ref, scale_ref, shift_ref, n_ref, nt_ref):
    normed, _, _ = norm_parts(x_ref[...].astype(F32), scale_ref[...], shift_ref[...])
    n_ref[...] = normed.astype(BF)
    nt_ref[...] = normed.T.astype(BF)


def norm_rows(x, scale, shift):
    tokens, width = x.shape
    rows = min(256, tokens)
    vector = pl.BlockSpec((1, width), lambda i: (0, 0))
    tile = pl.BlockSpec((rows, width), lambda i: (i, 0))
    return call(
        norm_kernel,
        10 * tokens * width,
        6 * tokens * width,
        grid=(tokens // rows,),
        in_specs=[tile, vector, vector],
        out_specs=[tile, pl.BlockSpec((width, rows), lambda i: (0, i))],
        out_shape=[
            jax.ShapeDtypeStruct((tokens, width), BF),
            jax.ShapeDtypeStruct((width, tokens), BF),
        ],
    )(x, scale, shift)


def qkv_kernel(n_ref, w_ref, b_ref, c_ref, sa_ref, sb_ref, q_ref, kv_ref, *, q_steps):
    step = pl.program_id(0)
    weight = w_ref[...].reshape(n_ref.shape[1], w_ref.shape[-1])
    rows = dot_nn(n_ref[...], weight) + b_ref[...]
    wide = rows.shape[1]

    def turned():
        tables = (c_ref[...], sa_ref[...], sb_ref[...])
        parts = [
            turn(rows[:, at : at + LANES], *tables).astype(BF) for at in range(0, wide, LANES)
        ]
        return jnp.concatenate(parts, axis=1)

    @pl.when(step < q_steps)
    def _():
        q_ref[...] = turned()

    @pl.when((step >= q_steps) & (step < 2 * q_steps))
    def _():
        kv_ref[...] = turned()

    @pl.when(step >= 2 * q_steps)
    def _():
        kv_ref[...] = rows.astype(BF)


def qkv_rows(normed, weight, bias, tables):
    tokens, width = normed.shape
    groups, _, deep, cols = weight.shape
    tile = next(t for t in (512, 256, LANES) if cols % t == 0)
    q_steps = cols // tile
    whole = lambda n: (0, 0)
    return call(
        functools.partial(qkv_kernel, q_steps=q_steps),
        2 * tokens * width * 3 * cols,
        2 * (tokens * width + width * 3 * cols + tokens * 3 * cols),
        grid=(3 * q_steps,),
        in_specs=[
            pl.BlockSpec((tokens, width), whole),
            pl.BlockSpec((groups, None, deep, tile), lambda n: (0, n // q_steps, 0, n % q_steps)),
            pl.BlockSpec((1, tile), lambda n: (0, n)),
        ]
        + [pl.BlockSpec((tokens, LANES), whole)] * 3,
        out_specs=[
            pl.BlockSpec((tokens, tile), lambda n: (0, jnp.minimum(n, q_steps - 1))),
            pl.BlockSpec((tokens, tile), lambda n: (0, jnp.maximum(n - q_steps, 0))),
        ],
        out_shape=[
            jax.ShapeDtypeStruct((tokens, cols), BF),
            jax.ShapeDtypeStruct((tokens, 2 * cols), BF),
        ],
    )(normed, weight, bias, *tables)


def attend_kernel(*refs, sources, rows_at):
    q_ref = refs[0]
    k_refs = refs[1 : 1 + sources]
    v_refs = refs[1 + sources : 1 + 2 * sources]
    o_ref, lse_ref = refs[1 + 2 * sources : 3 + 2 * sources]
    wide_refs = refs[3 + 2 * sources :]
    lane = lax.broadcasted_iota(jnp.int32, (1, LANES), 1)
    for v, wide in zip(v_refs, wide_refs):
        wide[:, :LANES] = v[...]
        wide[:, LANES:] = jnp.ones_like(v)

    def scores_of(q, head):
        q_head = jnp.where((lane // HD) == head, q, jnp.zeros_like(q))
        return [dot_nt(q_head, k[...]) for k in k_refs]

    def result(scores):
        peak = functools.reduce(
            jnp.maximum, [jnp.max(s, axis=1, keepdims=True) for s in scores]
        )
        weights = [jnp.exp2((s - peak) * (SCALE * LOG2E)).astype(BF) for s in scores]
        both = sum(dot_nn(w, v[...]) for w, v in zip(weights, wide_refs))
        total = both[:, LANES : LANES + 1]
        return both[:, :LANES] / both[:, LANES:], peak * (SCALE * LOG2E) + jnp.log2(total)

    for first in range(0, q_ref.shape[0], rows_at):
        rows = slice(first, first + rows_at)
        q = q_ref[rows, :]
        (out_0, log_0), (out_1, log_1) = [result(s) for s in [scores_of(q, h) for h in range(2)]]
        early = lane < HD
        o_ref[rows, :] = jnp.where(early, out_0, out_1).astype(BF)
        logs = jnp.where(early, log_0, log_1).T
        lse_ref[0, 0:1, rows] = logs[0:1]
        lse_ref[0, 1:2, rows] = logs[HD : HD + 1]


def attend(q, kvs, skip=0, pairs=None):
    tokens, cols = q.shape
    all_pairs = cols // LANES
    pairs = pairs or all_pairs
    cols = pairs * LANES
    keys = sum(kv.shape[0] for kv in kvs)
    q_spec = pl.BlockSpec((tokens, LANES), lambda i: (0, skip + i))
    k_specs = [pl.BlockSpec((kv.shape[0], LANES), lambda i: (0, skip + i)) for kv in kvs]
    v_specs = [
        pl.BlockSpec((kv.shape[0], LANES), lambda i: (0, all_pairs + skip + i)) for kv in kvs
    ]
    return call(
        functools.partial(attend_kernel, sources=len(kvs), rows_at=min(512, tokens)),
        4 * 4 * tokens * keys * cols,
        2 * (2 * tokens * cols + 2 * keys * cols),
        tokens * keys * 2 * pairs,
        grid=(pairs,),
        in_specs=[q_spec] + k_specs + v_specs,
        out_specs=[
            pl.BlockSpec((tokens, LANES), lambda i: (0, i)),
            pl.BlockSpec((1, 2, tokens), lambda i: (i, 0, 0)),
        ],
        out_shape=[
            jax.ShapeDtypeStruct((tokens, cols), BF),
            jax.ShapeDtypeStruct((pairs, 2, tokens), F32),
        ],
        scratch_shapes=[pltpu.VMEM((kv.shape[0], 2 * LANES), BF) for kv in kvs],
    )(q, *kvs, *kvs)


def attend_back_kernel(*refs, sources, keys_at, queries_at):
    q_ref, do_ref, o_ref, lse_ref, c_ref, sa_ref, sb_ref = refs[:7]
    at = 7
    k_refs = refs[at : at + sources]
    v_refs = refs[at + sources : at + 2 * sources]
    at += 2 * sources
    dq_ref = refs[at]
    dk_refs = refs[at + 1 : at + 1 + sources]
    dv_refs = refs[at + 1 + sources : at + 1 + 2 * sources]
    dq_acc, centre = refs[at + 1 + 2 * sources :]
    lane = lax.broadcasted_iota(jnp.int32, (1, LANES), 1)
    tokens = q_ref.shape[0]
    product = (do_ref[...].astype(F32) * o_ref[...].astype(F32)).T
    for head in range(2):
        centre[head : head + 1, :] = jnp.sum(
            product[head * HD : head * HD + HD], axis=0, keepdims=True
        )
    dq_acc[...] = jnp.zeros_like(dq_acc)
    for k_ref, v_ref, dk_ref, dv_ref in zip(k_refs, v_refs, dk_refs, dv_refs):

        def body(j, carry):
            rows = pl.ds(pl.multiple_of(j * keys_at, keys_at), keys_at)
            k, v = k_ref[rows, :], v_ref[rows, :]
            k_t = k.astype(F32).T.astype(BF)
            dv = jnp.zeros((keys_at, LANES), F32)
            dk = jnp.zeros((keys_at, LANES), F32)

            def products(cut, head):
                mine = (lane // HD) == head
                q, do = q_ref[cut, :], do_ref[cut, :]
                q_head = jnp.where(mine, q, jnp.zeros_like(q))
                do_head = jnp.where(mine, do, jnp.zeros_like(do))
                return q_head, do_head, dot_nt(k, q_head), dot_nt(v, do_head)

            steps = [
                (slice(first, first + queries_at), head)
                for first in range(0, tokens, queries_at)
                for head in range(2)
            ]
            later = products(*steps[0])
            for at, (cut, head) in enumerate(steps):
                q_head, do_head, scores, share_grad = later
                if at + 1 < len(steps):
                    later = products(*steps[at + 1])
                shares = jnp.exp2(scores * (SCALE * LOG2E) - lse_ref[0, head : head + 1, cut])
                score_grad = (shares * (share_grad - centre[head : head + 1, cut])).astype(BF)
                dv += dot_nn(shares.astype(BF), do_head)
                dk += dot_nn(score_grad, q_head)
                part = slice(head * HD, head * HD + HD)
                dq_acc[part, cut] += dot_nn(k_t[part], score_grad)
            dv_ref[rows, :] = dv.astype(BF)
            dk_ref[rows, :] = (dk * SCALE).astype(BF)
            return carry

        lax.fori_loop(0, k_ref.shape[0] // keys_at, body, 0)
    dq = (dq_acc[...] * SCALE).T
    dq_ref[...] = turn_back(dq, c_ref[...], sa_ref[...], sb_ref[...]).astype(BF)


def attend_back(q, out_grad, out, lse, kvs, tables, skip=0, pairs=None, at=0):
    tokens, cols = q.shape
    all_pairs = cols // LANES
    pairs = pairs or all_pairs
    cols = pairs * LANES
    keys = sum(kv.shape[0] for kv in kvs)
    q_spec = pl.BlockSpec((tokens, LANES), lambda i: (0, skip + i))
    o_spec = pl.BlockSpec((tokens, LANES), lambda i: (0, at + i))
    k_specs = [pl.BlockSpec((kv.shape[0], LANES), lambda i: (0, skip + i)) for kv in kvs]
    v_specs = [
        pl.BlockSpec((kv.shape[0], LANES), lambda i: (0, all_pairs + skip + i)) for kv in kvs
    ]
    dq_spec = pl.BlockSpec((tokens, LANES), lambda i: (0, i))
    dk_specs = [pl.BlockSpec((kv.shape[0], LANES), lambda i: (0, i)) for kv in kvs]
    table = pl.BlockSpec((tokens, LANES), lambda i: (0, 0))
    outs = call(
        functools.partial(
            attend_back_kernel, sources=len(kvs), keys_at=1024, queries_at=min(256, tokens)
        ),
        10 * 4 * tokens * keys * cols,
        2 * (4 * tokens * cols + 4 * keys * cols),
        tokens * keys * 2 * pairs,
        grid=(pairs,),
        in_specs=[q_spec, o_spec, o_spec]
        + [pl.BlockSpec((1, 2, tokens), lambda i: (at + i, 0, 0))]
        + [table] * 3
        + k_specs
        + v_specs,
        out_specs=[dq_spec] + dk_specs + dk_specs,
        out_shape=[jax.ShapeDtypeStruct((tokens, cols), BF)]
        + [jax.ShapeDtypeStruct((kv.shape[0], cols), BF) for kv in kvs] * 2,
        scratch_shapes=[pltpu.VMEM((LANES, tokens), F32), pltpu.VMEM((2, tokens), F32)],
    )(q, out_grad, out, lse, *tables, *kvs, *kvs)
    n = len(kvs)
    return outs[0], outs[1 : 1 + n], outs[1 + n :]


def key_sum_kernel(own_ref, got_ref, c_ref, sa_ref, sb_ref, dk_ref):
    total = own_ref[...].astype(F32) + got_ref[...].astype(F32)
    dk_ref[...] = turn_back(total, c_ref[...], sa_ref[...], sb_ref[...]).astype(BF)


def key_sum(own, got, tables):
    tokens, cols = own.shape
    spec = pl.BlockSpec((tokens, LANES), lambda i: (0, i))
    table = pl.BlockSpec((tokens, LANES), lambda i: (0, 0))
    return call(
        key_sum_kernel,
        12 * tokens * cols,
        6 * tokens * cols,
        grid=(cols // LANES,),
        in_specs=[spec, spec] + [table] * 3,
        out_specs=spec,
        out_shape=jax.ShapeDtypeStruct((tokens, cols), BF),
    )(own, got, *tables)


def gelu_parts(hidden):
    cdf = 0.5 + 0.5 * lax.erf(hidden * (1.0 / math.sqrt(2.0)))
    bell = jnp.exp2(hidden * hidden * (-0.5 * LOG2E))
    return hidden * cdf, cdf + hidden * (1.0 / math.sqrt(2.0 * math.pi)) * bell


def up_kernel(n_ref, w_ref, b_ref, acted_ref, slope_ref):
    hidden = dot_nn(n_ref[...], w_ref[...]) + b_ref[...]
    acted, slope = gelu_parts(hidden)
    acted_ref[...] = acted.astype(BF)
    slope_ref[...] = slope.astype(BF)


def up_rows(normed, weight, bias):
    tokens, width = normed.shape
    cols = weight.shape[1]
    tile = 512
    out = pl.BlockSpec((tokens, tile), lambda n: (0, n))
    return call(
        up_kernel,
        2 * tokens * width * cols,
        2 * (tokens * width + width * cols + 2 * tokens * cols),
        tokens * cols,
        grid=(cols // tile,),
        in_specs=[
            pl.BlockSpec((tokens, width), lambda n: (0, 0)),
            pl.BlockSpec((width, tile), lambda n: (0, n)),
            pl.BlockSpec((1, tile), lambda n: (0, n)),
        ],
        out_specs=[out, out],
        out_shape=[jax.ShapeDtypeStruct((tokens, cols), BF)] * 2,
    )(normed, weight, bias)


def hidden_grad_kernel(g_ref, w_ref, slope_ref, hg_ref, sum_ref, *, skip):
    weight = w_ref[:, skip:].reshape(hg_ref.shape[1], g_ref.shape[1])
    grad = dot_nt(g_ref[...], weight) * slope_ref[...].astype(F32)
    low = grad.astype(BF)
    hg_ref[...] = low
    sum_ref[...] = jnp.sum(low.astype(F32), axis=0, keepdims=True)


def hidden_grads(grad, down, slope):
    tokens, width = grad.shape
    down, skip = down
    groups, deep, _ = down.shape
    cols = slope.shape[1]
    tile = 512
    out = pl.BlockSpec((tokens, tile), lambda n: (0, n))
    if groups == 1:
        weight = pl.BlockSpec((1, tile, width), lambda n: (0, n, 0))
    else:
        weight = pl.BlockSpec((tile // (deep - skip), deep, width), lambda n: (n, 0, 0))
    return call(
        functools.partial(hidden_grad_kernel, skip=skip),
        2 * tokens * width * cols,
        2 * (tokens * width + width * cols + 2 * tokens * cols),
        grid=(cols // tile,),
        in_specs=[pl.BlockSpec((tokens, width), lambda n: (0, 0)), weight, out],
        out_specs=[out, pl.BlockSpec((1, tile), lambda n: (0, n))],
        out_shape=[
            jax.ShapeDtypeStruct((tokens, cols), BF),
            jax.ShapeDtypeStruct((1, cols), F32),
        ],
    )(grad, down, slope)


def norm_parts(values, gain, shift):
    centred = values - jnp.mean(values, axis=-1, keepdims=True)
    inv_dev = lax.rsqrt(jnp.mean(centred * centred, axis=-1, keepdims=True) + EPS)
    normal = centred * inv_dev
    return normal * gain + shift, normal, inv_dev


def norm_back(upstream, normal, inv_dev, gain):
    scaled = upstream * gain
    mean_first = jnp.mean(scaled, axis=-1, keepdims=True)
    mean_second = jnp.mean(scaled * normal, axis=-1, keepdims=True)
    back = inv_dev * (scaled - mean_first - normal * mean_second)
    return back, jnp.sum(upstream * normal, 0), jnp.sum(upstream, 0)


def tie(*trees):
    leaves, form = jax.tree.flatten(trees)
    return jax.tree.unflatten(form, lax.optimization_barrier(tuple(leaves)))


def project_kernel(*refs, parts):
    x_ref, b_ref, scale_ref, shift_ref = refs[:4]
    o_refs, w_refs = refs[4 : 4 + parts], refs[4 + parts : 4 + 2 * parts]
    resid_ref, n_ref, nt_ref = refs[4 + 2 * parts :]
    resid = x_ref[...].astype(F32) + b_ref[...]
    for o, w in zip(o_refs, w_refs):
        resid += dot_nn(o[...], w[...])
    normed, _, _ = norm_parts(resid, scale_ref[...], shift_ref[...])
    resid_ref[...] = resid
    n_ref[...] = normed.astype(BF)
    nt_ref[...] = normed.T.astype(BF)


def project_rows(x, bias, scale, shift, outs, weights):
    tokens, width = x.shape
    rows = min(256, tokens)
    vector = pl.BlockSpec((1, width), lambda i: (0, 0))
    tile = pl.BlockSpec((rows, width), lambda i: (i, 0))
    deep = sum(o.shape[1] for o in outs)
    return call(
        functools.partial(project_kernel, parts=len(outs)),
        2 * tokens * width * deep,
        2 * (tokens * deep + width * deep + 5 * tokens * width),
        grid=(tokens // rows,),
        in_specs=[tile, vector, vector, vector]
        + [pl.BlockSpec((rows, o.shape[1]), lambda i: (i, 0)) for o in outs]
        + [pl.BlockSpec(w.shape, lambda i: (0, 0)) for w in weights],
        out_specs=[tile, tile, pl.BlockSpec((width, rows), lambda i: (0, i))],
        out_shape=[
            jax.ShapeDtypeStruct((tokens, width), F32),
            jax.ShapeDtypeStruct((tokens, width), BF),
            jax.ShapeDtypeStruct((width, tokens), BF),
        ],
    )(x, bias, scale, shift, *outs, *weights)


def down_kernel(r_ref, b_ref, *refs, parts, skips):
    total = r_ref[...] + b_ref[...]
    for a, w, skip in zip(refs[:parts], refs[parts : 2 * parts], skips):
        total += dot_nn(a[...], w[:, skip:].reshape(a.shape[1], w.shape[2]))
    refs[-1][...] = total.astype(BF)


def down_rows(resid, bias, acts, weights):
    tokens, width = resid.shape
    weights, skips = zip(*weights)
    cols = min(512, width)
    tile = pl.BlockSpec((tokens, cols), lambda i: (0, i))
    deep = sum(a.shape[1] for a in acts)
    return call(
        functools.partial(down_kernel, parts=len(acts), skips=skips),
        2 * tokens * width * deep,
        2 * (tokens * deep + width * deep + 3 * tokens * width),
        grid=(width // cols,),
        in_specs=[tile, pl.BlockSpec((1, cols), lambda i: (0, i))]
        + [pl.BlockSpec(a.shape, lambda i: (0, 0)) for a in acts]
        + [pl.BlockSpec((*w.shape[:2], cols), lambda i: (0, 0, i)) for w in weights],
        out_specs=tile,
        out_shape=jax.ShapeDtypeStruct((tokens, width), BF),
    )(resid, bias, *acts, *weights)


def middle_kernel(r_ref, g_ref, scale_ref, *refs, parts):
    branch_ref, sums_ref = refs[-2:]
    upstream = sum(dot_nt(h[...], w[...]) for h, w in zip(refs[:parts], refs[parts : 2 * parts]))
    grad = g_ref[...].astype(F32)
    _, normal, inv_dev = norm_parts(r_ref[...], 1.0, 0.0)
    back, scale_sum, shift_sum = norm_back(upstream, normal, inv_dev, scale_ref[...])
    branch = (grad + back).astype(BF)
    branch_ref[...] = branch
    total = lambda v: jnp.sum(v, axis=0, keepdims=True)
    sums = [scale_sum[None, :], shift_sum[None, :], total(branch.astype(F32)), total(grad)]
    sums = jnp.concatenate(sums + [jnp.zeros((4, grad.shape[1]), F32)], axis=0)

    @pl.when(pl.program_id(0) == 0)
    def _():
        sums_ref[...] = sums

    @pl.when(pl.program_id(0) > 0)
    def _():
        sums_ref[...] += sums


def middle_rows(resid, grad, scale, hidden_gs, weights):
    tokens, width = resid.shape
    rows = min(256, tokens)
    tile = pl.BlockSpec((rows, width), lambda i: (i, 0))
    deep = sum(h.shape[1] for h in hidden_gs)
    return call(
        functools.partial(middle_kernel, parts=len(hidden_gs)),
        2 * tokens * width * deep,
        2 * (tokens * deep + width * deep + 4 * tokens * width),
        grid=(tokens // rows,),
        in_specs=[tile, tile, pl.BlockSpec((1, width), lambda i: (0, 0))]
        + [pl.BlockSpec((rows, h.shape[1]), lambda i: (i, 0)) for h in hidden_gs]
        + [pl.BlockSpec(w.shape, lambda i: (0, 0)) for w in weights],
        out_specs=[tile, pl.BlockSpec((8, width), lambda i: (0, 0))],
        out_shape=[
            jax.ShapeDtypeStruct((tokens, width), BF),
            jax.ShapeDtypeStruct((8, width), F32),
        ],
    )(resid, grad, scale, *hidden_gs, *weights)


def add_parts(total, refs, weights, units):
    for (w_ref, lo, count), start in zip(weights, units):
        for kind in range(3):
            parts = [refs[start + 3 * u + kind][...] for u in range(count)]
            cols = sum(p.shape[1] for p in parts)
            weight = w_ref[:, kind, :, lo : lo + cols].reshape(total.shape[1], cols)
            total += dot_nt(jnp.concatenate(parts, axis=1), weight)
    return total


def early_kernel(own_ref, oth_ref, *refs, units, cols):
    out_ref = refs[-1]
    weights = [(own_ref, 0, 1), (oth_ref, 0, units)]
    out_ref[...] = add_parts(jnp.zeros(out_ref.shape, F32), refs, weights, (0, 3))


def last_kernel(x_ref, g_ref, scale_ref, part_ref, own_ref, *refs, cols):
    in_grad_ref, sums_ref = refs[-2:]
    upstream = add_parts(part_ref[...], refs, [(own_ref, cols, 1)], (0,))
    _, normal, inv_dev = norm_parts(x_ref[...].astype(F32), 1.0, 0.0)
    back, scale_sum, shift_sum = norm_back(upstream, normal, inv_dev, scale_ref[...])
    in_grad_ref[...] = (g_ref[...].astype(F32) + back).astype(BF)
    sums = [scale_sum[None, :], shift_sum[None, :], jnp.zeros((6, x_ref.shape[1]), F32)]
    sums = jnp.concatenate(sums, axis=0)

    @pl.when(pl.program_id(0) == 0)
    def _():
        sums_ref[...] = sums

    @pl.when(pl.program_id(0) > 0)
    def _():
        sums_ref[...] += sums


def early_rows(own, oth, own_unit, oth_units):
    flat = list(own_unit) + [p for unit in oth_units for p in unit]
    tokens, cols = flat[0].shape
    width = own.shape[0] * own.shape[2]
    rows = min(512, tokens)
    return call(
        functools.partial(early_kernel, units=len(oth_units), cols=cols),
        2 * tokens * width * cols * len(flat),
        2 * (tokens * cols * len(flat) + width * cols * len(flat) + 2 * tokens * width),
        grid=(tokens // rows,),
        in_specs=[pl.BlockSpec(w.shape, lambda i: (0, 0, 0, 0)) for w in (own, oth)]
        + [pl.BlockSpec((rows, cols), lambda i: (i, 0)) for p in flat],
        out_specs=pl.BlockSpec((rows, width), lambda i: (i, 0)),
        out_shape=jax.ShapeDtypeStruct((tokens, width), F32),
    )(own, oth, *flat)


def last_rows(x, branch_grad, scale, partial, own, unit):
    tokens, width = x.shape
    cols = unit[0].shape[1]
    rows = min(256, tokens)
    tile = pl.BlockSpec((rows, width), lambda i: (i, 0))
    return call(
        functools.partial(last_kernel, cols=cols),
        6 * tokens * width * cols,
        2 * (3 * tokens * cols + 3 * width * cols + 5 * tokens * width),
        grid=(tokens // rows,),
        in_specs=[tile, tile, pl.BlockSpec((1, width), lambda i: (0, 0)), tile]
        + [pl.BlockSpec(own.shape, lambda i: (0, 0, 0, 0))]
        + [pl.BlockSpec((rows, cols), lambda i: (i, 0))] * 3,
        out_specs=[tile, pl.BlockSpec((8, width), lambda i: (0, 0))],
        out_shape=[
            jax.ShapeDtypeStruct((tokens, width), BF),
            jax.ShapeDtypeStruct((8, width), F32),
        ],
    )(x, branch_grad, scale, partial, own, *unit)


def unit_kernel(t_ref, nt_ref, dq_ref, dk_ref, gk_ref, dv_ref, gv_ref, c_ref, sa_ref, sb_ref, *refs, chips):
    keep_ref, send_ref, dk_out, dv_out, sum_ref, rows_ref, acc_ref = refs
    kind = pl.program_id(0)
    added = lambda a, b: a[...].astype(F32) + b[...].astype(F32)

    @pl.when(kind == 0)
    def _():
        rows_ref[...] = dq_ref[...]

    @pl.when(kind == 1)
    def _():
        total = added(dk_ref, gk_ref)
        tables = (c_ref[...], sa_ref[...], sb_ref[...])
        for at in range(0, total.shape[1], LANES):
            cut = slice(at, at + LANES)
            rows_ref[:, cut] = turn_back(total[:, cut], *tables).astype(BF)
        dk_out[...] = rows_ref[...]

    @pl.when(kind == 2)
    def _():
        rows_ref[...] = added(dv_ref, gv_ref).astype(BF)
        dv_out[...] = rows_ref[...]

    rows = rows_ref[...]
    acc_ref[...] = dot_nn(nt_ref[...], rows)
    piece = keep_ref.shape[1]
    for place in range(chips):
        for ref, which in ((keep_ref, place), (send_ref, chips + place)):
            at = pl.multiple_of(t_ref[which] * piece, piece)
            ref[place] = acc_ref[pl.ds(at, piece), :].astype(BF)
    sums = jnp.sum(rows.astype(F32), axis=0, keepdims=True)
    sum_ref[...] = jnp.broadcast_to(sums, sum_ref.shape)


def unit_grads(table, normed_t, dq, dk, got_k, dv, got_v, tables):
    width, tokens = normed_t.shape
    cols = dq.shape[1]
    chips = table.shape[0] // 2
    piece = width // (2 * chips)
    part = pl.BlockSpec((tokens, cols), lambda i, t: (0, 0))
    rotary = pl.BlockSpec((tokens, LANES), lambda i, t: (0, 0))
    blocks = pl.BlockSpec((chips, None, piece, cols), lambda i, t: (0, i, 0, 0))
    return pl.pallas_call(
        functools.partial(unit_kernel, chips=chips),
        grid_spec=pltpu.PrefetchScalarGridSpec(
            num_scalar_prefetch=1,
            grid=(3,),
            in_specs=[pl.BlockSpec((width, tokens), lambda i, t: (0, 0))] + [part] * 5 + [rotary] * 3,
            out_specs=[blocks, blocks, part, part, pl.BlockSpec((8, cols), lambda i, t: (0, i))],
            scratch_shapes=[pltpu.VMEM((tokens, cols), BF), pltpu.VMEM((width, cols), F32)],
        ),
        out_shape=[jax.ShapeDtypeStruct((chips, 3, piece, cols), BF)] * 2
        + [jax.ShapeDtypeStruct((tokens, cols), BF)] * 2
        + [jax.ShapeDtypeStruct((8, 3 * cols), F32)],
        compiler_params=pltpu.CompilerParams(vmem_limit_bytes=VMEM_BYTES),
        cost_estimate=pl.CostEstimate(
            flops=6 * tokens * width * cols,
            bytes_accessed=2 * (tokens * width + 7 * tokens * cols + 3 * width * cols),
            transcendentals=0,
        ),
    )(table, normed_t, dq, dk, got_k, dv, got_v, *tables)


def widen_kernel(t_ref, a_ref, b_ref, out_ref):
    count, piece, cols = a_ref.shape
    out_ref[:, :cols] = a_ref[...].reshape(out_ref.shape[0], cols).astype(F32)
    for place in range(count):
        rows = pl.ds(pl.multiple_of(t_ref[place] * piece, piece), piece)
        out_ref[rows, cols:] = b_ref[place].astype(F32)


def widen(table, unit_a, unit_b):
    n, _, piece, cols = unit_a.shape
    spec = pl.BlockSpec((n, None, piece, cols), lambda i, t: (0, i, 0, 0))
    return pl.pallas_call(
        widen_kernel,
        grid_spec=pltpu.PrefetchScalarGridSpec(
            num_scalar_prefetch=1,
            grid=(3,),
            in_specs=[spec, spec],
            out_specs=pl.BlockSpec((None, n * piece, 2 * cols), lambda i, t: (i, 0, 0)),
        ),
        out_shape=jax.ShapeDtypeStruct((3, n * piece, 2 * cols), F32),
        compiler_params=pltpu.CompilerParams(vmem_limit_bytes=VMEM_BYTES),
        cost_estimate=pl.CostEstimate(
            flops=0, bytes_accessed=36 * n * piece * cols, transcendentals=0
        ),
    )(table, unit_a, unit_b)


def split_kernel(t_ref, own_m, own_f, oth_m, oth_f, got_om, got_of, got_tm, got_tf, ka, kb, sa, sb, *, last):
    total = lambda a, b: (a[...].astype(F32) + b[...].astype(F32)).astype(BF)
    by_y = t_ref[last] == 0
    own_far, oth_me = total(own_f, got_of), total(oth_m, got_tm)
    ka[...] = total(own_m, got_om)
    kb[...] = jnp.where(by_y, own_far, oth_me)
    sa[...] = jnp.where(by_y, oth_me, own_far)
    sb[...] = total(oth_f, got_tf)


def first_split(table, own, oth, got_own, got_oth):
    chips, piece, cols = got_own.shape
    count = chips // 2
    own, oth = (g.reshape(chips, 2, piece, cols) for g in (own, oth))
    whole = lambda far: pl.BlockSpec(
        (None, None, piece, cols), lambda i, t: (t[far * count + i], t[2 * count], 0, 0)
    )
    part = lambda far: pl.BlockSpec((None, piece, cols), lambda i, t: (t[far * count + i], 0, 0))
    out = pl.BlockSpec((None, piece, cols), lambda i, t: (i, 0, 0))
    return pl.pallas_call(
        functools.partial(split_kernel, last=2 * count),
        grid_spec=pltpu.PrefetchScalarGridSpec(
            num_scalar_prefetch=1,
            grid=(count,),
            in_specs=[whole(0), whole(1)] * 2 + [part(0), part(1)] * 2,
            out_specs=[out] * 4,
        ),
        out_shape=[jax.ShapeDtypeStruct((count, piece, cols), BF)] * 4,
        compiler_params=pltpu.CompilerParams(vmem_limit_bytes=VMEM_BYTES),
        cost_estimate=pl.CostEstimate(
            flops=4 * count * piece * cols, bytes_accessed=24 * count * piece * cols, transcendentals=0
        ),
    )(table, own, own, oth, oth, got_own, got_own, got_oth, got_oth)


class Paired:
    def __init__(self, n_dp):
        self.n_dp = n_dp
        self.me_dp = lax.axis_index("dp")
        self.me_y = lax.axis_index("tensor")
        self.core = self.me_dp % 2
        self.first = self.core * (SEQ // 2)
        chips = n_dp // 2
        levels = chips.bit_length() - 1
        places = np.arange(chips)
        far = sum(((places >> (levels - 1 - k)) & 1) << k for k in range(levels))
        chip = jnp.asarray(far, jnp.int32) ^ (self.me_dp // 2)
        self.blocks = jnp.concatenate([chip * 2 + self.core, chip * 2 + 1 - self.core]).astype(
            jnp.int32
        )

    def move(self, x, to):
        pairs = []
        for dp in range(self.n_dp):
            for y in range(2):
                a, b = to(dp, y)
                pairs.append((dp * 2 + y, a * 2 + b))
        return lax.ppermute(x, ("dp", "tensor"), pairs)

    def swap_rows(self, rows):
        return self.move(rows, lambda dp, y: (dp - dp % 2 + y, dp % 2))

    def over_y(self, x):
        return self.move(x, lambda dp, y: (dp, 1 - y))

    def over_core(self, x):
        return self.move(x, lambda dp, y: (dp ^ 1, y))

    def piece(self, own, axis=0):
        rows = own.shape[axis] // self.n_dp
        return lax.dynamic_slice_in_dim(own, self.me_dp * rows, rows, axis)

    def spread(self, got):
        return lax.all_gather(got, "dp", axis=0, tiled=True)

    def core_send(self, half):
        rows, cols = half.shape
        blocks = half.reshape(self.n_dp // 2, 2, rows // self.n_dp, cols)
        return lax.dynamic_index_in_dim(blocks, 1 - self.core, 1, keepdims=False)

    def over_chip(self, x, level):
        return self.move(x, lambda dp, y: (dp ^ (2 << level), y))

    def over_first(self, x):
        return self.move(x, lambda dp, y: (dp ^ 2, y) if dp % 2 else (dp, 1 - y))

    def over_second(self, x):
        return self.move(x, lambda dp, y: (dp, 1 - y) if dp % 2 else (dp ^ 2, y))

    def over_z(self, x, level):
        return self.move(x, lambda dp, y: (dp ^ (4 << level), y))

    def blocks_of(self, x_bit):
        count = self.n_dp // 4
        levels = count.bit_length() - 1
        z = self.me_dp // 4
        places = np.arange(count)
        far = sum(((places >> (levels - 1 - k)) & 1) << k for k in range(levels))
        return (jnp.asarray(far, jnp.int32) ^ z) * 2 + x_bit

    def table(self):
        x = (self.me_dp // 2) % 2
        me, far = self.blocks_of(x), self.blocks_of(1 - x)
        return jnp.concatenate([me, far, jnp.stack([self.core])]).astype(jnp.int32)

    def gather(self, block):
        return lax.all_gather(block[0], "dp", axis=0, tiled=True)

    def reduce_vectors(self, both, own, other):
        k, width = both.shape
        both = both.reshape(k, 2, width // 2)
        take = lambda b: lax.dynamic_index_in_dim(both, b, 1, keepdims=False).reshape(-1)
        mine = jnp.concatenate([take(self.me_y), own]).reshape(-1, LANES)
        theirs = jnp.concatenate([take(1 - self.me_y), other]).reshape(-1, LANES)
        total = jnp.stack([mine, theirs])
        total = total + self.over_core(total)
        for level in range((self.n_dp // 2).bit_length() - 1):
            total = total + self.over_chip(total, level)
        total = (total[0] + self.over_y(total[1])).reshape(-1)
        return total[: k * width // 2].reshape(k, width // 2), total[k * width // 2 :]


class Spread:
    def __init__(self, tokens):
        self.first = lax.axis_index("tensor") * tokens

    def swap_rows(self, rows):
        return rows

    def keys(self, kv):
        return [lax.all_gather(kv, "tensor", axis=0, tiled=True)]

    def keys_back(self, grads):
        return lax.psum_scatter(grads[0], "tensor", scatter_dimension=0, tiled=True), None


def block_step(
    move,
    block_in,
    ln1_scale,
    ln1_shift,
    qkv_ws,
    qkv_bs,
    out_ws,
    out_bias,
    ln2_scale,
    ln2_shift,
    up_ws,
    up_bs,
    down_ws,
    down_bias,
    out_grad,
):
    f32 = lambda v: v.astype(F32)
    tokens = block_in.shape[0]
    tables = rotary_tables(move.first, tokens)
    ln1_gain, ln2_gain = f32(ln1_scale), f32(ln2_scale)
    block_in = move.swap_rows(block_in)
    x_rows = f32(block_in)
    normed1, normal1, inv_one = norm_parts(x_rows, ln1_gain, f32(ln1_shift))
    normed1 = normed1.astype(BF)
    queries, keys, outs, logs = [], [], [], []
    for weight, bias in zip(qkv_ws, qkv_bs):
        split = weight.reshape(1, weight.shape[0], 3, -1).transpose(0, 2, 1, 3)
        q, kv = qkv_rows(normed1, split, f32(bias)[None, :], tables)
        queries.append(q)
        keys.append(move.keys(kv))
    for q, kvs in zip(queries, keys):
        out, log = attend(q, kvs)
        outs.append(out)
        logs.append(log)
    grad_low = move.swap_rows(out_grad)
    grad_rows = f32(grad_low)
    branch_one = sum(dot_nn(o, w) for o, w in zip(outs, out_ws)) + f32(out_bias)
    resid = x_rows + branch_one
    normed2, normal2, inv_two = norm_parts(resid, ln2_gain, f32(ln2_shift))
    normed2 = normed2.astype(BF)
    acts, slopes = [], []
    for weight, bias in zip(up_ws, up_bs):
        acted, slope = up_rows(normed2, weight, f32(bias)[None, :])
        acts.append(acted)
        slopes.append(slope)
    branch_two = sum(dot_nn(a, w) for a, w in zip(acts, down_ws)) + f32(down_bias)
    block_out = move.swap_rows((resid + branch_two).astype(BF))
    down_bias_grad = jnp.sum(grad_rows, 0)
    down_grads = [dot_tn(a, grad_low).astype(BF) for a in acts]
    hidden_gs, up_b_grads = [], []
    for down, slope in zip(down_ws, slopes):
        hg, total = hidden_grads(grad_low, (down[None], 0), slope)
        hidden_gs.append(hg)
        up_b_grads.append(total[0])
    up_grads = [dot_tn(normed2, hg).astype(BF) for hg in hidden_gs]
    normed2_grad = sum(dot_nt(hg, w) for hg, w in zip(hidden_gs, up_ws))
    resid_part, ln2_scale_grad, ln2_shift_grad = norm_back(normed2_grad, normal2, inv_two, ln2_gain)
    resid_grad = grad_rows + resid_part
    branch_grad = resid_grad.astype(BF)
    out_bias_grad = jnp.sum(branch_grad, 0, dtype=F32)
    out_w_grads = [dot_tn(o, branch_grad).astype(BF) for o in outs]
    qkv_w_grads, qkv_b_grads = [], []
    normed1_grad = 0.0
    for q, kvs, out, log, out_w, qkv_w in zip(queries, keys, outs, logs, out_ws, qkv_ws):
        out_g = dot_nt(branch_grad, out_w).astype(BF)
        dq, dks, dvs = attend_back(q, out_g, out, log, kvs, tables)
        dk_own, dk_got = move.keys_back(dks)
        dv_own, dv_got = move.keys_back(dvs)
        if dk_got is None:
            dk_got, dv_got = jnp.zeros_like(dk_own), jnp.zeros_like(dv_own)
        dk = key_sum(dk_own, dk_got, tables)
        dv = dv_own + dv_got
        qkv_g = jnp.concatenate([dq, dk, dv], axis=1)
        qkv_w_grads.append(dot_tn(normed1, qkv_g).astype(BF))
        qkv_b_grads.append(jnp.sum(qkv_g, 0, dtype=F32))
        normed1_grad = normed1_grad + dot_nt(qkv_g, qkv_w)
    input_part, ln1_scale_grad, ln1_shift_grad = norm_back(normed1_grad, normal1, inv_one, ln1_gain)
    in_grad = move.swap_rows((resid_grad + input_part).astype(BF))
    vectors = [
        ln1_scale_grad,
        ln1_shift_grad,
        out_bias_grad,
        ln2_scale_grad,
        ln2_shift_grad,
        down_bias_grad,
    ]
    return (
        block_out,
        in_grad,
        vectors,
        (qkv_w_grads, out_w_grads, up_grads, down_grads),
        (qkv_b_grads, up_b_grads),
    )


class Reduction:
    def __init__(self, move, table, own, oth):
        self.move, self.table = move, table
        self.grads = own, oth
        self.sends = [move.core_send(g) for g in (own, oth)]
        self.at = 0

    def start(self):
        at = self.at
        if at == 0:
            go = self.move.over_core
        elif at == 1:
            go = self.move.over_first
        elif at == 2:
            go = self.move.over_second
        else:
            go = functools.partial(self.move.over_z, level=at - 3)
        return [go(x) for x in self.sends]

    def take(self, got):
        at, self.at = self.at, self.at + 1
        if at == 0:
            ka, kb, sa, sb = first_split(self.table, *self.grads, *got)
            self.keep, self.sends = (ka, kb), [sa, sb]
        elif at == 1:
            self.sends = [self.keep[1] + got[1]]
            self.keep = self.keep[0] + got[0]
        else:
            total = self.keep + got[0]
            half = total.shape[0] // 2
            if half:
                self.keep, self.sends = total[:half], [total[half:]]
            else:
                self.done = total

    @property
    def last(self):
        return 2 + (self.move.n_dp // 4).bit_length() - 1


def beside(compute, inputs, *steps, late=()):
    sends = [s.sends if isinstance(s, Reduction) else s[1] for s in steps]
    inputs, sends, late_sends = tie(inputs, sends, [s[1] for s in late])
    got = []
    for s, x in zip(steps, sends):
        if isinstance(s, Reduction):
            s.sends = x
            got.append(s.start())
        else:
            got.append(s[0](x))
    later = [s[0](x) for s, x in zip(late, late_sends)]
    out = compute(*inputs)
    out, got = tie(out, got)
    moved = []
    for s, x in zip(steps, got):
        if isinstance(s, Reduction):
            s.take(x)
        else:
            moved.append(x)
    return out, moved + later


def paired_device(n_dp, *args):
    (block_in, ln1_scale, ln1_shift, qkv_weight, qkv_bias, out_weight, out_bias) = args[:7]
    (ln2_scale, ln2_shift, up_weight, up_bias, down_weight, down_bias, out_grad) = args[7:]
    move = Paired(n_dp)
    row = lambda v: v.astype(F32)[None, :]
    width, _, part = qkv_weight.shape
    tokens = block_in.shape[0]
    pairs = part // LANES
    half = pairs // 2
    cols = half * LANES
    table = move.table()
    low_product = lambda a, b: dot_tn(a, b).astype(BF)

    qkv_own = jnp.transpose(qkv_weight, (1, 0, 2))
    small = jnp.concatenate([qkv_bias.reshape(3 * part), up_bias])
    qkv_piece = move.piece(qkv_own, 1)
    block_in = move.swap_rows(block_in)
    tables = rotary_tables(move.first, tokens)
    qkv_piece, tables = tie(qkv_piece, tables)
    qkv_got = move.over_y(qkv_piece)
    small_got = move.over_y(small)
    qkv_bs = [row(v[: 3 * part]) for v in (small, small_got)]
    up_bs = [row(v[3 * part :]) for v in (small, small_got)]
    qkv_own = qkv_own[None]
    qkv_oth = lax.all_gather(qkv_got, "dp")
    rest = [move.piece(up_weight), jnp.concatenate([move.piece(w) for w in (out_weight, down_weight)])]
    normed1, normed1_t = norm_rows(block_in, row(ln1_scale), row(ln1_shift))
    (q_own, kv_own), (rest,) = beside(
        lambda n: qkv_rows(n, qkv_own, qkv_bs[0], tables),
        (normed1,),
        (lambda ws: [move.over_y(w) for w in ws], rest),
    )
    kvs_own = [kv_own, move.over_core(kv_own)]
    up_got, mixed_got = (lax.all_gather(got, "dp") for got in rest)
    (out_a, log_a), _ = beside(lambda q, kvs: attend(q, kvs, 0, half), (q_own, kvs_own))
    qkv_oth, out_a, out_grad = tie(qkv_oth, out_a, out_grad)
    q_oth, kv_oth = qkv_rows(normed1, qkv_oth, qkv_bs[1], tables)
    (out_b, log_b), (kv_got, grad_low) = beside(
        lambda q, kvs: attend(q, kvs, half, half),
        (q_own, kvs_own),
        (move.over_core, kv_oth),
        late=[(move.swap_rows, out_grad)],
    )
    kvs_oth = [kv_oth, kv_got]
    (out_oth, log_oth), _ = beside(attend, (q_oth, kvs_oth))
    out_rows = part // n_dp
    out_got = mixed_got[:, :out_rows].reshape(part, width)
    up_ws = [up_weight, up_got.reshape(up_weight.shape)]
    down_ws = [(down_weight[None], 0), (mixed_got, out_rows)]
    outs = [out_a, out_b, out_oth]
    out_ws = [out_weight[:cols], out_weight[cols:], out_got]

    resid, normed2, normed2_t = project_rows(
        block_in, row(out_bias), row(ln2_scale), row(ln2_shift), outs, out_ws
    )
    acts, slopes = zip(*[up_rows(normed2, w, b) for w, b in zip(up_ws, up_bs)])
    block_out = down_rows(resid, row(down_bias), acts, down_ws)
    down_grads, (block_out,) = beside(
        lambda xs, g: [low_product(a, g) for a in xs],
        (acts, grad_low),
        late=[(move.swap_rows, block_out)],
    )
    down = Reduction(move, table, *down_grads)
    (hg_own, up_b_own), _ = beside(
        lambda g, slope: hidden_grads(g, down_ws[0], slope), (grad_low, slopes[0]), down
    )

    def others(g, hg_own):
        hg_oth, up_b_oth = hidden_grads(g, down_ws[1], slopes[1])
        return hg_oth, up_b_oth, [dot_nn(normed2_t, h).astype(BF) for h in (hg_own, hg_oth)]

    (hg_oth, up_b_oth, up_grads), _ = beside(others, (grad_low, hg_own), down)
    up = Reduction(move, table, *up_grads)
    (branch_grad, sums_two), _ = beside(
        lambda *hs: middle_rows(resid, grad_low, row(ln2_scale), hs, up_ws), (hg_own, hg_oth), up, down
    )

    def projected(outs, g):
        own = jnp.concatenate([low_product(o, g) for o in outs[:2]])
        out_w_grads = own, low_product(outs[2], g)
        return out_w_grads, [dot_nt(g, w).astype(BF) for w in out_ws]

    (out_w_grads, out_gs), _ = beside(projected, (outs, branch_grad), down)
    proj = Reduction(move, table, *out_w_grads)

    def back(which):
        own = which >= 2
        lo = (which % 2) * half
        q, kvs = (q_own, kvs_own) if own else (q_oth, kvs_oth)
        out, log, grad = (
            (outs[which - 2], (log_a, log_b)[which - 2], out_gs[which - 2])
            if own
            else (out_oth, log_oth, out_gs[2])
        )
        inputs = q, grad, out, log, kvs
        at = 0 if own else lo
        return lambda *xs: attend_back(*xs, tables, lo, half, at), inputs

    def keys_of(x):
        return lambda xs: [move.over_core(g) for g in xs], [x[1][1], x[2][1]]

    def unit(x, got):
        keep, send, dk, dv, sums = unit_grads(
            move.blocks, normed1_t, x[0], x[1][0], got[0], x[2][0], got[1], tables
        )
        return keep, send, (x[0], dk, dv), sums[0]

    level = lambda n: functools.partial(move.over_chip, level=n)

    def halves(total):
        return total[: total.shape[0] // 2], total[total.shape[0] // 2 :]

    oth_a, _ = beside(*back(0), up, down, proj)
    down_block, oth_a, block_out = tie(down.done, oth_a, block_out)
    down_all = move.gather(down_block)
    oth_b, (got,) = beside(*back(1), keys_of(oth_a), up, proj)
    keep_oth_a, send, parts_oth_a, bias_oth_a = unit(oth_a, got)
    own_a, (got, core_got) = beside(*back(2), keys_of(oth_b), (move.over_core, send), up, proj)
    y_send = keep_oth_a + core_got
    (keep_oth_b, send, parts_oth_b, bias_oth_b), (key_got, y_got_a) = beside(
        unit, (oth_b, got), keys_of(own_a), proj, late=[(move.over_y, y_send)]
    )
    (keep_a, send_a, parts_a, bias_a), (core_got,) = beside(
        unit, (own_a, key_got), (move.over_core, send), up, proj
    )
    mixed = jnp.concatenate([up.done[0], proj.done[0].reshape(-1, up.done.shape[2])])
    mixed, keep_a, down_all = tie(mixed, keep_a, down_all)
    mixed_all = lax.all_gather(mixed, "dp")
    own_b, (core_got_a, y_got_a, y_got_b) = beside(
        *back(3),
        (move.over_core, send_a),
        (lambda x: x, y_got_a),
        late=[(move.over_y, keep_oth_b + core_got)],
    )
    keep_a, send_a = halves(keep_a + core_got_a + y_got_a)
    partial, (key_got, a_got) = beside(
        lambda *ps: early_rows(qkv_own, qkv_oth, *ps),
        (parts_a, (parts_oth_a, parts_oth_b)),
        keys_of(own_b),
        late=[(level(0), send_a)],
    )
    (keep_b, send_b, parts_b, bias_b), (a_got, y_got_b) = beside(
        unit, (own_b, key_got), (lambda x: x, a_got), (lambda x: x, y_got_b)
    )
    keep_a, send_a = halves(keep_a + a_got)
    (in_grad, sums_one), (core_got, a_got) = beside(
        lambda *xs: last_rows(block_in, branch_grad, row(ln1_scale), *xs),
        (partial, qkv_own, parts_b),
        (move.over_core, send_b),
        (level(1), send_a),
    )
    keep_a, send_a = halves(keep_a + a_got)
    keep_b, send_b = halves(keep_b + core_got + y_got_b)
    in_grad, send_a, send_b, mixed_all = tie(in_grad, send_a, send_b, mixed_all)
    in_grad = move.swap_rows(in_grad)
    total_a = keep_a + move.over_chip(send_a, 2)
    unit_a = lax.all_gather(total_a[0], "dp")
    total_b = keep_b + move.over_chip(send_b, 0)
    levels = (n_dp // 2).bit_length() - 1
    for n in range(1, levels):
        keep_b, send_b = halves(total_b)
        total_b = keep_b + move.over_chip(send_b, n)
    for n in reversed(range(levels)):
        total_b = jnp.concatenate([total_b, move.over_chip(total_b, n)])
    total_b = jnp.concatenate([total_b, move.over_core(total_b)])
    qkv_g = jnp.transpose(widen(move.blocks, unit_a, total_b), (1, 0, 2))
    up_rows_each = width // n_dp
    up_all = mixed_all[:, :up_rows_each].reshape(width, -1)
    out_all = mixed_all[:, up_rows_each:].reshape(part, width)
    side = lambda a, b: jnp.concatenate([a.reshape(3, cols), b.reshape(3, cols)], axis=1).reshape(-1)
    vec, flat = move.reduce_vectors(
        jnp.concatenate([sums_one[:2], sums_two[:4]]),
        jnp.concatenate([side(bias_a, bias_b), up_b_own[0]]),
        jnp.concatenate([side(bias_oth_a, bias_oth_b), up_b_oth[0]]),
    )
    f32 = lambda v: v.astype(F32)
    return (
        block_out,
        in_grad,
        vec[0],
        vec[1],
        qkv_g,
        flat[: 3 * part].reshape(3, part),
        f32(out_all),
        vec[4],
        vec[2],
        vec[3],
        f32(up_all),
        flat[3 * part :],
        f32(down_all),
        vec[5],
    )


def spread_device(*args):
    (block_in, ln1_scale, ln1_shift, qkv_weight, qkv_bias, out_weight, out_bias) = args[:7]
    (ln2_scale, ln2_shift, up_weight, up_bias, down_weight, down_bias, out_grad) = args[7:]
    gather = lambda w, axis: lax.all_gather(w, "tensor", axis=axis, tiled=True)
    scatter = lambda g, axis: lax.psum(
        lax.psum_scatter(g, "tensor", scatter_dimension=axis, tiled=True), "dp"
    ).astype(F32)
    width = qkv_weight.shape[0]
    qkv_all = gather(qkv_weight, 2)
    full = qkv_all.shape[2]
    out = block_step(
        Spread(block_in.shape[0]),
        block_in,
        ln1_scale,
        ln1_shift,
        [qkv_all.reshape(width, 3 * full)],
        [gather(qkv_bias, 1).reshape(3 * full)],
        [gather(out_weight, 0)],
        out_bias,
        ln2_scale,
        ln2_shift,
        [gather(up_weight, 1)],
        [gather(up_bias, 0)],
        [gather(down_weight, 0)],
        down_bias,
        out_grad,
    )
    block_out, in_grad, vectors, weight_grads, (qkv_b, up_b) = out
    ((qkv_g,), (out_g,), (up_g,), (down_g,)) = weight_grads
    vec = scatter(jnp.stack(vectors), 1)
    return (
        block_out,
        in_grad,
        vec[0],
        vec[1],
        scatter(qkv_g.reshape(width, 3, full), 2),
        scatter(qkv_b[0].reshape(3, full), 1),
        scatter(out_g, 0),
        vec[2],
        vec[3],
        vec[4],
        scatter(up_g, 1),
        scatter(up_b[0], 0),
        scatter(down_g, 0),
        vec[5],
    )


def solution(mesh):
    n_dp, n_tensor = mesh.shape["dp"], mesh.shape["tensor"]
    rows = P(("dp", "tensor"), None)
    vector = P("tensor")
    placed = (
        rows,
        P(),
        P(),
        P(None, None, "tensor"),
        P(None, "tensor"),
        P("tensor", None),
        P(),
        P(),
        P(),
        P(None, "tensor"),
        vector,
        P("tensor", None),
        P(),
        rows,
    )
    paired = n_tensor == 2 and n_dp >= 8 and n_dp & (n_dp - 1) == 0
    return jax.shard_map(
        functools.partial(paired_device, n_dp) if paired else spread_device,
        mesh=mesh,
        in_specs=placed,
        out_specs=(
            rows,
            rows,
            vector,
            vector,
            P(None, None, "tensor"),
            P(None, "tensor"),
            P("tensor", None),
            vector,
            vector,
            vector,
            P(None, "tensor"),
            vector,
            P("tensor", None),
            vector,
        ),
        check_vma=False,
    )
```

```python
import functools
import math

import jax
import jax.numpy as jnp
import numpy as np
from jax import lax
from jax.experimental import pallas as pl
from jax.experimental.pallas import tpu as pltpu
from jax.sharding import PartitionSpec as P

HD = 64
GH = 16
GW = 16
SEQ = 2048
EPS = 1e-06
LANES = 128
ROT = 2 * (HD // 3 // 2)
HALF_ROT = ROT // 2
LOG2E = math.log2(math.e)
SCALE = 1.0 / math.sqrt(HD)
BF = jnp.bfloat16
F32 = jnp.float32
VMEM_BYTES = 56 << 20


def dot_nt(left, right):
    return lax.dot_general(left, right, (((1,), (1,)), ((), ())), preferred_element_type=F32)


def dot_nn(left, right):
    return lax.dot_general(left, right, (((1,), (0,)), ((), ())), preferred_element_type=F32)


def dot_tn(left, right):
    return lax.dot_general(left, right, (((0,), (0,)), ((), ())), preferred_element_type=F32)


def call(kernel, flops, moved, exps=0, **kw):
    return pl.pallas_call(
        kernel,
        compiler_params=pltpu.CompilerParams(vmem_limit_bytes=VMEM_BYTES),
        cost_estimate=pl.CostEstimate(flops=flops, bytes_accessed=moved, transcendentals=exps),
        **kw,
    )


def rotary_tables(first, count):
    lane = np.arange(LANES) % HD
    axis = lane // ROT
    inside = lane % ROT
    freq = np.float32(10000.0) ** (
        -(inside % HALF_ROT).astype(np.float32) / np.float32(HALF_ROT)
    )
    turned = axis < 3
    early = turned & (inside < HALF_ROT)
    late = turned & (inside >= HALF_ROT)
    index = first + jnp.arange(count, dtype=jnp.int32)[:, None]
    places = (index // (GH * GW), index // GW % GH, index % GW)
    place = jnp.where(axis == 0, places[0], jnp.where(axis == 1, places[1], places[2]))
    angle = place.astype(F32) * freq.astype(np.float32)[None, :]
    cos = jnp.where(turned, jnp.cos(angle), 1.0)
    sin = jnp.sin(angle)
    return cos, jnp.where(early, -sin, 0.0), jnp.where(late, sin, 0.0)


def turn(x, cos, sin_a, sin_b):
    return (
        x * cos
        + pltpu.roll(x, LANES - HALF_ROT, 1) * sin_a
        + pltpu.roll(x, HALF_ROT, 1) * sin_b
    )


def turn_back(g, cos, sin_a, sin_b):
    return (
        g * cos
        + pltpu.roll(g * sin_b, LANES - HALF_ROT, 1)
        + pltpu.roll(g * sin_a, HALF_ROT, 1)
    )


def norm_kernel(x_ref, scale_ref, shift_ref, n_ref, nt_ref):
    normed, _, _ = norm_parts(x_ref[...].astype(F32), scale_ref[...], shift_ref[...])
    n_ref[...] = normed.astype(BF)
    nt_ref[...] = normed.T.astype(BF)


def norm_rows(x, scale, shift):
    tokens, width = x.shape
    rows = min(256, tokens)
    vector = pl.BlockSpec((1, width), lambda i: (0, 0))
    tile = pl.BlockSpec((rows, width), lambda i: (i, 0))
    return call(
        norm_kernel,
        10 * tokens * width,
        6 * tokens * width,
        grid=(tokens // rows,),
        in_specs=[tile, vector, vector],
        out_specs=[tile, pl.BlockSpec((width, rows), lambda i: (0, i))],
        out_shape=[
            jax.ShapeDtypeStruct((tokens, width), BF),
            jax.ShapeDtypeStruct((width, tokens), BF),
        ],
    )(x, scale, shift)


def qkv_kernel(n_ref, w_ref, b_ref, c_ref, sa_ref, sb_ref, q_ref, kv_ref, *, q_steps):
    step = pl.program_id(0)
    weight = w_ref[...].reshape(n_ref.shape[1], w_ref.shape[-1])
    rows = dot_nn(n_ref[...], weight) + b_ref[...]
    wide = rows.shape[1]

    def turned():
        tables = (c_ref[...], sa_ref[...], sb_ref[...])
        parts = [
            turn(rows[:, at : at + LANES], *tables).astype(BF) for at in range(0, wide, LANES)
        ]
        return jnp.concatenate(parts, axis=1)

    @pl.when(step < q_steps)
    def _():
        q_ref[...] = turned()

    @pl.when((step >= q_steps) & (step < 2 * q_steps))
    def _():
        kv_ref[...] = turned()

    @pl.when(step >= 2 * q_steps)
    def _():
        kv_ref[...] = rows.astype(BF)


def qkv_rows(normed, weight, bias, tables):
    tokens, width = normed.shape
    groups, _, deep, cols = weight.shape
    tile = next(t for t in (512, 256, LANES) if cols % t == 0)
    q_steps = cols // tile
    whole = lambda n: (0, 0)
    return call(
        functools.partial(qkv_kernel, q_steps=q_steps),
        2 * tokens * width * 3 * cols,
        2 * (tokens * width + width * 3 * cols + tokens * 3 * cols),
        grid=(3 * q_steps,),
        in_specs=[
            pl.BlockSpec((tokens, width), whole),
            pl.BlockSpec((groups, None, deep, tile), lambda n: (0, n // q_steps, 0, n % q_steps)),
            pl.BlockSpec((1, tile), lambda n: (0, n)),
        ]
        + [pl.BlockSpec((tokens, LANES), whole)] * 3,
        out_specs=[
            pl.BlockSpec((tokens, tile), lambda n: (0, jnp.minimum(n, q_steps - 1))),
            pl.BlockSpec((tokens, tile), lambda n: (0, jnp.maximum(n - q_steps, 0))),
        ],
        out_shape=[
            jax.ShapeDtypeStruct((tokens, cols), BF),
            jax.ShapeDtypeStruct((tokens, 2 * cols), BF),
        ],
    )(normed, weight, bias, *tables)


def attend_kernel(*refs, sources, rows_at):
    q_ref = refs[0]
    k_refs = refs[1 : 1 + sources]
    v_refs = refs[1 + sources : 1 + 2 * sources]
    o_ref, lse_ref = refs[1 + 2 * sources : 3 + 2 * sources]
    wide_refs = refs[3 + 2 * sources :]
    lane = lax.broadcasted_iota(jnp.int32, (1, LANES), 1)
    for v, wide in zip(v_refs, wide_refs):
        wide[:, :LANES] = v[...]
        wide[:, LANES:] = jnp.ones_like(v)

    def scores_of(q, head):
        q_head = jnp.where((lane // HD) == head, q, jnp.zeros_like(q))
        return [dot_nt(q_head, k[...]) for k in k_refs]

    def result(scores):
        peak = functools.reduce(
            jnp.maximum, [jnp.max(s, axis=1, keepdims=True) for s in scores]
        )
        weights = [jnp.exp2((s - peak) * (SCALE * LOG2E)).astype(BF) for s in scores]
        both = sum(dot_nn(w, v[...]) for w, v in zip(weights, wide_refs))
        total = both[:, LANES : LANES + 1]
        return both[:, :LANES] / both[:, LANES:], peak * (SCALE * LOG2E) + jnp.log2(total)

    for first in range(0, q_ref.shape[0], rows_at):
        rows = slice(first, first + rows_at)
        q = q_ref[rows, :]
        (out_0, log_0), (out_1, log_1) = [result(s) for s in [scores_of(q, h) for h in range(2)]]
        early = lane < HD
        o_ref[rows, :] = jnp.where(early, out_0, out_1).astype(BF)
        logs = jnp.where(early, log_0, log_1).T
        lse_ref[0, 0:1, rows] = logs[0:1]
        lse_ref[0, 1:2, rows] = logs[HD : HD + 1]


def attend(q, kvs, skip=0, pairs=None):
    tokens, cols = q.shape
    all_pairs = cols // LANES
    pairs = pairs or all_pairs
    cols = pairs * LANES
    keys = sum(kv.shape[0] for kv in kvs)
    q_spec = pl.BlockSpec((tokens, LANES), lambda i: (0, skip + i))
    k_specs = [pl.BlockSpec((kv.shape[0], LANES), lambda i: (0, skip + i)) for kv in kvs]
    v_specs = [
        pl.BlockSpec((kv.shape[0], LANES), lambda i: (0, all_pairs + skip + i)) for kv in kvs
    ]
    return call(
        functools.partial(attend_kernel, sources=len(kvs), rows_at=min(512, tokens)),
        4 * 4 * tokens * keys * cols,
        2 * (2 * tokens * cols + 2 * keys * cols),
        tokens * keys * 2 * pairs,
        grid=(pairs,),
        in_specs=[q_spec] + k_specs + v_specs,
        out_specs=[
            pl.BlockSpec((tokens, LANES), lambda i: (0, i)),
            pl.BlockSpec((1, 2, tokens), lambda i: (i, 0, 0)),
        ],
        out_shape=[
            jax.ShapeDtypeStruct((tokens, cols), BF),
            jax.ShapeDtypeStruct((pairs, 2, tokens), F32),
        ],
        scratch_shapes=[pltpu.VMEM((kv.shape[0], 2 * LANES), BF) for kv in kvs],
    )(q, *kvs, *kvs)


def attend_back_kernel(*refs, sources, keys_at, queries_at):
    q_ref, do_ref, o_ref, lse_ref, c_ref, sa_ref, sb_ref = refs[:7]
    at = 7
    k_refs = refs[at : at + sources]
    v_refs = refs[at + sources : at + 2 * sources]
    at += 2 * sources
    dq_ref = refs[at]
    dkv_refs = refs[at + 1 : at + 1 + sources]
    dq_acc, centre = refs[at + 1 + sources :]
    lane = lax.broadcasted_iota(jnp.int32, (1, LANES), 1)
    tokens = q_ref.shape[0]
    product = (do_ref[...].astype(F32) * o_ref[...].astype(F32)).T
    for head in range(2):
        centre[head : head + 1, :] = jnp.sum(
            product[head * HD : head * HD + HD], axis=0, keepdims=True
        )
    dq_acc[...] = jnp.zeros_like(dq_acc)
    for k_ref, v_ref, dkv_ref in zip(k_refs, v_refs, dkv_refs):

        def body(j, carry):
            rows = pl.ds(pl.multiple_of(j * keys_at, keys_at), keys_at)
            k, v = k_ref[rows, :], v_ref[rows, :]
            k_t = k.astype(F32).T.astype(BF)
            dv = jnp.zeros((keys_at, LANES), F32)
            dk = jnp.zeros((keys_at, LANES), F32)

            def products(cut, head):
                mine = (lane // HD) == head
                q, do = q_ref[cut, :], do_ref[cut, :]
                q_head = jnp.where(mine, q, jnp.zeros_like(q))
                do_head = jnp.where(mine, do, jnp.zeros_like(do))
                return q_head, do_head, dot_nt(k, q_head), dot_nt(v, do_head)

            steps = [
                (slice(first, first + queries_at), head)
                for first in range(0, tokens, queries_at)
                for head in range(2)
            ]
            later = products(*steps[0])
            for at, (cut, head) in enumerate(steps):
                q_head, do_head, scores, share_grad = later
                if at + 1 < len(steps):
                    later = products(*steps[at + 1])
                shares = jnp.exp2(scores * (SCALE * LOG2E) - lse_ref[0, head : head + 1, cut])
                score_grad = (shares * (share_grad - centre[head : head + 1, cut])).astype(BF)
                dv += dot_nn(shares.astype(BF), do_head)
                dk += dot_nn(score_grad, q_head)
                part = slice(head * HD, head * HD + HD)
                dq_acc[part, cut] += dot_nn(k_t[part], score_grad)
            dkv_ref[0, rows, :] = (dk * SCALE).astype(BF)
            dkv_ref[1, rows, :] = dv.astype(BF)
            return carry

        lax.fori_loop(0, k_ref.shape[0] // keys_at, body, 0)
    dq = (dq_acc[...] * SCALE).T
    dq_ref[...] = turn_back(dq, c_ref[...], sa_ref[...], sb_ref[...]).astype(BF)


def attend_back(q, out_grad, out, lse, kvs, tables, skip=0, pairs=None, at=0):
    tokens, cols = q.shape
    all_pairs = cols // LANES
    pairs = pairs or all_pairs
    cols = pairs * LANES
    keys = sum(kv.shape[0] for kv in kvs)
    q_spec = pl.BlockSpec((tokens, LANES), lambda i: (0, skip + i))
    o_spec = pl.BlockSpec((tokens, LANES), lambda i: (0, at + i))
    k_specs = [pl.BlockSpec((kv.shape[0], LANES), lambda i: (0, skip + i)) for kv in kvs]
    v_specs = [
        pl.BlockSpec((kv.shape[0], LANES), lambda i: (0, all_pairs + skip + i)) for kv in kvs
    ]
    dq_spec = pl.BlockSpec((tokens, LANES), lambda i: (0, i))
    dkv_specs = [pl.BlockSpec((2, kv.shape[0], LANES), lambda i: (0, 0, i)) for kv in kvs]
    table = pl.BlockSpec((tokens, LANES), lambda i: (0, 0))
    outs = call(
        functools.partial(
            attend_back_kernel, sources=len(kvs), keys_at=1024, queries_at=min(256, tokens)
        ),
        10 * 4 * tokens * keys * cols,
        2 * (4 * tokens * cols + 4 * keys * cols),
        tokens * keys * 2 * pairs,
        grid=(pairs,),
        in_specs=[q_spec, o_spec, o_spec]
        + [pl.BlockSpec((1, 2, tokens), lambda i: (at + i, 0, 0))]
        + [table] * 3
        + k_specs
        + v_specs,
        out_specs=[dq_spec] + dkv_specs,
        out_shape=[jax.ShapeDtypeStruct((tokens, cols), BF)]
        + [jax.ShapeDtypeStruct((2, kv.shape[0], cols), BF) for kv in kvs],
        scratch_shapes=[pltpu.VMEM((LANES, tokens), F32), pltpu.VMEM((2, tokens), F32)],
    )(q, out_grad, out, lse, *tables, *kvs, *kvs)
    return outs[0], outs[1:]


def key_sum_kernel(own_ref, got_ref, c_ref, sa_ref, sb_ref, dk_ref):
    total = own_ref[...].astype(F32) + got_ref[...].astype(F32)
    dk_ref[...] = turn_back(total, c_ref[...], sa_ref[...], sb_ref[...]).astype(BF)


def key_sum(own, got, tables):
    tokens, cols = own.shape
    spec = pl.BlockSpec((tokens, LANES), lambda i: (0, i))
    table = pl.BlockSpec((tokens, LANES), lambda i: (0, 0))
    return call(
        key_sum_kernel,
        12 * tokens * cols,
        6 * tokens * cols,
        grid=(cols // LANES,),
        in_specs=[spec, spec] + [table] * 3,
        out_specs=spec,
        out_shape=jax.ShapeDtypeStruct((tokens, cols), BF),
    )(own, got, *tables)


def gelu_parts(hidden):
    cdf = 0.5 + 0.5 * lax.erf(hidden * (1.0 / math.sqrt(2.0)))
    bell = jnp.exp2(hidden * hidden * (-0.5 * LOG2E))
    return hidden * cdf, cdf + hidden * (1.0 / math.sqrt(2.0 * math.pi)) * bell


def up_kernel(n_ref, w_ref, b_ref, acted_ref, slope_ref):
    hidden = dot_nn(n_ref[...], w_ref[...]) + b_ref[...]
    acted, slope = gelu_parts(hidden)
    acted_ref[...] = acted.astype(BF)
    slope_ref[...] = slope.astype(BF)


def up_rows(normed, weight, bias):
    tokens, width = normed.shape
    cols = weight.shape[1]
    tile = 512
    out = pl.BlockSpec((tokens, tile), lambda n: (0, n))
    return call(
        up_kernel,
        2 * tokens * width * cols,
        2 * (tokens * width + width * cols + 2 * tokens * cols),
        tokens * cols,
        grid=(cols // tile,),
        in_specs=[
            pl.BlockSpec((tokens, width), lambda n: (0, 0)),
            pl.BlockSpec((width, tile), lambda n: (0, n)),
            pl.BlockSpec((1, tile), lambda n: (0, n)),
        ],
        out_specs=[out, out],
        out_shape=[jax.ShapeDtypeStruct((tokens, cols), BF)] * 2,
    )(normed, weight, bias)


def hidden_grad_kernel(g_ref, w_ref, slope_ref, hg_ref, sum_ref, *, skip):
    weight = w_ref[:, skip:].reshape(hg_ref.shape[1], g_ref.shape[1])
    grad = dot_nt(g_ref[...], weight) * slope_ref[...].astype(F32)
    low = grad.astype(BF)
    hg_ref[...] = low
    sum_ref[...] = jnp.sum(low.astype(F32), axis=0, keepdims=True)


def hidden_grads(grad, down, slope):
    tokens, width = grad.shape
    down, skip = down
    groups, deep, _ = down.shape
    cols = slope.shape[1]
    tile = 512
    out = pl.BlockSpec((tokens, tile), lambda n: (0, n))
    if groups == 1:
        weight = pl.BlockSpec((1, tile, width), lambda n: (0, n, 0))
    else:
        weight = pl.BlockSpec((tile // (deep - skip), deep, width), lambda n: (n, 0, 0))
    return call(
        functools.partial(hidden_grad_kernel, skip=skip),
        2 * tokens * width * cols,
        2 * (tokens * width + width * cols + 2 * tokens * cols),
        grid=(cols // tile,),
        in_specs=[pl.BlockSpec((tokens, width), lambda n: (0, 0)), weight, out],
        out_specs=[out, pl.BlockSpec((1, tile), lambda n: (0, n))],
        out_shape=[
            jax.ShapeDtypeStruct((tokens, cols), BF),
            jax.ShapeDtypeStruct((1, cols), F32),
        ],
    )(grad, down, slope)


def norm_parts(values, gain, shift):
    centred = values - jnp.mean(values, axis=-1, keepdims=True)
    inv_dev = lax.rsqrt(jnp.mean(centred * centred, axis=-1, keepdims=True) + EPS)
    normal = centred * inv_dev
    return normal * gain + shift, normal, inv_dev


def norm_back(upstream, normal, inv_dev, gain):
    scaled = upstream * gain
    mean_first = jnp.mean(scaled, axis=-1, keepdims=True)
    mean_second = jnp.mean(scaled * normal, axis=-1, keepdims=True)
    back = inv_dev * (scaled - mean_first - normal * mean_second)
    return back, jnp.sum(upstream * normal, 0), jnp.sum(upstream, 0)


def tie(*trees):
    leaves, form = jax.tree.flatten(trees)
    return jax.tree.unflatten(form, lax.optimization_barrier(tuple(leaves)))


def project_kernel(*refs, parts):
    x_ref, b_ref, scale_ref, shift_ref = refs[:4]
    o_refs, w_refs = refs[4 : 4 + parts], refs[4 + parts : 4 + 2 * parts]
    resid_ref, n_ref, nt_ref = refs[4 + 2 * parts :]
    resid = x_ref[...].astype(F32) + b_ref[...]
    for o, w in zip(o_refs, w_refs):
        resid += dot_nn(o[...], w[...])
    normed, _, _ = norm_parts(resid, scale_ref[...], shift_ref[...])
    resid_ref[...] = resid
    n_ref[...] = normed.astype(BF)
    nt_ref[...] = normed.T.astype(BF)


def project_rows(x, bias, scale, shift, outs, weights):
    tokens, width = x.shape
    rows = min(256, tokens)
    vector = pl.BlockSpec((1, width), lambda i: (0, 0))
    tile = pl.BlockSpec((rows, width), lambda i: (i, 0))
    deep = sum(o.shape[1] for o in outs)
    return call(
        functools.partial(project_kernel, parts=len(outs)),
        2 * tokens * width * deep,
        2 * (tokens * deep + width * deep + 5 * tokens * width),
        grid=(tokens // rows,),
        in_specs=[tile, vector, vector, vector]
        + [pl.BlockSpec((rows, o.shape[1]), lambda i: (i, 0)) for o in outs]
        + [pl.BlockSpec(w.shape, lambda i: (0, 0)) for w in weights],
        out_specs=[tile, tile, pl.BlockSpec((width, rows), lambda i: (0, i))],
        out_shape=[
            jax.ShapeDtypeStruct((tokens, width), F32),
            jax.ShapeDtypeStruct((tokens, width), BF),
            jax.ShapeDtypeStruct((width, tokens), BF),
        ],
    )(x, bias, scale, shift, *outs, *weights)


def down_kernel(r_ref, b_ref, *refs, parts, skips):
    total = r_ref[...] + b_ref[...]
    for a, w, skip in zip(refs[:parts], refs[parts : 2 * parts], skips):
        total += dot_nn(a[...], w[:, skip:].reshape(a.shape[1], w.shape[2]))
    refs[-1][...] = total.astype(BF)


def down_rows(resid, bias, acts, weights):
    tokens, width = resid.shape
    weights, skips = zip(*weights)
    cols = min(512, width)
    tile = pl.BlockSpec((tokens, cols), lambda i: (0, i))
    deep = sum(a.shape[1] for a in acts)
    return call(
        functools.partial(down_kernel, parts=len(acts), skips=skips),
        2 * tokens * width * deep,
        2 * (tokens * deep + width * deep + 3 * tokens * width),
        grid=(width // cols,),
        in_specs=[tile, pl.BlockSpec((1, cols), lambda i: (0, i))]
        + [pl.BlockSpec(a.shape, lambda i: (0, 0)) for a in acts]
        + [pl.BlockSpec((*w.shape[:2], cols), lambda i: (0, 0, i)) for w in weights],
        out_specs=tile,
        out_shape=jax.ShapeDtypeStruct((tokens, width), BF),
    )(resid, bias, *acts, *weights)


def middle_kernel(r_ref, g_ref, scale_ref, *refs, parts):
    branch_ref, sums_ref = refs[-2:]
    upstream = sum(dot_nt(h[...], w[...]) for h, w in zip(refs[:parts], refs[parts : 2 * parts]))
    grad = g_ref[...].astype(F32)
    _, normal, inv_dev = norm_parts(r_ref[...], 1.0, 0.0)
    back, scale_sum, shift_sum = norm_back(upstream, normal, inv_dev, scale_ref[...])
    branch = (grad + back).astype(BF)
    branch_ref[...] = branch
    total = lambda v: jnp.sum(v, axis=0, keepdims=True)
    sums = [scale_sum[None, :], shift_sum[None, :], total(branch.astype(F32)), total(grad)]
    sums = jnp.concatenate(sums + [jnp.zeros((4, grad.shape[1]), F32)], axis=0)

    @pl.when(pl.program_id(0) == 0)
    def _():
        sums_ref[...] = sums

    @pl.when(pl.program_id(0) > 0)
    def _():
        sums_ref[...] += sums


def middle_rows(resid, grad, scale, hidden_gs, weights):
    tokens, width = resid.shape
    rows = min(256, tokens)
    tile = pl.BlockSpec((rows, width), lambda i: (i, 0))
    deep = sum(h.shape[1] for h in hidden_gs)
    return call(
        functools.partial(middle_kernel, parts=len(hidden_gs)),
        2 * tokens * width * deep,
        2 * (tokens * deep + width * deep + 4 * tokens * width),
        grid=(tokens // rows,),
        in_specs=[tile, tile, pl.BlockSpec((1, width), lambda i: (0, 0))]
        + [pl.BlockSpec((rows, h.shape[1]), lambda i: (i, 0)) for h in hidden_gs]
        + [pl.BlockSpec(w.shape, lambda i: (0, 0)) for w in weights],
        out_specs=[tile, pl.BlockSpec((8, width), lambda i: (0, 0))],
        out_shape=[
            jax.ShapeDtypeStruct((tokens, width), BF),
            jax.ShapeDtypeStruct((8, width), F32),
        ],
    )(resid, grad, scale, *hidden_gs, *weights)


def add_parts(total, w_ref, rows_ref, lo):
    cols = rows_ref.shape[1] // 3
    for kind in range(3):
        weight = w_ref[:, kind, :, lo : lo + cols].reshape(total.shape[1], cols)
        total += dot_nt(rows_ref[:, kind * cols : (kind + 1) * cols], weight)
    return total


def early_kernel(own_ref, oth_ref, own_rows, oth_rows, out_ref):
    total = add_parts(jnp.zeros(out_ref.shape, F32), oth_ref, oth_rows, 0)
    out_ref[...] = add_parts(total, own_ref, own_rows, 0)


def last_kernel(x_ref, g_ref, scale_ref, part_ref, own_ref, rows_ref, in_grad_ref, sums_ref):
    upstream = add_parts(part_ref[...], own_ref, rows_ref, rows_ref.shape[1] // 3)
    _, normal, inv_dev = norm_parts(x_ref[...].astype(F32), 1.0, 0.0)
    back, scale_sum, shift_sum = norm_back(upstream, normal, inv_dev, scale_ref[...])
    in_grad_ref[...] = (g_ref[...].astype(F32) + back).astype(BF)
    sums = [scale_sum[None, :], shift_sum[None, :], jnp.zeros((6, x_ref.shape[1]), F32)]
    sums = jnp.concatenate(sums, axis=0)

    @pl.when(pl.program_id(0) == 0)
    def _():
        sums_ref[...] = sums

    @pl.when(pl.program_id(0) > 0)
    def _():
        sums_ref[...] += sums


def early_rows(own, oth, own_rows, oth_rows):
    tokens, deep = own_rows.shape[0], own_rows.shape[1] + oth_rows.shape[1]
    width = own.shape[0] * own.shape[2]
    rows = min(512, tokens)
    return call(
        early_kernel,
        2 * tokens * width * deep,
        2 * (tokens * deep + width * deep + 2 * tokens * width),
        grid=(tokens // rows,),
        in_specs=[pl.BlockSpec(w.shape, lambda i: (0, 0, 0, 0)) for w in (own, oth)]
        + [pl.BlockSpec((rows, p.shape[1]), lambda i: (i, 0)) for p in (own_rows, oth_rows)],
        out_specs=pl.BlockSpec((rows, width), lambda i: (i, 0)),
        out_shape=jax.ShapeDtypeStruct((tokens, width), F32),
    )(own, oth, own_rows, oth_rows)


def last_rows(x, branch_grad, scale, partial, own, own_rows):
    tokens, width = x.shape
    deep = own_rows.shape[1]
    rows = min(256, tokens)
    tile = pl.BlockSpec((rows, width), lambda i: (i, 0))
    return call(
        last_kernel,
        2 * tokens * width * deep,
        2 * (tokens * deep + width * deep + 5 * tokens * width),
        grid=(tokens // rows,),
        in_specs=[tile, tile, pl.BlockSpec((1, width), lambda i: (0, 0)), tile]
        + [pl.BlockSpec(own.shape, lambda i: (0, 0, 0, 0)), pl.BlockSpec((rows, deep), lambda i: (i, 0))],
        out_specs=[tile, pl.BlockSpec((8, width), lambda i: (0, 0))],
        out_shape=[
            jax.ShapeDtypeStruct((tokens, width), BF),
            jax.ShapeDtypeStruct((8, width), F32),
        ],
    )(x, branch_grad, scale, partial, own, own_rows)


def unit_kernel(t_ref, nt_ref, c_ref, sa_ref, sb_ref, *refs, chips, parts):
    dq_refs, own_refs, got_refs = refs[:parts], refs[parts : 2 * parts], refs[2 * parts : 3 * parts]
    keep_ref, send_ref, rows_out, sum_ref, acc_ref = refs[3 * parts :]
    kind = pl.program_id(0)
    cols = dq_refs[0].shape[1]
    added = lambda a, b: a[...].astype(F32) + b[...].astype(F32)

    @pl.when(kind == 0)
    def _():
        for u, dq in enumerate(dq_refs):
            rows_out[:, u * cols : (u + 1) * cols] = dq[...]

    @pl.when(kind == 1)
    def _():
        tables = (c_ref[...], sa_ref[...], sb_ref[...])
        for u, (own, got) in enumerate(zip(own_refs, got_refs)):
            total = added(own, got)
            for at in range(0, cols, LANES):
                turned = turn_back(total[:, at : at + LANES], *tables).astype(BF)
                rows_out[:, u * cols + at : u * cols + at + LANES] = turned

    @pl.when(kind == 2)
    def _():
        for u, (own, got) in enumerate(zip(own_refs, got_refs)):
            rows_out[:, u * cols : (u + 1) * cols] = added(own, got).astype(BF)

    rows = rows_out[...]
    acc_ref[...] = dot_nn(nt_ref[...], rows)
    piece = keep_ref.shape[1]
    for place in range(chips):
        for ref, which in ((keep_ref, place), (send_ref, chips + place)):
            at = pl.multiple_of(t_ref[which] * piece, piece)
            ref[place] = acc_ref[pl.ds(at, piece), :].astype(BF)
    sums = jnp.sum(rows.astype(F32), axis=0, keepdims=True)
    sum_ref[...] = jnp.broadcast_to(sums, sum_ref.shape)


def unit_grads(table, normed_t, tables, dqs, owns, gots):
    width, tokens = normed_t.shape
    parts = len(dqs)
    cols = dqs[0].shape[1]
    wide = parts * cols
    chips = table.shape[0] // 2
    piece = width // (2 * chips)
    rotary = pl.BlockSpec((tokens, LANES), lambda i, t: (0, 0))
    part = pl.BlockSpec((tokens, cols), lambda i, t: (0, 0))
    pair = pl.BlockSpec((None, tokens, cols), lambda i, t: (jnp.maximum(i - 1, 0), 0, 0))
    blocks = pl.BlockSpec((chips, None, piece, wide), lambda i, t: (0, i, 0, 0))
    return pl.pallas_call(
        functools.partial(unit_kernel, chips=chips, parts=parts),
        grid_spec=pltpu.PrefetchScalarGridSpec(
            num_scalar_prefetch=1,
            grid=(3,),
            in_specs=[pl.BlockSpec((width, tokens), lambda i, t: (0, 0))]
            + [rotary] * 3
            + [part] * parts
            + [pair] * (2 * parts),
            out_specs=[
                blocks,
                blocks,
                pl.BlockSpec((tokens, wide), lambda i, t: (0, i)),
                pl.BlockSpec((8, wide), lambda i, t: (0, i)),
            ],
            scratch_shapes=[pltpu.VMEM((width, wide), F32)],
        ),
        out_shape=[jax.ShapeDtypeStruct((chips, 3, piece, wide), BF)] * 2
        + [jax.ShapeDtypeStruct((tokens, 3 * wide), BF), jax.ShapeDtypeStruct((8, 3 * wide), F32)],
        compiler_params=pltpu.CompilerParams(vmem_limit_bytes=VMEM_BYTES),
        cost_estimate=pl.CostEstimate(
            flops=6 * tokens * width * wide,
            bytes_accessed=2 * (tokens * width + 8 * tokens * wide + 3 * width * wide),
            transcendentals=0,
        ),
    )(table, normed_t, *tables, *dqs, *owns, *gots)


def widen_kernel(t_ref, a_ref, b_ref, out_ref):
    count, piece, cols = a_ref.shape
    out_ref[:, :cols] = a_ref[...].reshape(out_ref.shape[0], cols).astype(F32)
    for place in range(count):
        rows = pl.ds(pl.multiple_of(t_ref[place] * piece, piece), piece)
        out_ref[rows, cols:] = b_ref[place].astype(F32)


def widen(table, unit_a, unit_b):
    n, _, piece, cols = unit_a.shape
    spec = pl.BlockSpec((n, None, piece, cols), lambda i, t: (0, i, 0, 0))
    return pl.pallas_call(
        widen_kernel,
        grid_spec=pltpu.PrefetchScalarGridSpec(
            num_scalar_prefetch=1,
            grid=(3,),
            in_specs=[spec, spec],
            out_specs=pl.BlockSpec((None, n * piece, 2 * cols), lambda i, t: (i, 0, 0)),
        ),
        out_shape=jax.ShapeDtypeStruct((3, n * piece, 2 * cols), F32),
        compiler_params=pltpu.CompilerParams(vmem_limit_bytes=VMEM_BYTES),
        cost_estimate=pl.CostEstimate(
            flops=0, bytes_accessed=36 * n * piece * cols, transcendentals=0
        ),
    )(table, unit_a, unit_b)


def split_kernel(t_ref, own_m, own_f, oth_m, oth_f, got_om, got_of, got_tm, got_tf, ka, kb, send, *, last):
    total = lambda a, b: (a[...].astype(F32) + b[...].astype(F32)).astype(BF)
    by_y = t_ref[last] == 0
    own_far, oth_me = total(own_f, got_of), total(oth_m, got_tm)
    ka[...] = total(own_m, got_om)
    kb[...] = jnp.where(by_y, own_far, oth_me)
    send[0] = jnp.where(by_y, oth_me, own_far)
    send[1] = total(oth_f, got_tf)


def first_split(table, own, oth, got_own, got_oth):
    chips, piece, cols = got_own.shape
    count = chips // 2
    own, oth = (g.reshape(chips, 2, piece, cols) for g in (own, oth))
    whole = lambda far: pl.BlockSpec(
        (None, None, piece, cols), lambda i, t: (t[far * count + i], t[2 * count], 0, 0)
    )
    part = lambda far: pl.BlockSpec((None, piece, cols), lambda i, t: (t[far * count + i], 0, 0))
    out = pl.BlockSpec((None, piece, cols), lambda i, t: (i, 0, 0))
    return pl.pallas_call(
        functools.partial(split_kernel, last=2 * count),
        grid_spec=pltpu.PrefetchScalarGridSpec(
            num_scalar_prefetch=1,
            grid=(count,),
            in_specs=[whole(0), whole(1)] * 2 + [part(0), part(1)] * 2,
            out_specs=[out, out, pl.BlockSpec((2, None, piece, cols), lambda i, t: (0, i, 0, 0))],
        ),
        out_shape=[jax.ShapeDtypeStruct((count, piece, cols), BF)] * 2
        + [jax.ShapeDtypeStruct((2, count, piece, cols), BF)],
        compiler_params=pltpu.CompilerParams(vmem_limit_bytes=VMEM_BYTES),
        cost_estimate=pl.CostEstimate(
            flops=4 * count * piece * cols, bytes_accessed=24 * count * piece * cols, transcendentals=0
        ),
    )(table, own, own, oth, oth, got_own, got_own, got_oth, got_oth)


class Paired:
    def __init__(self, n_dp):
        self.n_dp = n_dp
        self.me_dp = lax.axis_index("dp")
        self.me_y = lax.axis_index("tensor")
        self.core = self.me_dp % 2
        self.first = self.core * (SEQ // 2)
        chips = n_dp // 2
        levels = chips.bit_length() - 1
        places = np.arange(chips)
        far = sum(((places >> (levels - 1 - k)) & 1) << k for k in range(levels))
        chip = jnp.asarray(far, jnp.int32) ^ (self.me_dp // 2)
        self.blocks = jnp.concatenate([chip * 2 + self.core, chip * 2 + 1 - self.core]).astype(
            jnp.int32
        )

    def move(self, x, to):
        pairs = []
        for dp in range(self.n_dp):
            for y in range(2):
                a, b = to(dp, y)
                if (a, b) != (dp, y):
                    pairs.append((dp * 2 + y, a * 2 + b))
        return lax.ppermute(x, ("dp", "tensor"), pairs)

    def swap_rows(self, rows):
        got = self.move(rows, lambda dp, y: (dp - dp % 2 + y, dp % 2))
        return jnp.where(self.core == self.me_y, rows, got)

    def over_y(self, x):
        return self.move(x, lambda dp, y: (dp, 1 - y))

    def over_core(self, x):
        return self.move(x, lambda dp, y: (dp ^ 1, y))

    def piece(self, own, axis=0):
        rows = own.shape[axis] // self.n_dp
        return lax.dynamic_slice_in_dim(own, self.me_dp * rows, rows, axis)

    def spread(self, got):
        return lax.all_gather(got, "dp", axis=0, tiled=True)

    def core_send(self, half):
        rows, cols = half.shape
        blocks = half.reshape(self.n_dp // 2, 2, rows // self.n_dp, cols)
        return lax.dynamic_index_in_dim(blocks, 1 - self.core, 1, keepdims=False)

    def over_chip(self, x, level):
        return self.move(x, lambda dp, y: (dp ^ (2 << level), y))

    def over_first(self, x):
        return self.move(x, lambda dp, y: (dp ^ 2, y) if dp % 2 else (dp, 1 - y))

    def over_second(self, x):
        return self.move(x, lambda dp, y: (dp, 1 - y) if dp % 2 else (dp ^ 2, y))

    def over_z(self, x, level):
        return self.move(x, lambda dp, y: (dp ^ (4 << level), y))

    def blocks_of(self, x_bit):
        count = self.n_dp // 4
        levels = count.bit_length() - 1
        z = self.me_dp // 4
        places = np.arange(count)
        far = sum(((places >> (levels - 1 - k)) & 1) << k for k in range(levels))
        return (jnp.asarray(far, jnp.int32) ^ z) * 2 + x_bit

    def table(self):
        x = (self.me_dp // 2) % 2
        me, far = self.blocks_of(x), self.blocks_of(1 - x)
        return jnp.concatenate([me, far, jnp.stack([self.core])]).astype(jnp.int32)

    def gather(self, block):
        return lax.all_gather(block[0], "dp", axis=0, tiled=True)

    def reduce_vectors(self, both, own, other):
        k, width = both.shape
        both = both.reshape(k, 2, width // 2)
        take = lambda b: lax.dynamic_index_in_dim(both, b, 1, keepdims=False).reshape(-1)
        mine = jnp.concatenate([take(self.me_y), own]).reshape(-1, LANES)
        theirs = jnp.concatenate([take(1 - self.me_y), other]).reshape(-1, LANES)
        total = jnp.stack([mine, theirs])
        total = total + self.over_core(total)
        for level in range((self.n_dp // 2).bit_length() - 1):
            total = total + self.over_chip(total, level)
        total = (total[0] + self.over_y(total[1])).reshape(-1)
        return total[: k * width // 2].reshape(k, width // 2), total[k * width // 2 :]


class Spread:
    def __init__(self, tokens):
        self.first = lax.axis_index("tensor") * tokens

    def swap_rows(self, rows):
        return rows

    def keys(self, kv):
        return [lax.all_gather(kv, "tensor", axis=0, tiled=True)]

    def keys_back(self, grads):
        return lax.psum_scatter(grads, "tensor", scatter_dimension=1, tiled=True)


def block_step(
    move,
    block_in,
    ln1_scale,
    ln1_shift,
    qkv_ws,
    qkv_bs,
    out_ws,
    out_bias,
    ln2_scale,
    ln2_shift,
    up_ws,
    up_bs,
    down_ws,
    down_bias,
    out_grad,
):
    f32 = lambda v: v.astype(F32)
    tokens = block_in.shape[0]
    tables = rotary_tables(move.first, tokens)
    ln1_gain, ln2_gain = f32(ln1_scale), f32(ln2_scale)
    block_in = move.swap_rows(block_in)
    x_rows = f32(block_in)
    normed1, normal1, inv_one = norm_parts(x_rows, ln1_gain, f32(ln1_shift))
    normed1 = normed1.astype(BF)
    queries, keys, outs, logs = [], [], [], []
    for weight, bias in zip(qkv_ws, qkv_bs):
        split = weight.reshape(1, weight.shape[0], 3, -1).transpose(0, 2, 1, 3)
        q, kv = qkv_rows(normed1, split, f32(bias)[None, :], tables)
        queries.append(q)
        keys.append(move.keys(kv))
    for q, kvs in zip(queries, keys):
        out, log = attend(q, kvs)
        outs.append(out)
        logs.append(log)
    grad_low = move.swap_rows(out_grad)
    grad_rows = f32(grad_low)
    branch_one = sum(dot_nn(o, w) for o, w in zip(outs, out_ws)) + f32(out_bias)
    resid = x_rows + branch_one
    normed2, normal2, inv_two = norm_parts(resid, ln2_gain, f32(ln2_shift))
    normed2 = normed2.astype(BF)
    acts, slopes = [], []
    for weight, bias in zip(up_ws, up_bs):
        acted, slope = up_rows(normed2, weight, f32(bias)[None, :])
        acts.append(acted)
        slopes.append(slope)
    branch_two = sum(dot_nn(a, w) for a, w in zip(acts, down_ws)) + f32(down_bias)
    block_out = move.swap_rows((resid + branch_two).astype(BF))
    down_bias_grad = jnp.sum(grad_rows, 0)
    down_grads = [dot_tn(a, grad_low).astype(BF) for a in acts]
    hidden_gs, up_b_grads = [], []
    for down, slope in zip(down_ws, slopes):
        hg, total = hidden_grads(grad_low, (down[None], 0), slope)
        hidden_gs.append(hg)
        up_b_grads.append(total[0])
    up_grads = [dot_tn(normed2, hg).astype(BF) for hg in hidden_gs]
    normed2_grad = sum(dot_nt(hg, w) for hg, w in zip(hidden_gs, up_ws))
    resid_part, ln2_scale_grad, ln2_shift_grad = norm_back(normed2_grad, normal2, inv_two, ln2_gain)
    resid_grad = grad_rows + resid_part
    branch_grad = resid_grad.astype(BF)
    out_bias_grad = jnp.sum(branch_grad, 0, dtype=F32)
    out_w_grads = [dot_tn(o, branch_grad).astype(BF) for o in outs]
    qkv_w_grads, qkv_b_grads = [], []
    normed1_grad = 0.0
    for q, kvs, out, log, out_w, qkv_w in zip(queries, keys, outs, logs, out_ws, qkv_ws):
        out_g = dot_nt(branch_grad, out_w).astype(BF)
        dq, (dkv,) = attend_back(q, out_g, out, log, kvs, tables)
        dk, dv = move.keys_back(dkv)
        dk = key_sum(dk, jnp.zeros_like(dk), tables)
        qkv_g = jnp.concatenate([dq, dk, dv], axis=1)
        qkv_w_grads.append(dot_tn(normed1, qkv_g).astype(BF))
        qkv_b_grads.append(jnp.sum(qkv_g, 0, dtype=F32))
        normed1_grad = normed1_grad + dot_nt(qkv_g, qkv_w)
    input_part, ln1_scale_grad, ln1_shift_grad = norm_back(normed1_grad, normal1, inv_one, ln1_gain)
    in_grad = move.swap_rows((resid_grad + input_part).astype(BF))
    vectors = [
        ln1_scale_grad,
        ln1_shift_grad,
        out_bias_grad,
        ln2_scale_grad,
        ln2_shift_grad,
        down_bias_grad,
    ]
    return (
        block_out,
        in_grad,
        vectors,
        (qkv_w_grads, out_w_grads, up_grads, down_grads),
        (qkv_b_grads, up_b_grads),
    )


class Reduction:
    def __init__(self, move, table, own, oth):
        self.move, self.table = move, table
        self.grads = own, oth
        self.sends = [move.core_send(g) for g in (own, oth)]
        self.at = 0

    def start(self):
        at = self.at
        if at == 0:
            go = self.move.over_core
        elif at == 1:
            go = self.move.over_first
        elif at == 2:
            go = self.move.over_second
        else:
            go = functools.partial(self.move.over_z, level=at - 3)
        return [go(x) for x in self.sends]

    def take(self, got):
        at, self.at = self.at, self.at + 1
        if at == 0:
            ka, kb, send = first_split(self.table, *self.grads, *got)
            self.keep, self.sends = (ka, kb), [send]
        elif at == 1:
            self.sends = [self.keep[1] + got[0][1]]
            self.keep = self.keep[0] + got[0][0]
        else:
            total = self.keep + got[0]
            half = total.shape[0] // 2
            if half:
                self.keep, self.sends = total[:half], [total[half:]]
            else:
                self.done = total

    @property
    def last(self):
        return 2 + (self.move.n_dp // 4).bit_length() - 1


def beside(compute, inputs, *steps, late=()):
    sends = [s.sends if isinstance(s, Reduction) else s[1] for s in steps]
    inputs, sends, late_sends = tie(inputs, sends, [s[1] for s in late])
    got = []
    for s, x in zip(steps, sends):
        if isinstance(s, Reduction):
            s.sends = x
            got.append(s.start())
        else:
            got.append(s[0](x))
    later = [s[0](x) for s, x in zip(late, late_sends)]
    out = compute(*inputs)
    out, got = tie(out, got)
    moved = []
    for s, x in zip(steps, got):
        if isinstance(s, Reduction):
            s.take(x)
        else:
            moved.append(x)
    return out, moved + later


def paired_device(n_dp, *args):
    (block_in, ln1_scale, ln1_shift, qkv_weight, qkv_bias, out_weight, out_bias) = args[:7]
    (ln2_scale, ln2_shift, up_weight, up_bias, down_weight, down_bias, out_grad) = args[7:]
    move = Paired(n_dp)
    row = lambda v: v.astype(F32)[None, :]
    width, _, part = qkv_weight.shape
    tokens = block_in.shape[0]
    pairs = part // LANES
    half = pairs // 2
    cols = half * LANES
    table = move.table()
    low_product = lambda a, b: dot_tn(a, b).astype(BF)

    qkv_own = jnp.transpose(qkv_weight, (1, 0, 2))
    small = jnp.concatenate([qkv_bias.reshape(3 * part), up_bias])
    qkv_piece = move.piece(qkv_own, 1)
    block_in = move.swap_rows(block_in)
    tables = rotary_tables(move.first, tokens)
    qkv_got = move.over_y(qkv_piece)
    small_got = move.over_y(small)
    qkv_bs = [row(v[: 3 * part]) for v in (small, small_got)]
    up_bs = [row(v[3 * part :]) for v in (small, small_got)]
    qkv_own = qkv_own[None]
    qkv_oth = lax.all_gather(qkv_got, "dp")
    rest = [move.piece(up_weight), jnp.concatenate([move.piece(w) for w in (out_weight, down_weight)])]
    normed1, normed1_t = norm_rows(block_in, row(ln1_scale), row(ln1_shift))
    (q_own, kv_own), (rest,) = beside(
        lambda n: qkv_rows(n, qkv_own, qkv_bs[0], tables),
        (normed1,),
        (lambda ws: [move.over_y(w) for w in ws], rest),
    )
    kvs_own = [kv_own, move.over_core(kv_own)]
    up_got, mixed_got = (lax.all_gather(got, "dp") for got in rest)
    (out_a, log_a), _ = beside(lambda q, kvs: attend(q, kvs, 0, half), (q_own, kvs_own))
    qkv_oth, out_a, out_grad = tie(qkv_oth, out_a, out_grad)
    q_oth, kv_oth = qkv_rows(normed1, qkv_oth, qkv_bs[1], tables)
    (out_b, log_b), (kv_got, grad_low) = beside(
        lambda q, kvs: attend(q, kvs, half, half),
        (q_own, kvs_own),
        (move.over_core, kv_oth),
        late=[(move.swap_rows, out_grad)],
    )
    kvs_oth = [kv_oth, kv_got]
    (out_oth, log_oth), _ = beside(attend, (q_oth, kvs_oth))
    out_rows = part // n_dp
    out_got = mixed_got[:, :out_rows].reshape(part, width)
    up_ws = [up_weight, up_got.reshape(up_weight.shape)]
    down_ws = [(down_weight[None], 0), (mixed_got, out_rows)]
    outs = [out_a, out_b, out_oth]
    out_ws = [out_weight[:cols], out_weight[cols:], out_got]

    resid, normed2, normed2_t = project_rows(
        block_in, row(out_bias), row(ln2_scale), row(ln2_shift), outs, out_ws
    )
    acts, slopes = zip(*[up_rows(normed2, w, b) for w, b in zip(up_ws, up_bs)])
    block_out = down_rows(resid, row(down_bias), acts, down_ws)
    down_grads, (block_out,) = beside(
        lambda xs, g: [low_product(a, g) for a in xs],
        (acts, grad_low),
        late=[(move.swap_rows, block_out)],
    )
    down = Reduction(move, table, *down_grads)
    (hg_own, up_b_own), _ = beside(
        lambda g, slope: hidden_grads(g, down_ws[0], slope), (grad_low, slopes[0]), down
    )

    def others(g, hg_own):
        hg_oth, up_b_oth = hidden_grads(g, down_ws[1], slopes[1])
        return hg_oth, up_b_oth, [dot_nn(normed2_t, h).astype(BF) for h in (hg_own, hg_oth)]

    (hg_oth, up_b_oth, up_grads), _ = beside(others, (grad_low, hg_own), down)
    up = Reduction(move, table, *up_grads)
    (branch_grad, sums_two), _ = beside(
        lambda *hs: middle_rows(resid, grad_low, row(ln2_scale), hs, up_ws), (hg_own, hg_oth), up, down
    )

    def projected(outs, g):
        own = jnp.concatenate([low_product(o, g) for o in outs[:2]])
        out_w_grads = own, low_product(outs[2], g)
        return out_w_grads, [dot_nt(g, w).astype(BF) for w in out_ws]

    (out_w_grads, out_gs), _ = beside(projected, (outs, branch_grad), down)
    proj = Reduction(move, table, *out_w_grads)

    def back(which):
        own = which >= 2
        lo = (which % 2) * half
        q, kvs = (q_own, kvs_own) if own else (q_oth, kvs_oth)
        out, log, grad = (
            (outs[which - 2], (log_a, log_b)[which - 2], out_gs[which - 2])
            if own
            else (out_oth, log_oth, out_gs[2])
        )
        inputs = q, grad, out, log, kvs
        at = 0 if own else lo
        return lambda *xs: attend_back(*xs, tables, lo, half, at), inputs

    def keys_of(x):
        return move.over_core, x[1][1]

    def unit(xs, gots):
        return unit_grads(
            move.blocks, normed1_t, tables, [x[0] for x in xs], [x[1][0] for x in xs], gots
        )

    level = lambda n: functools.partial(move.over_chip, level=n)

    def halves(total):
        return total[: total.shape[0] // 2], total[total.shape[0] // 2 :]

    oth_a, _ = beside(*back(0), up, down, proj)
    down_block, oth_a, block_out = tie(down.done, oth_a, block_out)
    down_all = move.gather(down_block)
    oth_b, (got_a,) = beside(*back(1), keys_of(oth_a), up, proj)
    own_a, (got_b,) = beside(*back(2), keys_of(oth_b), up, proj)
    (keep_oth, send, rows_oth, bias_oth), (key_got,) = beside(
        unit, ((oth_a, oth_b), (got_a, got_b)), keys_of(own_a), up, proj
    )
    (keep_a, send_a, rows_a, bias_a), (core_got,) = beside(
        unit, ((own_a,), (key_got,)), (move.over_core, send), proj
    )
    mixed = jnp.concatenate([up.done[0], proj.done[0].reshape(-1, up.done.shape[2])])
    mixed, keep_a, down_all = tie(mixed, keep_a, down_all)
    mixed_all = lax.all_gather(mixed, "dp")
    y_sends = [keep_oth[..., at : at + cols] + core_got[..., at : at + cols] for at in (0, cols)]
    own_b, (core_got_a, y_got_a, y_got_b) = beside(
        *back(3), (move.over_core, send_a), late=[(move.over_y, y) for y in y_sends]
    )
    y_got_a, own_b = tie(y_got_a, own_b)
    keep_a, send_a = halves(keep_a + core_got_a + y_got_a)
    partial, (key_got, a_got) = beside(
        lambda *xs: early_rows(qkv_own, qkv_oth, *xs),
        (rows_a, rows_oth),
        keys_of(own_b),
        late=[(level(0), send_a)],
    )
    (keep_b, send_b, rows_b, bias_b), _ = beside(unit, ((own_b,), (key_got,)))
    keep_b, a_got, y_got_b = tie(keep_b, a_got, y_got_b)
    keep_a, send_a = halves(keep_a + a_got)
    (in_grad, sums_one), (core_got, a_got) = beside(
        lambda *xs: last_rows(block_in, branch_grad, row(ln1_scale), *xs),
        (partial, qkv_own, rows_b),
        (move.over_core, send_b),
        (level(1), send_a),
    )
    keep_a, send_a = halves(keep_a + a_got)
    keep_b, send_b = halves(keep_b + core_got + y_got_b)
    in_grad, send_a, send_b, mixed_all = tie(in_grad, send_a, send_b, mixed_all)
    in_grad = move.swap_rows(in_grad)
    total_a = keep_a + move.over_chip(send_a, 2)
    unit_a = lax.all_gather(total_a[0], "dp")
    total_b = keep_b + move.over_chip(send_b, 0)
    levels = (n_dp // 2).bit_length() - 1
    for n in range(1, levels):
        keep_b, send_b = halves(total_b)
        total_b = keep_b + move.over_chip(send_b, n)
    for n in reversed(range(levels)):
        total_b = jnp.concatenate([total_b, move.over_chip(total_b, n)])
    total_b = jnp.concatenate([total_b, move.over_core(total_b)])
    qkv_g = jnp.transpose(widen(move.blocks, unit_a, total_b), (1, 0, 2))
    up_rows_each = width // n_dp
    up_all = mixed_all[:, :up_rows_each].reshape(width, -1)
    out_all = mixed_all[:, up_rows_each:].reshape(part, width)
    side = lambda a, b: jnp.concatenate([a.reshape(3, cols), b.reshape(3, cols)], axis=1).reshape(-1)
    vec, flat = move.reduce_vectors(
        jnp.concatenate([sums_one[:2], sums_two[:4]]),
        jnp.concatenate([side(bias_a[0], bias_b[0]), up_b_own[0]]),
        jnp.concatenate([bias_oth[0], up_b_oth[0]]),
    )
    f32 = lambda v: v.astype(F32)
    return (
        block_out,
        in_grad,
        vec[0],
        vec[1],
        qkv_g,
        flat[: 3 * part].reshape(3, part),
        f32(out_all),
        vec[4],
        vec[2],
        vec[3],
        f32(up_all),
        flat[3 * part :],
        f32(down_all),
        vec[5],
    )


def spread_device(*args):
    (block_in, ln1_scale, ln1_shift, qkv_weight, qkv_bias, out_weight, out_bias) = args[:7]
    (ln2_scale, ln2_shift, up_weight, up_bias, down_weight, down_bias, out_grad) = args[7:]
    gather = lambda w, axis: lax.all_gather(w, "tensor", axis=axis, tiled=True)
    scatter = lambda g, axis: lax.psum(
        lax.psum_scatter(g, "tensor", scatter_dimension=axis, tiled=True), "dp"
    ).astype(F32)
    width = qkv_weight.shape[0]
    qkv_all = gather(qkv_weight, 2)
    full = qkv_all.shape[2]
    out = block_step(
        Spread(block_in.shape[0]),
        block_in,
        ln1_scale,
        ln1_shift,
        [qkv_all.reshape(width, 3 * full)],
        [gather(qkv_bias, 1).reshape(3 * full)],
        [gather(out_weight, 0)],
        out_bias,
        ln2_scale,
        ln2_shift,
        [gather(up_weight, 1)],
        [gather(up_bias, 0)],
        [gather(down_weight, 0)],
        down_bias,
        out_grad,
    )
    block_out, in_grad, vectors, weight_grads, (qkv_b, up_b) = out
    ((qkv_g,), (out_g,), (up_g,), (down_g,)) = weight_grads
    vec = scatter(jnp.stack(vectors), 1)
    return (
        block_out,
        in_grad,
        vec[0],
        vec[1],
        scatter(qkv_g.reshape(width, 3, full), 2),
        scatter(qkv_b[0].reshape(3, full), 1),
        scatter(out_g, 0),
        vec[2],
        vec[3],
        vec[4],
        scatter(up_g, 1),
        scatter(up_b[0], 0),
        scatter(down_g, 0),
        vec[5],
    )


def solution(mesh):
    n_dp, n_tensor = mesh.shape["dp"], mesh.shape["tensor"]
    rows = P(("dp", "tensor"), None)
    vector = P("tensor")
    placed = (
        rows,
        P(),
        P(),
        P(None, None, "tensor"),
        P(None, "tensor"),
        P("tensor", None),
        P(),
        P(),
        P(),
        P(None, "tensor"),
        vector,
        P("tensor", None),
        P(),
        rows,
    )
    paired = n_tensor == 2 and n_dp >= 8 and n_dp & (n_dp - 1) == 0
    return jax.shard_map(
        functools.partial(paired_device, n_dp) if paired else spread_device,
        mesh=mesh,
        in_specs=placed,
        out_specs=(
            rows,
            rows,
            vector,
            vector,
            P(None, None, "tensor"),
            P(None, "tensor"),
            P("tensor", None),
            vector,
            vector,
            vector,
            P(None, "tensor"),
            vector,
            P("tensor", None),
            vector,
        ),
        check_vma=False,
    )
```

```python
import functools
import math

import jax
import jax.numpy as jnp
import numpy as np
from jax import lax
from jax.experimental import pallas as pl
from jax.experimental.pallas import tpu as pltpu
from jax.sharding import PartitionSpec as P

HD = 64
GH = 16
GW = 16
SEQ = 2048
EPS = 1e-06
LANES = 128
ROT = 2 * (HD // 3 // 2)
HALF_ROT = ROT // 2
LOG2E = math.log2(math.e)
SCALE = 1.0 / math.sqrt(HD)
BF = jnp.bfloat16
F32 = jnp.float32
VMEM_BYTES = 56 << 20


def dot_nt(left, right):
    return lax.dot_general(left, right, (((1,), (1,)), ((), ())), preferred_element_type=F32)


def dot_nn(left, right):
    return lax.dot_general(left, right, (((1,), (0,)), ((), ())), preferred_element_type=F32)


def dot_tn(left, right):
    return lax.dot_general(left, right, (((0,), (0,)), ((), ())), preferred_element_type=F32)


def call(kernel, flops, moved, exps=0, **kw):
    return pl.pallas_call(
        kernel,
        compiler_params=pltpu.CompilerParams(vmem_limit_bytes=VMEM_BYTES),
        cost_estimate=pl.CostEstimate(flops=flops, bytes_accessed=moved, transcendentals=exps),
        **kw,
    )


def rotary_tables(first, count):
    lane = np.arange(LANES) % HD
    axis = lane // ROT
    inside = lane % ROT
    freq = np.float32(10000.0) ** (
        -(inside % HALF_ROT).astype(np.float32) / np.float32(HALF_ROT)
    )
    turned = axis < 3
    early = turned & (inside < HALF_ROT)
    late = turned & (inside >= HALF_ROT)
    index = first + jnp.arange(count, dtype=jnp.int32)[:, None]
    places = (index // (GH * GW), index // GW % GH, index % GW)
    place = jnp.where(axis == 0, places[0], jnp.where(axis == 1, places[1], places[2]))
    angle = place.astype(F32) * freq.astype(np.float32)[None, :]
    cos = jnp.where(turned, jnp.cos(angle), 1.0)
    sin = jnp.sin(angle)
    return cos, jnp.where(early, -sin, 0.0), jnp.where(late, sin, 0.0)


def turn(x, cos, sin_a, sin_b):
    return (
        x * cos
        + pltpu.roll(x, LANES - HALF_ROT, 1) * sin_a
        + pltpu.roll(x, HALF_ROT, 1) * sin_b
    )


def turn_back(g, cos, sin_a, sin_b):
    return (
        g * cos
        + pltpu.roll(g * sin_b, LANES - HALF_ROT, 1)
        + pltpu.roll(g * sin_a, HALF_ROT, 1)
    )


def norm_kernel(stay_ref, x_ref, got_ref, scale_ref, shift_ref, rows_ref, n_ref, nt_ref):
    rows = jnp.where(stay_ref[0] == 1, x_ref[...].astype(F32), got_ref[...].astype(F32))
    rows_ref[...] = rows.astype(BF)
    normed, _, _ = norm_parts(rows, scale_ref[...], shift_ref[...])
    n_ref[...] = normed.astype(BF)
    nt_ref[...] = normed.T.astype(BF)


def norm_rows(stay, x, got, scale, shift):
    tokens, width = x.shape
    rows = min(256, tokens)
    vector = pl.BlockSpec((1, width), lambda i, t: (0, 0))
    tile = pl.BlockSpec((rows, width), lambda i, t: (i, 0))
    return pl.pallas_call(
        norm_kernel,
        grid_spec=pltpu.PrefetchScalarGridSpec(
            num_scalar_prefetch=1,
            grid=(tokens // rows,),
            in_specs=[tile, tile, vector, vector],
            out_specs=[tile, tile, pl.BlockSpec((width, rows), lambda i, t: (0, i))],
        ),
        out_shape=[jax.ShapeDtypeStruct((tokens, width), BF)] * 2
        + [jax.ShapeDtypeStruct((width, tokens), BF)],
        compiler_params=pltpu.CompilerParams(vmem_limit_bytes=VMEM_BYTES),
        cost_estimate=pl.CostEstimate(
            flops=10 * tokens * width, bytes_accessed=10 * tokens * width, transcendentals=0
        ),
    )(stay, x, got, scale, shift)


def qkv_kernel(n_ref, w_ref, b_ref, c_ref, sa_ref, sb_ref, q_ref, kv_ref, *, q_steps):
    step = pl.program_id(0)
    weight = w_ref[...].reshape(n_ref.shape[1], w_ref.shape[-1])
    rows = dot_nn(n_ref[...], weight) + b_ref[...]
    wide = rows.shape[1]

    def turned():
        tables = (c_ref[...], sa_ref[...], sb_ref[...])
        parts = [
            turn(rows[:, at : at + LANES], *tables).astype(BF) for at in range(0, wide, LANES)
        ]
        return jnp.concatenate(parts, axis=1)

    @pl.when(step < q_steps)
    def _():
        q_ref[...] = turned()

    @pl.when((step >= q_steps) & (step < 2 * q_steps))
    def _():
        kv_ref[...] = turned()

    @pl.when(step >= 2 * q_steps)
    def _():
        kv_ref[...] = rows.astype(BF)


def qkv_rows(normed, weight, bias, tables):
    tokens, width = normed.shape
    groups, _, deep, cols = weight.shape
    tile = next(t for t in (512, 256, LANES) if cols % t == 0)
    q_steps = cols // tile
    whole = lambda n: (0, 0)
    return call(
        functools.partial(qkv_kernel, q_steps=q_steps),
        2 * tokens * width * 3 * cols,
        2 * (tokens * width + width * 3 * cols + tokens * 3 * cols),
        grid=(3 * q_steps,),
        in_specs=[
            pl.BlockSpec((tokens, width), whole),
            pl.BlockSpec((groups, None, deep, tile), lambda n: (0, n // q_steps, 0, n % q_steps)),
            pl.BlockSpec((1, tile), lambda n: (0, n)),
        ]
        + [pl.BlockSpec((tokens, LANES), whole)] * 3,
        out_specs=[
            pl.BlockSpec((tokens, tile), lambda n: (0, jnp.minimum(n, q_steps - 1))),
            pl.BlockSpec((tokens, tile), lambda n: (0, jnp.maximum(n - q_steps, 0))),
        ],
        out_shape=[
            jax.ShapeDtypeStruct((tokens, cols), BF),
            jax.ShapeDtypeStruct((tokens, 2 * cols), BF),
        ],
    )(normed, weight, bias, *tables)


def attend_kernel(*refs, sources, rows_at):
    q_ref = refs[0]
    k_refs = refs[1 : 1 + sources]
    v_refs = refs[1 + sources : 1 + 2 * sources]
    o_ref, lse_ref = refs[1 + 2 * sources : 3 + 2 * sources]
    wide_refs = refs[3 + 2 * sources :]
    lane = lax.broadcasted_iota(jnp.int32, (1, LANES), 1)
    for v, wide in zip(v_refs, wide_refs):
        wide[:, :LANES] = v[...]
        wide[:, LANES:] = jnp.ones_like(v)

    def scores_of(q, head):
        q_head = jnp.where((lane // HD) == head, q, jnp.zeros_like(q))
        return [dot_nt(q_head, k[...]) for k in k_refs]

    def result(scores):
        peak = functools.reduce(
            jnp.maximum, [jnp.max(s, axis=1, keepdims=True) for s in scores]
        )
        weights = [jnp.exp2((s - peak) * (SCALE * LOG2E)).astype(BF) for s in scores]
        both = sum(dot_nn(w, v[...]) for w, v in zip(weights, wide_refs))
        total = both[:, LANES : LANES + 1]
        return both[:, :LANES] / both[:, LANES:], peak * (SCALE * LOG2E) + jnp.log2(total)

    for first in range(0, q_ref.shape[0], rows_at):
        rows = slice(first, first + rows_at)
        q = q_ref[rows, :]
        (out_0, log_0), (out_1, log_1) = [result(s) for s in [scores_of(q, h) for h in range(2)]]
        early = lane < HD
        o_ref[rows, :] = jnp.where(early, out_0, out_1).astype(BF)
        logs = jnp.where(early, log_0, log_1).T
        lse_ref[0, 0:1, rows] = logs[0:1]
        lse_ref[0, 1:2, rows] = logs[HD : HD + 1]


def attend(q, kvs, skip=0, pairs=None):
    tokens, cols = q.shape
    all_pairs = cols // LANES
    pairs = pairs or all_pairs
    cols = pairs * LANES
    keys = sum(kv.shape[0] for kv in kvs)
    q_spec = pl.BlockSpec((tokens, LANES), lambda i: (0, skip + i))
    k_specs = [pl.BlockSpec((kv.shape[0], LANES), lambda i: (0, skip + i)) for kv in kvs]
    v_specs = [
        pl.BlockSpec((kv.shape[0], LANES), lambda i: (0, all_pairs + skip + i)) for kv in kvs
    ]
    return call(
        functools.partial(attend_kernel, sources=len(kvs), rows_at=min(512, tokens)),
        4 * 4 * tokens * keys * cols,
        2 * (2 * tokens * cols + 2 * keys * cols),
        tokens * keys * 2 * pairs,
        grid=(pairs,),
        in_specs=[q_spec] + k_specs + v_specs,
        out_specs=[
            pl.BlockSpec((tokens, LANES), lambda i: (0, i)),
            pl.BlockSpec((1, 2, tokens), lambda i: (i, 0, 0)),
        ],
        out_shape=[
            jax.ShapeDtypeStruct((tokens, cols), BF),
            jax.ShapeDtypeStruct((pairs, 2, tokens), F32),
        ],
        scratch_shapes=[pltpu.VMEM((kv.shape[0], 2 * LANES), BF) for kv in kvs],
    )(q, *kvs, *kvs)


def attend_back_kernel(*refs, sources, keys_at, queries_at):
    q_ref, do_ref, o_ref, lse_ref, c_ref, sa_ref, sb_ref = refs[:7]
    at = 7
    k_refs = refs[at : at + sources]
    v_refs = refs[at + sources : at + 2 * sources]
    at += 2 * sources
    dq_ref = refs[at]
    dkv_refs = refs[at + 1 : at + 1 + sources]
    dq_acc, centre = refs[at + 1 + sources :]
    lane = lax.broadcasted_iota(jnp.int32, (1, LANES), 1)
    tokens = q_ref.shape[0]
    product = (do_ref[...].astype(F32) * o_ref[...].astype(F32)).T
    for head in range(2):
        centre[head : head + 1, :] = jnp.sum(
            product[head * HD : head * HD + HD], axis=0, keepdims=True
        )
    dq_acc[...] = jnp.zeros_like(dq_acc)
    for k_ref, v_ref, dkv_ref in zip(k_refs, v_refs, dkv_refs):

        def body(j, carry):
            rows = pl.ds(pl.multiple_of(j * keys_at, keys_at), keys_at)
            k, v = k_ref[rows, :], v_ref[rows, :]
            k_t = k.astype(F32).T.astype(BF)
            dv = jnp.zeros((keys_at, LANES), F32)
            dk = jnp.zeros((keys_at, LANES), F32)

            def products(cut, head):
                mine = (lane // HD) == head
                q, do = q_ref[cut, :], do_ref[cut, :]
                q_head = jnp.where(mine, q, jnp.zeros_like(q))
                do_head = jnp.where(mine, do, jnp.zeros_like(do))
                return q_head, do_head, dot_nt(k, q_head), dot_nt(v, do_head)

            steps = [
                (slice(first, first + queries_at), head)
                for first in range(0, tokens, queries_at)
                for head in range(2)
            ]
            later = products(*steps[0])
            for at, (cut, head) in enumerate(steps):
                q_head, do_head, scores, share_grad = later
                if at + 1 < len(steps):
                    later = products(*steps[at + 1])
                shares = jnp.exp2(scores * (SCALE * LOG2E) - lse_ref[0, head : head + 1, cut])
                score_grad = (shares * (share_grad - centre[head : head + 1, cut])).astype(BF)
                dv += dot_nn(shares.astype(BF), do_head)
                dk += dot_nn(score_grad, q_head)
                part = slice(head * HD, head * HD + HD)
                dq_acc[part, cut] += dot_nn(k_t[part], score_grad)
            dkv_ref[0, rows, :] = (dk * SCALE).astype(BF)
            dkv_ref[1, rows, :] = dv.astype(BF)
            return carry

        lax.fori_loop(0, k_ref.shape[0] // keys_at, body, 0)
    dq = (dq_acc[...] * SCALE).T
    dq_ref[...] = turn_back(dq, c_ref[...], sa_ref[...], sb_ref[...]).astype(BF)


def attend_back(q, out_grad, out, lse, kvs, tables, skip=0, pairs=None, at=0):
    tokens, cols = q.shape
    all_pairs = cols // LANES
    pairs = pairs or all_pairs
    cols = pairs * LANES
    keys = sum(kv.shape[0] for kv in kvs)
    q_spec = pl.BlockSpec((tokens, LANES), lambda i: (0, skip + i))
    o_spec = pl.BlockSpec((tokens, LANES), lambda i: (0, at + i))
    k_specs = [pl.BlockSpec((kv.shape[0], LANES), lambda i: (0, skip + i)) for kv in kvs]
    v_specs = [
        pl.BlockSpec((kv.shape[0], LANES), lambda i: (0, all_pairs + skip + i)) for kv in kvs
    ]
    dq_spec = pl.BlockSpec((tokens, LANES), lambda i: (0, i))
    dkv_specs = [pl.BlockSpec((2, kv.shape[0], LANES), lambda i: (0, 0, i)) for kv in kvs]
    table = pl.BlockSpec((tokens, LANES), lambda i: (0, 0))
    outs = call(
        functools.partial(
            attend_back_kernel, sources=len(kvs), keys_at=1024, queries_at=min(256, tokens)
        ),
        10 * 4 * tokens * keys * cols,
        2 * (4 * tokens * cols + 4 * keys * cols),
        tokens * keys * 2 * pairs,
        grid=(pairs,),
        in_specs=[q_spec, o_spec, o_spec]
        + [pl.BlockSpec((1, 2, tokens), lambda i: (at + i, 0, 0))]
        + [table] * 3
        + k_specs
        + v_specs,
        out_specs=[dq_spec] + dkv_specs,
        out_shape=[jax.ShapeDtypeStruct((tokens, cols), BF)]
        + [jax.ShapeDtypeStruct((2, kv.shape[0], cols), BF) for kv in kvs],
        scratch_shapes=[pltpu.VMEM((LANES, tokens), F32), pltpu.VMEM((2, tokens), F32)],
    )(q, out_grad, out, lse, *tables, *kvs, *kvs)
    return outs[0], outs[1:]


def key_sum_kernel(own_ref, got_ref, c_ref, sa_ref, sb_ref, dk_ref):
    total = own_ref[...].astype(F32) + got_ref[...].astype(F32)
    dk_ref[...] = turn_back(total, c_ref[...], sa_ref[...], sb_ref[...]).astype(BF)


def key_sum(own, got, tables):
    tokens, cols = own.shape
    spec = pl.BlockSpec((tokens, LANES), lambda i: (0, i))
    table = pl.BlockSpec((tokens, LANES), lambda i: (0, 0))
    return call(
        key_sum_kernel,
        12 * tokens * cols,
        6 * tokens * cols,
        grid=(cols // LANES,),
        in_specs=[spec, spec] + [table] * 3,
        out_specs=spec,
        out_shape=jax.ShapeDtypeStruct((tokens, cols), BF),
    )(own, got, *tables)


def gelu_parts(hidden):
    cdf = 0.5 + 0.5 * lax.erf(hidden * (1.0 / math.sqrt(2.0)))
    bell = jnp.exp2(hidden * hidden * (-0.5 * LOG2E))
    return hidden * cdf, cdf + hidden * (1.0 / math.sqrt(2.0 * math.pi)) * bell


def up_kernel(n_ref, w_ref, b_ref, acted_ref, slope_ref):
    hidden = dot_nn(n_ref[...], w_ref[...]) + b_ref[...]
    acted, slope = gelu_parts(hidden)
    acted_ref[...] = acted.astype(BF)
    slope_ref[...] = slope.astype(BF)


def up_rows(normed, weight, bias):
    tokens, width = normed.shape
    cols = weight.shape[1]
    tile = 512
    out = pl.BlockSpec((tokens, tile), lambda n: (0, n))
    return call(
        up_kernel,
        2 * tokens * width * cols,
        2 * (tokens * width + width * cols + 2 * tokens * cols),
        tokens * cols,
        grid=(cols // tile,),
        in_specs=[
            pl.BlockSpec((tokens, width), lambda n: (0, 0)),
            pl.BlockSpec((width, tile), lambda n: (0, n)),
            pl.BlockSpec((1, tile), lambda n: (0, n)),
        ],
        out_specs=[out, out],
        out_shape=[jax.ShapeDtypeStruct((tokens, cols), BF)] * 2,
    )(normed, weight, bias)


def hidden_grad_kernel(g_ref, w_ref, slope_ref, hg_ref, sum_ref, *, skip):
    weight = w_ref[:, skip:].reshape(hg_ref.shape[1], g_ref.shape[1])
    grad = dot_nt(g_ref[...], weight) * slope_ref[...].astype(F32)
    low = grad.astype(BF)
    hg_ref[...] = low
    sum_ref[...] = jnp.sum(low.astype(F32), axis=0, keepdims=True)


def hidden_grads(grad, down, slope):
    tokens, width = grad.shape
    down, skip = down
    groups, deep, _ = down.shape
    cols = slope.shape[1]
    tile = 512
    out = pl.BlockSpec((tokens, tile), lambda n: (0, n))
    if groups == 1:
        weight = pl.BlockSpec((1, tile, width), lambda n: (0, n, 0))
    else:
        weight = pl.BlockSpec((tile // (deep - skip), deep, width), lambda n: (n, 0, 0))
    return call(
        functools.partial(hidden_grad_kernel, skip=skip),
        2 * tokens * width * cols,
        2 * (tokens * width + width * cols + 2 * tokens * cols),
        grid=(cols // tile,),
        in_specs=[pl.BlockSpec((tokens, width), lambda n: (0, 0)), weight, out],
        out_specs=[out, pl.BlockSpec((1, tile), lambda n: (0, n))],
        out_shape=[
            jax.ShapeDtypeStruct((tokens, cols), BF),
            jax.ShapeDtypeStruct((1, cols), F32),
        ],
    )(grad, down, slope)


def norm_parts(values, gain, shift):
    centred = values - jnp.mean(values, axis=-1, keepdims=True)
    inv_dev = lax.rsqrt(jnp.mean(centred * centred, axis=-1, keepdims=True) + EPS)
    normal = centred * inv_dev
    return normal * gain + shift, normal, inv_dev


def norm_back(upstream, normal, inv_dev, gain):
    scaled = upstream * gain
    mean_first = jnp.mean(scaled, axis=-1, keepdims=True)
    mean_second = jnp.mean(scaled * normal, axis=-1, keepdims=True)
    back = inv_dev * (scaled - mean_first - normal * mean_second)
    return back, jnp.sum(upstream * normal, 0), jnp.sum(upstream, 0)


def tie(*trees):
    leaves, form = jax.tree.flatten(trees)
    return jax.tree.unflatten(form, lax.optimization_barrier(tuple(leaves)))


def project_kernel(*refs, parts):
    x_ref, b_ref, scale_ref, shift_ref = refs[:4]
    o_refs, w_refs = refs[4 : 4 + parts], refs[4 + parts : 4 + 2 * parts]
    resid_ref, n_ref, nt_ref = refs[4 + 2 * parts :]
    resid = x_ref[...].astype(F32) + b_ref[...]
    for o, w in zip(o_refs, w_refs):
        resid += dot_nn(o[...], w[...])
    normed, _, _ = norm_parts(resid, scale_ref[...], shift_ref[...])
    resid_ref[...] = resid
    n_ref[...] = normed.astype(BF)
    nt_ref[...] = normed.T.astype(BF)


def project_rows(x, bias, scale, shift, outs, weights):
    tokens, width = x.shape
    rows = min(256, tokens)
    vector = pl.BlockSpec((1, width), lambda i: (0, 0))
    tile = pl.BlockSpec((rows, width), lambda i: (i, 0))
    deep = sum(o.shape[1] for o in outs)
    return call(
        functools.partial(project_kernel, parts=len(outs)),
        2 * tokens * width * deep,
        2 * (tokens * deep + width * deep + 5 * tokens * width),
        grid=(tokens // rows,),
        in_specs=[tile, vector, vector, vector]
        + [pl.BlockSpec((rows, o.shape[1]), lambda i: (i, 0)) for o in outs]
        + [pl.BlockSpec(w.shape, lambda i: (0, 0)) for w in weights],
        out_specs=[tile, tile, pl.BlockSpec((width, rows), lambda i: (0, i))],
        out_shape=[
            jax.ShapeDtypeStruct((tokens, width), F32),
            jax.ShapeDtypeStruct((tokens, width), BF),
            jax.ShapeDtypeStruct((width, tokens), BF),
        ],
    )(x, bias, scale, shift, *outs, *weights)


def down_kernel(r_ref, b_ref, *refs, parts, skips):
    total = r_ref[...] + b_ref[...]
    for a, w, skip in zip(refs[:parts], refs[parts : 2 * parts], skips):
        total += dot_nn(a[...], w[:, skip:].reshape(a.shape[1], w.shape[2]))
    refs[-1][...] = total.astype(BF)


def down_rows(resid, bias, acts, weights):
    tokens, width = resid.shape
    weights, skips = zip(*weights)
    cols = min(512, width)
    tile = pl.BlockSpec((tokens, cols), lambda i: (0, i))
    deep = sum(a.shape[1] for a in acts)
    return call(
        functools.partial(down_kernel, parts=len(acts), skips=skips),
        2 * tokens * width * deep,
        2 * (tokens * deep + width * deep + 3 * tokens * width),
        grid=(width // cols,),
        in_specs=[tile, pl.BlockSpec((1, cols), lambda i: (0, i))]
        + [pl.BlockSpec(a.shape, lambda i: (0, 0)) for a in acts]
        + [pl.BlockSpec((*w.shape[:2], cols), lambda i: (0, 0, i)) for w in weights],
        out_specs=tile,
        out_shape=jax.ShapeDtypeStruct((tokens, width), BF),
    )(resid, bias, *acts, *weights)


def middle_kernel(r_ref, g_ref, scale_ref, *refs, parts):
    branch_ref, sums_ref = refs[-2:]
    upstream = sum(dot_nt(h[...], w[...]) for h, w in zip(refs[:parts], refs[parts : 2 * parts]))
    grad = g_ref[...].astype(F32)
    _, normal, inv_dev = norm_parts(r_ref[...], 1.0, 0.0)
    back, scale_sum, shift_sum = norm_back(upstream, normal, inv_dev, scale_ref[...])
    branch = (grad + back).astype(BF)
    branch_ref[...] = branch
    total = lambda v: jnp.sum(v, axis=0, keepdims=True)
    sums = [scale_sum[None, :], shift_sum[None, :], total(branch.astype(F32)), total(grad)]
    sums = jnp.concatenate(sums + [jnp.zeros((4, grad.shape[1]), F32)], axis=0)

    @pl.when(pl.program_id(0) == 0)
    def _():
        sums_ref[...] = sums

    @pl.when(pl.program_id(0) > 0)
    def _():
        sums_ref[...] += sums


def middle_rows(resid, grad, scale, hidden_gs, weights):
    tokens, width = resid.shape
    rows = min(256, tokens)
    tile = pl.BlockSpec((rows, width), lambda i: (i, 0))
    deep = sum(h.shape[1] for h in hidden_gs)
    return call(
        functools.partial(middle_kernel, parts=len(hidden_gs)),
        2 * tokens * width * deep,
        2 * (tokens * deep + width * deep + 4 * tokens * width),
        grid=(tokens // rows,),
        in_specs=[tile, tile, pl.BlockSpec((1, width), lambda i: (0, 0))]
        + [pl.BlockSpec((rows, h.shape[1]), lambda i: (i, 0)) for h in hidden_gs]
        + [pl.BlockSpec(w.shape, lambda i: (0, 0)) for w in weights],
        out_specs=[tile, pl.BlockSpec((8, width), lambda i: (0, 0))],
        out_shape=[
            jax.ShapeDtypeStruct((tokens, width), BF),
            jax.ShapeDtypeStruct((8, width), F32),
        ],
    )(resid, grad, scale, *hidden_gs, *weights)


def add_parts(total, w_ref, rows_ref, lo):
    cols = rows_ref.shape[1] // 3
    for kind in range(3):
        weight = w_ref[:, kind, :, lo : lo + cols].reshape(total.shape[1], cols)
        total += dot_nt(rows_ref[:, kind * cols : (kind + 1) * cols], weight)
    return total


def early_kernel(*refs):
    w_ref, rows_ref, out_ref = refs[0], refs[1], refs[-1]
    total = refs[2][...] if len(refs) == 4 else jnp.zeros(out_ref.shape, F32)
    out_ref[...] = add_parts(total, w_ref, rows_ref, 0)


def last_kernel(x_ref, g_ref, scale_ref, part_ref, own_ref, rows_ref, in_grad_ref, sums_ref):
    upstream = add_parts(part_ref[...], own_ref, rows_ref, rows_ref.shape[1] // 3)
    _, normal, inv_dev = norm_parts(x_ref[...].astype(F32), 1.0, 0.0)
    back, scale_sum, shift_sum = norm_back(upstream, normal, inv_dev, scale_ref[...])
    in_grad_ref[...] = (g_ref[...].astype(F32) + back).astype(BF)
    sums = [scale_sum[None, :], shift_sum[None, :], jnp.zeros((6, x_ref.shape[1]), F32)]
    sums = jnp.concatenate(sums, axis=0)

    @pl.when(pl.program_id(0) == 0)
    def _():
        sums_ref[...] = sums

    @pl.when(pl.program_id(0) > 0)
    def _():
        sums_ref[...] += sums


def early_rows(weight, rows_grad, *before):
    tokens, deep = rows_grad.shape
    width = weight.shape[0] * weight.shape[2]
    rows = min(512, tokens)
    block = (weight.shape[0], 3, weight.shape[2], deep // 3)
    tile = pl.BlockSpec((rows, width), lambda i: (i, 0))
    return call(
        early_kernel,
        2 * tokens * width * deep,
        2 * (tokens * deep + width * deep + 2 * tokens * width),
        grid=(tokens // rows,),
        in_specs=[
            pl.BlockSpec(block, lambda i: (0, 0, 0, 0)),
            pl.BlockSpec((rows, deep), lambda i: (i, 0)),
        ]
        + [tile for _ in before],
        out_specs=tile,
        out_shape=jax.ShapeDtypeStruct((tokens, width), F32),
    )(weight, rows_grad, *before)


def last_rows(x, branch_grad, scale, partial, own, own_rows):
    tokens, width = x.shape
    deep = own_rows.shape[1]
    rows = min(256, tokens)
    tile = pl.BlockSpec((rows, width), lambda i: (i, 0))
    return call(
        last_kernel,
        2 * tokens * width * deep,
        2 * (tokens * deep + width * deep + 5 * tokens * width),
        grid=(tokens // rows,),
        in_specs=[tile, tile, pl.BlockSpec((1, width), lambda i: (0, 0)), tile]
        + [pl.BlockSpec(own.shape, lambda i: (0, 0, 0, 0)), pl.BlockSpec((rows, deep), lambda i: (i, 0))],
        out_specs=[tile, pl.BlockSpec((8, width), lambda i: (0, 0))],
        out_shape=[
            jax.ShapeDtypeStruct((tokens, width), BF),
            jax.ShapeDtypeStruct((8, width), F32),
        ],
    )(x, branch_grad, scale, partial, own, own_rows)


def unit_kernel(t_ref, nt_ref, c_ref, sa_ref, sb_ref, *refs, chips, parts):
    dq_refs, own_refs, got_refs = refs[:parts], refs[parts : 2 * parts], refs[2 * parts : 3 * parts]
    keep_ref, send_ref, rows_out, sum_ref, acc_ref = refs[3 * parts :]
    kind = pl.program_id(0)
    cols = dq_refs[0].shape[1]
    added = lambda a, b: a[...].astype(F32) + b[...].astype(F32)

    @pl.when(kind == 0)
    def _():
        for u, dq in enumerate(dq_refs):
            rows_out[:, u * cols : (u + 1) * cols] = dq[...]

    @pl.when(kind == 1)
    def _():
        tables = (c_ref[...], sa_ref[...], sb_ref[...])
        for u, (own, got) in enumerate(zip(own_refs, got_refs)):
            total = added(own, got)
            for at in range(0, cols, LANES):
                turned = turn_back(total[:, at : at + LANES], *tables).astype(BF)
                rows_out[:, u * cols + at : u * cols + at + LANES] = turned

    @pl.when(kind == 2)
    def _():
        for u, (own, got) in enumerate(zip(own_refs, got_refs)):
            rows_out[:, u * cols : (u + 1) * cols] = added(own, got).astype(BF)

    rows = rows_out[...]
    acc_ref[...] = dot_nn(nt_ref[...], rows)
    piece = keep_ref.shape[1]
    for place in range(chips):
        for ref, which in ((keep_ref, place), (send_ref, chips + place)):
            at = pl.multiple_of(t_ref[which] * piece, piece)
            ref[place] = acc_ref[pl.ds(at, piece), :].astype(BF)
    sums = jnp.sum(rows.astype(F32), axis=0, keepdims=True)
    sum_ref[...] = jnp.broadcast_to(sums, sum_ref.shape)


def unit_grads(table, normed_t, tables, dqs, owns, gots):
    width, tokens = normed_t.shape
    parts = len(dqs)
    cols = dqs[0].shape[1]
    wide = parts * cols
    chips = table.shape[0] // 2
    piece = width // (2 * chips)
    rotary = pl.BlockSpec((tokens, LANES), lambda i, t: (0, 0))
    part = pl.BlockSpec((tokens, cols), lambda i, t: (0, 0))
    pair = pl.BlockSpec((None, tokens, cols), lambda i, t: (jnp.maximum(i - 1, 0), 0, 0))
    blocks = pl.BlockSpec((chips, None, piece, wide), lambda i, t: (0, i, 0, 0))
    return pl.pallas_call(
        functools.partial(unit_kernel, chips=chips, parts=parts),
        grid_spec=pltpu.PrefetchScalarGridSpec(
            num_scalar_prefetch=1,
            grid=(3,),
            in_specs=[pl.BlockSpec((width, tokens), lambda i, t: (0, 0))]
            + [rotary] * 3
            + [part] * parts
            + [pair] * (2 * parts),
            out_specs=[
                blocks,
                blocks,
                pl.BlockSpec((tokens, wide), lambda i, t: (0, i)),
                pl.BlockSpec((8, wide), lambda i, t: (0, i)),
            ],
            scratch_shapes=[pltpu.VMEM((width, wide), F32)],
        ),
        out_shape=[jax.ShapeDtypeStruct((chips, 3, piece, wide), BF)] * 2
        + [jax.ShapeDtypeStruct((tokens, 3 * wide), BF), jax.ShapeDtypeStruct((8, 3 * wide), F32)],
        compiler_params=pltpu.CompilerParams(vmem_limit_bytes=VMEM_BYTES),
        cost_estimate=pl.CostEstimate(
            flops=6 * tokens * width * wide,
            bytes_accessed=2 * (tokens * width + 8 * tokens * wide + 3 * width * wide),
            transcendentals=0,
        ),
    )(table, normed_t, *tables, *dqs, *owns, *gots)


def widen_kernel(t_ref, a_ref, b_ref, out_ref):
    count, piece, cols = a_ref.shape
    out_ref[:, :cols] = a_ref[...].reshape(out_ref.shape[0], cols).astype(F32)
    for place in range(count):
        rows = pl.ds(pl.multiple_of(t_ref[place] * piece, piece), piece)
        out_ref[rows, cols:] = b_ref[place].astype(F32)


def widen(table, unit_a, unit_b):
    n, _, piece, cols = unit_a.shape
    spec = pl.BlockSpec((n, None, piece, cols), lambda i, t: (0, i, 0, 0))
    return pl.pallas_call(
        widen_kernel,
        grid_spec=pltpu.PrefetchScalarGridSpec(
            num_scalar_prefetch=1,
            grid=(3,),
            in_specs=[spec, spec],
            out_specs=pl.BlockSpec((None, n * piece, 2 * cols), lambda i, t: (i, 0, 0)),
        ),
        out_shape=jax.ShapeDtypeStruct((3, n * piece, 2 * cols), F32),
        compiler_params=pltpu.CompilerParams(vmem_limit_bytes=VMEM_BYTES),
        cost_estimate=pl.CostEstimate(
            flops=0, bytes_accessed=36 * n * piece * cols, transcendentals=0
        ),
    )(table, unit_a, unit_b)


def split_kernel(t_ref, own_m, own_f, oth_m, oth_f, got_om, got_of, got_tm, got_tf, ka, kb, send, *, last):
    total = lambda a, b: (a[...].astype(F32) + b[...].astype(F32)).astype(BF)
    by_y = t_ref[last] == 0
    own_far, oth_me = total(own_f, got_of), total(oth_m, got_tm)
    ka[...] = total(own_m, got_om)
    kb[...] = jnp.where(by_y, own_far, oth_me)
    send[0] = jnp.where(by_y, oth_me, own_far)
    send[1] = total(oth_f, got_tf)


def first_split(table, own, oth, got_own, got_oth):
    chips, piece, cols = got_own.shape
    count = chips // 2
    own, oth = (g.reshape(chips, 2, piece, cols) for g in (own, oth))
    whole = lambda far: pl.BlockSpec(
        (None, None, piece, cols), lambda i, t: (t[far * count + i], t[2 * count], 0, 0)
    )
    part = lambda far: pl.BlockSpec((None, piece, cols), lambda i, t: (t[far * count + i], 0, 0))
    out = pl.BlockSpec((None, piece, cols), lambda i, t: (i, 0, 0))
    return pl.pallas_call(
        functools.partial(split_kernel, last=2 * count),
        grid_spec=pltpu.PrefetchScalarGridSpec(
            num_scalar_prefetch=1,
            grid=(count,),
            in_specs=[whole(0), whole(1)] * 2 + [part(0), part(1)] * 2,
            out_specs=[out, out, pl.BlockSpec((2, None, piece, cols), lambda i, t: (0, i, 0, 0))],
        ),
        out_shape=[jax.ShapeDtypeStruct((count, piece, cols), BF)] * 2
        + [jax.ShapeDtypeStruct((2, count, piece, cols), BF)],
        compiler_params=pltpu.CompilerParams(vmem_limit_bytes=VMEM_BYTES),
        cost_estimate=pl.CostEstimate(
            flops=4 * count * piece * cols, bytes_accessed=24 * count * piece * cols, transcendentals=0
        ),
    )(table, own, own, oth, oth, got_own, got_own, got_oth, got_oth)


class Paired:
    def __init__(self, n_dp):
        self.n_dp = n_dp
        self.me_dp = lax.axis_index("dp")
        self.me_y = lax.axis_index("tensor")
        self.core = self.me_dp % 2
        self.first = self.core * (SEQ // 2)
        chips = n_dp // 2
        levels = chips.bit_length() - 1
        places = np.arange(chips)
        far = sum(((places >> (levels - 1 - k)) & 1) << k for k in range(levels))
        chip = jnp.asarray(far, jnp.int32) ^ (self.me_dp // 2)
        self.blocks = jnp.concatenate([chip * 2 + self.core, chip * 2 + 1 - self.core]).astype(
            jnp.int32
        )

    def move(self, x, to):
        pairs = []
        for dp in range(self.n_dp):
            for y in range(2):
                a, b = to(dp, y)
                if (a, b) != (dp, y):
                    pairs.append((dp * 2 + y, a * 2 + b))
        return lax.ppermute(x, ("dp", "tensor"), pairs)

    def swap(self, rows):
        return self.move(rows, lambda dp, y: (dp - dp % 2 + y, dp % 2))

    def stays(self, rows, got):
        return jnp.where(self.core == self.me_y, rows, got)

    def over_y(self, x):
        return self.move(x, lambda dp, y: (dp, 1 - y))

    def over_core(self, x):
        return self.move(x, lambda dp, y: (dp ^ 1, y))

    def piece(self, own, axis=0):
        rows = own.shape[axis] // self.n_dp
        return lax.dynamic_slice_in_dim(own, self.me_dp * rows, rows, axis)

    def spread(self, got):
        return lax.all_gather(got, "dp", axis=0, tiled=True)

    def core_send(self, half):
        rows, cols = half.shape
        blocks = half.reshape(self.n_dp // 2, 2, rows // self.n_dp, cols)
        return lax.dynamic_index_in_dim(blocks, 1 - self.core, 1, keepdims=False)

    def over_chip(self, x, level):
        return self.move(x, lambda dp, y: (dp ^ (2 << level), y))

    def over_first(self, x):
        return self.move(x, lambda dp, y: (dp ^ 2, y) if dp % 2 else (dp, 1 - y))

    def over_second(self, x):
        return self.move(x, lambda dp, y: (dp, 1 - y) if dp % 2 else (dp ^ 2, y))

    def over_z(self, x, level):
        return self.move(x, lambda dp, y: (dp ^ (4 << level), y))

    def blocks_of(self, x_bit):
        count = self.n_dp // 4
        levels = count.bit_length() - 1
        z = self.me_dp // 4
        places = np.arange(count)
        far = sum(((places >> (levels - 1 - k)) & 1) << k for k in range(levels))
        return (jnp.asarray(far, jnp.int32) ^ z) * 2 + x_bit

    def table(self):
        x = (self.me_dp // 2) % 2
        me, far = self.blocks_of(x), self.blocks_of(1 - x)
        return jnp.concatenate([me, far, jnp.stack([self.core])]).astype(jnp.int32)

    def gather(self, block):
        return lax.all_gather(block[0], "dp", axis=0, tiled=True)

    def reduce_vectors(self, both, own, other):
        k, width = both.shape
        both = both.reshape(k, 2, width // 2)
        take = lambda b: lax.dynamic_index_in_dim(both, b, 1, keepdims=False).reshape(-1)
        mine = jnp.concatenate([take(self.me_y), own]).reshape(-1, LANES)
        theirs = jnp.concatenate([take(1 - self.me_y), other]).reshape(-1, LANES)
        total = jnp.stack([mine, theirs])
        total = total + self.over_core(total)
        for level in range((self.n_dp // 2).bit_length() - 1):
            total = total + self.over_chip(total, level)
        total = (total[0] + self.over_y(total[1])).reshape(-1)
        return total[: k * width // 2].reshape(k, width // 2), total[k * width // 2 :]


class Spread:
    def __init__(self, tokens):
        self.first = lax.axis_index("tensor") * tokens

    def swap_rows(self, rows):
        return rows

    def keys(self, kv):
        return [lax.all_gather(kv, "tensor", axis=0, tiled=True)]

    def keys_back(self, grads):
        return lax.psum_scatter(grads, "tensor", scatter_dimension=1, tiled=True)


def block_step(
    move,
    block_in,
    ln1_scale,
    ln1_shift,
    qkv_ws,
    qkv_bs,
    out_ws,
    out_bias,
    ln2_scale,
    ln2_shift,
    up_ws,
    up_bs,
    down_ws,
    down_bias,
    out_grad,
):
    f32 = lambda v: v.astype(F32)
    tokens = block_in.shape[0]
    tables = rotary_tables(move.first, tokens)
    ln1_gain, ln2_gain = f32(ln1_scale), f32(ln2_scale)
    block_in = move.swap_rows(block_in)
    x_rows = f32(block_in)
    normed1, normal1, inv_one = norm_parts(x_rows, ln1_gain, f32(ln1_shift))
    normed1 = normed1.astype(BF)
    queries, keys, outs, logs = [], [], [], []
    for weight, bias in zip(qkv_ws, qkv_bs):
        split = weight.reshape(1, weight.shape[0], 3, -1).transpose(0, 2, 1, 3)
        q, kv = qkv_rows(normed1, split, f32(bias)[None, :], tables)
        queries.append(q)
        keys.append(move.keys(kv))
    for q, kvs in zip(queries, keys):
        out, log = attend(q, kvs)
        outs.append(out)
        logs.append(log)
    grad_low = move.swap_rows(out_grad)
    grad_rows = f32(grad_low)
    branch_one = sum(dot_nn(o, w) for o, w in zip(outs, out_ws)) + f32(out_bias)
    resid = x_rows + branch_one
    normed2, normal2, inv_two = norm_parts(resid, ln2_gain, f32(ln2_shift))
    normed2 = normed2.astype(BF)
    acts, slopes = [], []
    for weight, bias in zip(up_ws, up_bs):
        acted, slope = up_rows(normed2, weight, f32(bias)[None, :])
        acts.append(acted)
        slopes.append(slope)
    branch_two = sum(dot_nn(a, w) for a, w in zip(acts, down_ws)) + f32(down_bias)
    block_out = move.swap_rows((resid + branch_two).astype(BF))
    down_bias_grad = jnp.sum(grad_rows, 0)
    down_grads = [dot_tn(a, grad_low).astype(BF) for a in acts]
    hidden_gs, up_b_grads = [], []
    for down, slope in zip(down_ws, slopes):
        hg, total = hidden_grads(grad_low, (down[None], 0), slope)
        hidden_gs.append(hg)
        up_b_grads.append(total[0])
    up_grads = [dot_tn(normed2, hg).astype(BF) for hg in hidden_gs]
    normed2_grad = sum(dot_nt(hg, w) for hg, w in zip(hidden_gs, up_ws))
    resid_part, ln2_scale_grad, ln2_shift_grad = norm_back(normed2_grad, normal2, inv_two, ln2_gain)
    resid_grad = grad_rows + resid_part
    branch_grad = resid_grad.astype(BF)
    out_bias_grad = jnp.sum(branch_grad, 0, dtype=F32)
    out_w_grads = [dot_tn(o, branch_grad).astype(BF) for o in outs]
    qkv_w_grads, qkv_b_grads = [], []
    normed1_grad = 0.0
    for q, kvs, out, log, out_w, qkv_w in zip(queries, keys, outs, logs, out_ws, qkv_ws):
        out_g = dot_nt(branch_grad, out_w).astype(BF)
        dq, (dkv,) = attend_back(q, out_g, out, log, kvs, tables)
        dk, dv = move.keys_back(dkv)
        dk = key_sum(dk, jnp.zeros_like(dk), tables)
        qkv_g = jnp.concatenate([dq, dk, dv], axis=1)
        qkv_w_grads.append(dot_tn(normed1, qkv_g).astype(BF))
        qkv_b_grads.append(jnp.sum(qkv_g, 0, dtype=F32))
        normed1_grad = normed1_grad + dot_nt(qkv_g, qkv_w)
    input_part, ln1_scale_grad, ln1_shift_grad = norm_back(normed1_grad, normal1, inv_one, ln1_gain)
    in_grad = move.swap_rows((resid_grad + input_part).astype(BF))
    vectors = [
        ln1_scale_grad,
        ln1_shift_grad,
        out_bias_grad,
        ln2_scale_grad,
        ln2_shift_grad,
        down_bias_grad,
    ]
    return (
        block_out,
        in_grad,
        vectors,
        (qkv_w_grads, out_w_grads, up_grads, down_grads),
        (qkv_b_grads, up_b_grads),
    )


class Reduction:
    def __init__(self, move, table, own, oth):
        self.move, self.table = move, table
        self.grads = own, oth
        self.sends = [move.core_send(g) for g in (own, oth)]
        self.at = 0

    def start(self):
        at = self.at
        if at == 0:
            go = self.move.over_core
        elif at == 1:
            go = self.move.over_first
        elif at == 2:
            go = self.move.over_second
        else:
            go = functools.partial(self.move.over_z, level=at - 3)
        return [go(x) for x in self.sends]

    def take(self, got):
        at, self.at = self.at, self.at + 1
        if at == 0:
            ka, kb, send = first_split(self.table, *self.grads, *got)
            self.keep, self.sends = (ka, kb), [send]
        elif at == 1:
            self.sends = [self.keep[1] + got[0][1]]
            self.keep = self.keep[0] + got[0][0]
        else:
            total = self.keep + got[0]
            half = total.shape[0] // 2
            if half:
                self.keep, self.sends = total[:half], [total[half:]]
            else:
                self.done = total

    @property
    def last(self):
        return 2 + (self.move.n_dp // 4).bit_length() - 1


def beside(compute, inputs, *steps, late=()):
    sends = [s.sends if isinstance(s, Reduction) else s[1] for s in steps]
    inputs, sends, late_sends = tie(inputs, sends, [s[1] for s in late])
    got = []
    for s, x in zip(steps, sends):
        if isinstance(s, Reduction):
            s.sends = x
            got.append(s.start())
        else:
            got.append(s[0](x))
    later = [s[0](x) for s, x in zip(late, late_sends)]
    out = compute(*inputs)
    out, got = tie(out, got)
    moved = []
    for s, x in zip(steps, got):
        if isinstance(s, Reduction):
            s.take(x)
        else:
            moved.append(x)
    return out, moved + later


def paired_device(n_dp, *args):
    (block_in, ln1_scale, ln1_shift, qkv_weight, qkv_bias, out_weight, out_bias) = args[:7]
    (ln2_scale, ln2_shift, up_weight, up_bias, down_weight, down_bias, out_grad) = args[7:]
    move = Paired(n_dp)
    row = lambda v: v.astype(F32)[None, :]
    width, _, part = qkv_weight.shape
    tokens = block_in.shape[0]
    pairs = part // LANES
    half = pairs // 2
    cols = half * LANES
    table = move.table()
    low_product = lambda a, b: dot_tn(a, b).astype(BF)

    block_got = move.swap(block_in)
    qkv_own = jnp.transpose(qkv_weight, (1, 0, 2))
    small = jnp.concatenate([qkv_bias.reshape(3 * part), up_bias])
    out_piece = move.piece(out_weight)
    out_piece = jnp.concatenate([out_piece[:, at : at + part] for at in range(0, width, part)])
    first_piece = jnp.concatenate([move.piece(qkv_own, 1), out_piece[None]])
    first_got = move.over_y(first_piece)
    small_got = move.over_y(small)
    qkv_bs = [row(v[: 3 * part]) for v in (small, small_got)]
    up_bs = [row(v[3 * part :]) for v in (small, small_got)]
    tables = rotary_tables(move.first, tokens)
    qkv_own = qkv_own[None]
    qkv_oth = lax.all_gather(first_got, "dp")
    rest = [move.piece(w) for w in (up_weight, down_weight)]
    stay = jnp.stack([(move.core == move.me_y).astype(jnp.int32)])
    block_in, normed1, normed1_t = norm_rows(
        stay, block_in, block_got, row(ln1_scale), row(ln1_shift)
    )
    (q_own, kv_own), (rest,) = beside(
        lambda n: qkv_rows(n, qkv_own, qkv_bs[0], tables),
        (normed1,),
        (lambda ws: [move.over_y(w) for w in ws], rest),
    )
    kvs_own = [kv_own, move.over_core(kv_own)]
    up_got, down_got = (move.gather(got[None]) for got in rest)
    (out_a, log_a), _ = beside(lambda q, kvs: attend(q, kvs, 0, half), (q_own, kvs_own))
    qkv_oth, out_a, out_grad = tie(qkv_oth, out_a, out_grad)
    q_oth, kv_oth = qkv_rows(normed1, qkv_oth, qkv_bs[1], tables)
    (out_b, log_b), (kv_got, grad_got) = beside(
        lambda q, kvs: attend(q, kvs, half, half),
        (q_own, kvs_own),
        (move.over_core, kv_oth),
        late=[(move.swap, out_grad)],
    )
    kvs_oth = [kv_oth, kv_got]
    (out_oth, log_oth), _ = beside(attend, (q_oth, kvs_oth))
    grad_low = move.stays(out_grad, grad_got)
    out_got = qkv_oth[:, 3].reshape(n_dp, width // part, part // n_dp, part)
    out_got = out_got.transpose(0, 2, 1, 3).reshape(part, width)
    up_ws = [up_weight, up_got]
    down_ws = [(w[None], 0) for w in (down_weight, down_got)]
    outs = [out_a, out_b, out_oth]
    out_ws = [out_weight[:cols], out_weight[cols:], out_got]

    resid, normed2, normed2_t = project_rows(
        block_in, row(out_bias), row(ln2_scale), row(ln2_shift), outs, out_ws
    )
    acts, slopes = zip(*[up_rows(normed2, w, b) for w, b in zip(up_ws, up_bs)])
    block_out = down_rows(resid, row(down_bias), acts, down_ws)
    down_grads, (block_got,) = beside(
        lambda xs, g: [low_product(a, g) for a in xs],
        (acts, grad_low),
        late=[(move.swap, block_out)],
    )
    down = Reduction(move, table, *down_grads)
    (hg_own, up_b_own), _ = beside(
        lambda g, slope: hidden_grads(g, down_ws[0], slope), (grad_low, slopes[0]), down
    )

    def others(g, hg_own):
        hg_oth, up_b_oth = hidden_grads(g, down_ws[1], slopes[1])
        return hg_oth, up_b_oth, [dot_nn(normed2_t, h).astype(BF) for h in (hg_own, hg_oth)]

    (hg_oth, up_b_oth, up_grads), _ = beside(others, (grad_low, hg_own), down)
    up = Reduction(move, table, *up_grads)
    (branch_grad, sums_two), _ = beside(
        lambda *hs: middle_rows(resid, grad_low, row(ln2_scale), hs, up_ws), (hg_own, hg_oth), up, down
    )

    def projected(outs, g):
        own = jnp.concatenate([low_product(o, g) for o in outs[:2]])
        out_w_grads = own, low_product(outs[2], g)
        return out_w_grads, [dot_nt(g, w).astype(BF) for w in out_ws]

    (out_w_grads, out_gs), _ = beside(projected, (outs, branch_grad), down)
    out_gs, block_got = tie(out_gs, block_got)
    proj = Reduction(move, table, *out_w_grads)

    def back(which):
        own = which >= 2
        lo = (which % 2) * half
        q, kvs = (q_own, kvs_own) if own else (q_oth, kvs_oth)
        out, log, grad = (
            (outs[which - 2], (log_a, log_b)[which - 2], out_gs[which - 2])
            if own
            else (out_oth, log_oth, out_gs[2])
        )
        inputs = q, grad, out, log, kvs
        at = 0 if own else lo
        return lambda *xs: attend_back(*xs, tables, lo, half, at), inputs

    def keys_of(x):
        return move.over_core, x[1][1]

    def unit(xs, gots):
        return unit_grads(
            move.blocks, normed1_t, tables, [x[0] for x in xs], [x[1][0] for x in xs], gots
        )

    over_x = functools.partial(move.over_chip, level=0)
    others_z = (8, 4, 12)

    def over_z(parts):
        return [
            move.move(p, lambda dp, y, far=far: (dp ^ far, y)) for p, far in zip(parts, others_z)
        ]

    def z_parts(total):
        return total[:1], [total[n : n + 1] for n in range(1, 4)]

    def halves(total):
        return total[: total.shape[0] // 2], total[total.shape[0] // 2 :]

    oth_a, _ = beside(*back(0), up, down, proj)
    down_block, oth_a = tie(down.done, oth_a)
    down_all = move.gather(down_block)
    oth_b, (got_a,) = beside(*back(1), keys_of(oth_a), up, proj)
    own_a, (got_b,) = beside(*back(2), keys_of(oth_b), up, proj)
    (keep_oth, send, rows_oth, bias_oth), (key_got,) = beside(
        unit, ((oth_a, oth_b), (got_a, got_b)), keys_of(own_a), up, proj
    )
    (keep_a, send_a, rows_a, bias_a), (core_got,) = beside(
        unit, ((own_a,), (key_got,)), (move.over_core, send), proj
    )
    mixed = jnp.concatenate([up.done[0], proj.done[0].reshape(-1, up.done.shape[2])])
    mixed, keep_a, down_all = tie(mixed, keep_a, down_all)
    mixed_all = lax.all_gather(mixed, "dp")
    y_sends = [keep_oth[..., at : at + cols] + core_got[..., at : at + cols] for at in (0, cols)]
    own_b, (core_got_a, y_got_a, y_got_b) = beside(
        *back(3), (move.over_core, send_a), late=[(move.over_y, y) for y in y_sends]
    )
    y_got_a, own_b = tie(y_got_a, own_b)
    keep_a, send_a = halves(keep_a + core_got_a + y_got_a)
    partial, (key_got, a_got) = beside(
        early_rows, (qkv_oth, rows_oth), keys_of(own_b), late=[(over_x, send_a)]
    )
    (keep_b, send_b, rows_b, bias_b), _ = beside(unit, ((own_b,), (key_got,)))
    keep_b, a_got, y_got_b = tie(keep_b, a_got, y_got_b)
    keep_a, send_a = z_parts(keep_a + a_got)
    partial, (core_got, a_got) = beside(
        early_rows, (qkv_own, rows_a, partial), (move.over_core, send_b), (over_z, send_a)
    )
    total_a = keep_a + sum(a_got)
    keep_b, send_b = halves(keep_b + core_got + y_got_b)
    mixed_all, partial, total_a = tie(mixed_all, partial, total_a)
    unit_a = lax.all_gather(total_a[0], "dp")
    (in_grad, sums_one), (b_got,) = beside(
        lambda *xs: last_rows(block_in, branch_grad, row(ln1_scale), *xs),
        (partial, qkv_own, rows_b),
        (over_x, send_b),
    )
    in_grad, mixed_all, block_got, down_all = tie(in_grad, mixed_all, block_got, down_all)
    in_grad_got = move.swap(in_grad)
    keep_b, send_b = z_parts(keep_b + b_got)
    total_b = keep_b + sum(over_z(send_b))
    total_b = jnp.concatenate([total_b] + over_z([total_b] * 3))
    total_b, unit_a = tie(total_b, unit_a)
    total_b = jnp.concatenate([total_b, over_x(total_b)])
    total_b = jnp.concatenate([total_b, move.over_core(total_b)])
    qkv_g = jnp.transpose(widen(move.blocks, unit_a, total_b), (1, 0, 2))
    up_rows_each = width // n_dp
    up_all = mixed_all[:, :up_rows_each].reshape(width, -1)
    out_all = mixed_all[:, up_rows_each:].reshape(part, width)
    side = lambda a, b: jnp.concatenate([a.reshape(3, cols), b.reshape(3, cols)], axis=1).reshape(-1)
    vec, flat = move.reduce_vectors(
        jnp.concatenate([sums_one[:2], sums_two[:4]]),
        jnp.concatenate([side(bias_a[0], bias_b[0]), up_b_own[0]]),
        jnp.concatenate([bias_oth[0], up_b_oth[0]]),
    )
    f32 = lambda v: v.astype(F32)
    return (
        move.stays(block_out, block_got),
        move.stays(in_grad, in_grad_got),
        vec[0],
        vec[1],
        qkv_g,
        flat[: 3 * part].reshape(3, part),
        f32(out_all),
        vec[4],
        vec[2],
        vec[3],
        f32(up_all),
        flat[3 * part :],
        f32(down_all),
        vec[5],
    )


def spread_device(*args):
    (block_in, ln1_scale, ln1_shift, qkv_weight, qkv_bias, out_weight, out_bias) = args[:7]
    (ln2_scale, ln2_shift, up_weight, up_bias, down_weight, down_bias, out_grad) = args[7:]
    gather = lambda w, axis: lax.all_gather(w, "tensor", axis=axis, tiled=True)
    scatter = lambda g, axis: lax.psum(
        lax.psum_scatter(g, "tensor", scatter_dimension=axis, tiled=True), "dp"
    ).astype(F32)
    width = qkv_weight.shape[0]
    qkv_all = gather(qkv_weight, 2)
    full = qkv_all.shape[2]
    out = block_step(
        Spread(block_in.shape[0]),
        block_in,
        ln1_scale,
        ln1_shift,
        [qkv_all.reshape(width, 3 * full)],
        [gather(qkv_bias, 1).reshape(3 * full)],
        [gather(out_weight, 0)],
        out_bias,
        ln2_scale,
        ln2_shift,
        [gather(up_weight, 1)],
        [gather(up_bias, 0)],
        [gather(down_weight, 0)],
        down_bias,
        out_grad,
    )
    block_out, in_grad, vectors, weight_grads, (qkv_b, up_b) = out
    ((qkv_g,), (out_g,), (up_g,), (down_g,)) = weight_grads
    vec = scatter(jnp.stack(vectors), 1)
    return (
        block_out,
        in_grad,
        vec[0],
        vec[1],
        scatter(qkv_g.reshape(width, 3, full), 2),
        scatter(qkv_b[0].reshape(3, full), 1),
        scatter(out_g, 0),
        vec[2],
        vec[3],
        vec[4],
        scatter(up_g, 1),
        scatter(up_b[0], 0),
        scatter(down_g, 0),
        vec[5],
    )


def solution(mesh):
    n_dp, n_tensor = mesh.shape["dp"], mesh.shape["tensor"]
    rows = P(("dp", "tensor"), None)
    vector = P("tensor")
    placed = (
        rows,
        P(),
        P(),
        P(None, None, "tensor"),
        P(None, "tensor"),
        P("tensor", None),
        P(),
        P(),
        P(),
        P(None, "tensor"),
        vector,
        P("tensor", None),
        P(),
        rows,
    )
    paired = n_tensor == 2 and n_dp == 16
    return jax.shard_map(
        functools.partial(paired_device, n_dp) if paired else spread_device,
        mesh=mesh,
        in_specs=placed,
        out_specs=(
            rows,
            rows,
            vector,
            vector,
            P(None, None, "tensor"),
            P(None, "tensor"),
            P("tensor", None),
            vector,
            vector,
            vector,
            P(None, "tensor"),
            vector,
            P("tensor", None),
            vector,
        ),
        check_vma=False,
    )
```

```python
import functools
import math

import jax
import jax.numpy as jnp
import numpy as np
from jax import lax
from jax.experimental import pallas as pl
from jax.experimental.pallas import tpu as pltpu
from jax.sharding import PartitionSpec as P

HD = 64
GH = 16
GW = 16
SEQ = 2048
EPS = 1e-06
LANES = 128
ROT = 2 * (HD // 3 // 2)
HALF_ROT = ROT // 2
LOG2E = math.log2(math.e)
SCALE = 1.0 / math.sqrt(HD)
BF = jnp.bfloat16
F32 = jnp.float32
VMEM_BYTES = 56 << 20


def dot_nt(left, right):
    return lax.dot_general(left, right, (((1,), (1,)), ((), ())), preferred_element_type=F32)


def dot_nn(left, right):
    return lax.dot_general(left, right, (((1,), (0,)), ((), ())), preferred_element_type=F32)


def dot_tn(left, right):
    return lax.dot_general(left, right, (((0,), (0,)), ((), ())), preferred_element_type=F32)


def call(kernel, flops, moved, exps=0, **kw):
    return pl.pallas_call(
        kernel,
        compiler_params=pltpu.CompilerParams(vmem_limit_bytes=VMEM_BYTES),
        cost_estimate=pl.CostEstimate(flops=flops, bytes_accessed=moved, transcendentals=exps),
        **kw,
    )


def rotary_tables(first, count):
    lane = np.arange(LANES) % HD
    axis = lane // ROT
    inside = lane % ROT
    freq = np.float32(10000.0) ** (
        -(inside % HALF_ROT).astype(np.float32) / np.float32(HALF_ROT)
    )
    turned = axis < 3
    early = turned & (inside < HALF_ROT)
    late = turned & (inside >= HALF_ROT)
    index = first + jnp.arange(count, dtype=jnp.int32)[:, None]
    places = (index // (GH * GW), index // GW % GH, index % GW)
    place = jnp.where(axis == 0, places[0], jnp.where(axis == 1, places[1], places[2]))
    angle = place.astype(F32) * freq.astype(np.float32)[None, :]
    cos = jnp.where(turned, jnp.cos(angle), 1.0)
    sin = jnp.sin(angle)
    return cos, jnp.where(early, -sin, 0.0), jnp.where(late, sin, 0.0)


def turn(x, cos, sin_a, sin_b):
    return (
        x * cos
        + pltpu.roll(x, LANES - HALF_ROT, 1) * sin_a
        + pltpu.roll(x, HALF_ROT, 1) * sin_b
    )


def turn_back(g, cos, sin_a, sin_b):
    return (
        g * cos
        + pltpu.roll(g * sin_b, LANES - HALF_ROT, 1)
        + pltpu.roll(g * sin_a, HALF_ROT, 1)
    )


def norm_kernel(stay_ref, x_ref, got_ref, scale_ref, shift_ref, rows_ref, n_ref, nt_ref):
    rows = jnp.where(stay_ref[0] == 1, x_ref[...].astype(F32), got_ref[...].astype(F32))
    rows_ref[...] = rows.astype(BF)
    normed, _, _ = norm_parts(rows, scale_ref[...], shift_ref[...])
    n_ref[...] = normed.astype(BF)
    nt_ref[...] = normed.T.astype(BF)


def norm_rows(stay, x, got, scale, shift):
    tokens, width = x.shape
    rows = min(256, tokens)
    vector = pl.BlockSpec((1, width), lambda i, t: (0, 0))
    tile = pl.BlockSpec((rows, width), lambda i, t: (i, 0))
    return pl.pallas_call(
        norm_kernel,
        grid_spec=pltpu.PrefetchScalarGridSpec(
            num_scalar_prefetch=1,
            grid=(tokens // rows,),
            in_specs=[tile, tile, vector, vector],
            out_specs=[tile, tile, pl.BlockSpec((width, rows), lambda i, t: (0, i))],
        ),
        out_shape=[jax.ShapeDtypeStruct((tokens, width), BF)] * 2
        + [jax.ShapeDtypeStruct((width, tokens), BF)],
        compiler_params=pltpu.CompilerParams(vmem_limit_bytes=VMEM_BYTES),
        cost_estimate=pl.CostEstimate(
            flops=10 * tokens * width, bytes_accessed=10 * tokens * width, transcendentals=0
        ),
    )(stay, x, got, scale, shift)


def qkv_kernel(n_ref, w_ref, b_ref, c_ref, sa_ref, sb_ref, q_ref, kv_ref, *, q_steps):
    step = pl.program_id(0)
    weight = w_ref[...].reshape(n_ref.shape[1], w_ref.shape[-1])
    rows = dot_nn(n_ref[...], weight) + b_ref[...]
    wide = rows.shape[1]

    def turned():
        tables = (c_ref[...], sa_ref[...], sb_ref[...])
        parts = [
            turn(rows[:, at : at + LANES], *tables).astype(BF) for at in range(0, wide, LANES)
        ]
        return jnp.concatenate(parts, axis=1)

    @pl.when(step < q_steps)
    def _():
        q_ref[...] = turned()

    @pl.when((step >= q_steps) & (step < 2 * q_steps))
    def _():
        kv_ref[...] = turned()

    @pl.when(step >= 2 * q_steps)
    def _():
        kv_ref[...] = rows.astype(BF)


def qkv_rows(normed, weight, bias, tables):
    tokens, width = normed.shape
    groups, _, deep, cols = weight.shape
    tile = next(t for t in (512, 256, LANES) if cols % t == 0)
    q_steps = cols // tile
    whole = lambda n: (0, 0)
    return call(
        functools.partial(qkv_kernel, q_steps=q_steps),
        2 * tokens * width * 3 * cols,
        2 * (tokens * width + width * 3 * cols + tokens * 3 * cols),
        grid=(3 * q_steps,),
        in_specs=[
            pl.BlockSpec((tokens, width), whole),
            pl.BlockSpec((groups, None, deep, tile), lambda n: (0, n // q_steps, 0, n % q_steps)),
            pl.BlockSpec((1, tile), lambda n: (0, n)),
        ]
        + [pl.BlockSpec((tokens, LANES), whole)] * 3,
        out_specs=[
            pl.BlockSpec((tokens, tile), lambda n: (0, jnp.minimum(n, q_steps - 1))),
            pl.BlockSpec((tokens, tile), lambda n: (0, jnp.maximum(n - q_steps, 0))),
        ],
        out_shape=[
            jax.ShapeDtypeStruct((tokens, cols), BF),
            jax.ShapeDtypeStruct((tokens, 2 * cols), BF),
        ],
    )(normed, weight, bias, *tables)


def attend_kernel(*refs, sources, rows_at):
    q_ref = refs[0]
    k_refs = refs[1 : 1 + sources]
    v_refs = refs[1 + sources : 1 + 2 * sources]
    o_ref, lse_ref = refs[1 + 2 * sources : 3 + 2 * sources]
    wide_refs = refs[3 + 2 * sources :]
    lane = lax.broadcasted_iota(jnp.int32, (1, LANES), 1)
    for v, wide in zip(v_refs, wide_refs):
        wide[:, :LANES] = v[...]
        wide[:, LANES:] = jnp.ones_like(v)

    def scores_of(q, head):
        q_head = jnp.where((lane // HD) == head, q, jnp.zeros_like(q))
        return [dot_nt(q_head, k[...]) for k in k_refs]

    def result(scores):
        peak = functools.reduce(
            jnp.maximum, [jnp.max(s, axis=1, keepdims=True) for s in scores]
        )
        weights = [jnp.exp2((s - peak) * (SCALE * LOG2E)).astype(BF) for s in scores]
        both = sum(dot_nn(w, v[...]) for w, v in zip(weights, wide_refs))
        total = both[:, LANES : LANES + 1]
        return both[:, :LANES] / both[:, LANES:], peak * (SCALE * LOG2E) + jnp.log2(total)

    for first in range(0, q_ref.shape[0], rows_at):
        rows = slice(first, first + rows_at)
        q = q_ref[rows, :]
        (out_0, log_0), (out_1, log_1) = [result(s) for s in [scores_of(q, h) for h in range(2)]]
        early = lane < HD
        o_ref[rows, :] = jnp.where(early, out_0, out_1).astype(BF)
        logs = jnp.where(early, log_0, log_1).T
        lse_ref[0, 0:1, rows] = logs[0:1]
        lse_ref[0, 1:2, rows] = logs[HD : HD + 1]


def attend(q, kvs, skip=0, pairs=None):
    tokens, cols = q.shape
    all_pairs = cols // LANES
    pairs = pairs or all_pairs
    cols = pairs * LANES
    keys = sum(kv.shape[0] for kv in kvs)
    q_spec = pl.BlockSpec((tokens, LANES), lambda i: (0, skip + i))
    k_specs = [pl.BlockSpec((kv.shape[0], LANES), lambda i: (0, skip + i)) for kv in kvs]
    v_specs = [
        pl.BlockSpec((kv.shape[0], LANES), lambda i: (0, all_pairs + skip + i)) for kv in kvs
    ]
    return call(
        functools.partial(attend_kernel, sources=len(kvs), rows_at=min(512, tokens)),
        4 * 4 * tokens * keys * cols,
        2 * (2 * tokens * cols + 2 * keys * cols),
        tokens * keys * 2 * pairs,
        grid=(pairs,),
        in_specs=[q_spec] + k_specs + v_specs,
        out_specs=[
            pl.BlockSpec((tokens, LANES), lambda i: (0, i)),
            pl.BlockSpec((1, 2, tokens), lambda i: (i, 0, 0)),
        ],
        out_shape=[
            jax.ShapeDtypeStruct((tokens, cols), BF),
            jax.ShapeDtypeStruct((pairs, 2, tokens), F32),
        ],
        scratch_shapes=[pltpu.VMEM((kv.shape[0], 2 * LANES), BF) for kv in kvs],
    )(q, *kvs, *kvs)


def attend_back_kernel(*refs, sources, keys_at, queries_at):
    q_ref, do_ref, o_ref, lse_ref, c_ref, sa_ref, sb_ref = refs[:7]
    at = 7
    k_refs = refs[at : at + sources]
    v_refs = refs[at + sources : at + 2 * sources]
    at += 2 * sources
    dq_ref = refs[at]
    dkv_refs = refs[at + 1 : at + 1 + sources]
    dq_acc, centre = refs[at + 1 + sources :]
    lane = lax.broadcasted_iota(jnp.int32, (1, LANES), 1)
    tokens = q_ref.shape[0]
    product = (do_ref[...].astype(F32) * o_ref[...].astype(F32)).T
    for head in range(2):
        centre[head : head + 1, :] = jnp.sum(
            product[head * HD : head * HD + HD], axis=0, keepdims=True
        )
    dq_acc[...] = jnp.zeros_like(dq_acc)
    for k_ref, v_ref, dkv_ref in zip(k_refs, v_refs, dkv_refs):

        def body(j, carry):
            rows = pl.ds(pl.multiple_of(j * keys_at, keys_at), keys_at)
            k, v = k_ref[rows, :], v_ref[rows, :]
            k_t = k.astype(F32).T.astype(BF)
            dv = jnp.zeros((keys_at, LANES), F32)
            dk = jnp.zeros((keys_at, LANES), F32)

            def products(cut, head):
                mine = (lane // HD) == head
                q, do = q_ref[cut, :], do_ref[cut, :]
                q_head = jnp.where(mine, q, jnp.zeros_like(q))
                do_head = jnp.where(mine, do, jnp.zeros_like(do))
                return q_head, do_head, dot_nt(k, q_head), dot_nt(v, do_head)

            steps = [
                (slice(first, first + queries_at), head)
                for first in range(0, tokens, queries_at)
                for head in range(2)
            ]
            later = products(*steps[0])
            for at, (cut, head) in enumerate(steps):
                q_head, do_head, scores, share_grad = later
                if at + 1 < len(steps):
                    later = products(*steps[at + 1])
                shares = jnp.exp2(scores * (SCALE * LOG2E) - lse_ref[0, head : head + 1, cut])
                score_grad = (shares * (share_grad - centre[head : head + 1, cut])).astype(BF)
                dv += dot_nn(shares.astype(BF), do_head)
                dk += dot_nn(score_grad, q_head)
                part = slice(head * HD, head * HD + HD)
                dq_acc[part, cut] += dot_nn(k_t[part], score_grad)
            dkv_ref[0, rows, :] = (dk * SCALE).astype(BF)
            dkv_ref[1, rows, :] = dv.astype(BF)
            return carry

        lax.fori_loop(0, k_ref.shape[0] // keys_at, body, 0)
    dq = (dq_acc[...] * SCALE).T
    dq_ref[...] = turn_back(dq, c_ref[...], sa_ref[...], sb_ref[...]).astype(BF)


def attend_back(q, out_grad, out, lse, kvs, tables, skip=0, pairs=None, at=0):
    tokens, cols = q.shape
    all_pairs = cols // LANES
    pairs = pairs or all_pairs
    cols = pairs * LANES
    keys = sum(kv.shape[0] for kv in kvs)
    q_spec = pl.BlockSpec((tokens, LANES), lambda i: (0, skip + i))
    o_spec = pl.BlockSpec((tokens, LANES), lambda i: (0, at + i))
    k_specs = [pl.BlockSpec((kv.shape[0], LANES), lambda i: (0, skip + i)) for kv in kvs]
    v_specs = [
        pl.BlockSpec((kv.shape[0], LANES), lambda i: (0, all_pairs + skip + i)) for kv in kvs
    ]
    dq_spec = pl.BlockSpec((tokens, LANES), lambda i: (0, i))
    dkv_specs = [pl.BlockSpec((2, kv.shape[0], LANES), lambda i: (0, 0, i)) for kv in kvs]
    table = pl.BlockSpec((tokens, LANES), lambda i: (0, 0))
    outs = call(
        functools.partial(
            attend_back_kernel, sources=len(kvs), keys_at=1024, queries_at=min(256, tokens)
        ),
        10 * 4 * tokens * keys * cols,
        2 * (4 * tokens * cols + 4 * keys * cols),
        tokens * keys * 2 * pairs,
        grid=(pairs,),
        in_specs=[q_spec, o_spec, o_spec]
        + [pl.BlockSpec((1, 2, tokens), lambda i: (at + i, 0, 0))]
        + [table] * 3
        + k_specs
        + v_specs,
        out_specs=[dq_spec] + dkv_specs,
        out_shape=[jax.ShapeDtypeStruct((tokens, cols), BF)]
        + [jax.ShapeDtypeStruct((2, kv.shape[0], cols), BF) for kv in kvs],
        scratch_shapes=[pltpu.VMEM((LANES, tokens), F32), pltpu.VMEM((2, tokens), F32)],
    )(q, out_grad, out, lse, *tables, *kvs, *kvs)
    return outs[0], outs[1:]


def key_sum_kernel(own_ref, got_ref, c_ref, sa_ref, sb_ref, dk_ref):
    total = own_ref[...].astype(F32) + got_ref[...].astype(F32)
    dk_ref[...] = turn_back(total, c_ref[...], sa_ref[...], sb_ref[...]).astype(BF)


def key_sum(own, got, tables):
    tokens, cols = own.shape
    spec = pl.BlockSpec((tokens, LANES), lambda i: (0, i))
    table = pl.BlockSpec((tokens, LANES), lambda i: (0, 0))
    return call(
        key_sum_kernel,
        12 * tokens * cols,
        6 * tokens * cols,
        grid=(cols // LANES,),
        in_specs=[spec, spec] + [table] * 3,
        out_specs=spec,
        out_shape=jax.ShapeDtypeStruct((tokens, cols), BF),
    )(own, got, *tables)


def gelu_parts(hidden):
    cdf = 0.5 + 0.5 * lax.erf(hidden * (1.0 / math.sqrt(2.0)))
    bell = jnp.exp2(hidden * hidden * (-0.5 * LOG2E))
    return hidden * cdf, cdf + hidden * (1.0 / math.sqrt(2.0 * math.pi)) * bell


def up_kernel(n_ref, w_ref, b_ref, acted_ref, slope_ref):
    hidden = dot_nn(n_ref[...], w_ref[...]) + b_ref[...]
    acted, slope = gelu_parts(hidden)
    acted_ref[...] = acted.astype(BF)
    slope_ref[...] = slope.astype(BF)


def up_rows(normed, weight, bias):
    tokens, width = normed.shape
    cols = weight.shape[1]
    tile = 512
    out = pl.BlockSpec((tokens, tile), lambda n: (0, n))
    return call(
        up_kernel,
        2 * tokens * width * cols,
        2 * (tokens * width + width * cols + 2 * tokens * cols),
        tokens * cols,
        grid=(cols // tile,),
        in_specs=[
            pl.BlockSpec((tokens, width), lambda n: (0, 0)),
            pl.BlockSpec((width, tile), lambda n: (0, n)),
            pl.BlockSpec((1, tile), lambda n: (0, n)),
        ],
        out_specs=[out, out],
        out_shape=[jax.ShapeDtypeStruct((tokens, cols), BF)] * 2,
    )(normed, weight, bias)


def hidden_grad_kernel(g_ref, w_ref, slope_ref, hg_ref, sum_ref, *, skip):
    weight = w_ref[:, skip:].reshape(hg_ref.shape[1], g_ref.shape[1])
    grad = dot_nt(g_ref[...], weight) * slope_ref[...].astype(F32)
    low = grad.astype(BF)
    hg_ref[...] = low
    sum_ref[...] = jnp.sum(low.astype(F32), axis=0, keepdims=True)


def hidden_grads(grad, down, slope):
    tokens, width = grad.shape
    down, skip = down
    groups, deep, _ = down.shape
    cols = slope.shape[1]
    tile = 512
    out = pl.BlockSpec((tokens, tile), lambda n: (0, n))
    if groups == 1:
        weight = pl.BlockSpec((1, tile, width), lambda n: (0, n, 0))
    else:
        weight = pl.BlockSpec((tile // (deep - skip), deep, width), lambda n: (n, 0, 0))
    return call(
        functools.partial(hidden_grad_kernel, skip=skip),
        2 * tokens * width * cols,
        2 * (tokens * width + width * cols + 2 * tokens * cols),
        grid=(cols // tile,),
        in_specs=[pl.BlockSpec((tokens, width), lambda n: (0, 0)), weight, out],
        out_specs=[out, pl.BlockSpec((1, tile), lambda n: (0, n))],
        out_shape=[
            jax.ShapeDtypeStruct((tokens, cols), BF),
            jax.ShapeDtypeStruct((1, cols), F32),
        ],
    )(grad, down, slope)


def norm_parts(values, gain, shift):
    centred = values - jnp.mean(values, axis=-1, keepdims=True)
    inv_dev = lax.rsqrt(jnp.mean(centred * centred, axis=-1, keepdims=True) + EPS)
    normal = centred * inv_dev
    return normal * gain + shift, normal, inv_dev


def norm_back(upstream, normal, inv_dev, gain):
    scaled = upstream * gain
    mean_first = jnp.mean(scaled, axis=-1, keepdims=True)
    mean_second = jnp.mean(scaled * normal, axis=-1, keepdims=True)
    back = inv_dev * (scaled - mean_first - normal * mean_second)
    return back, jnp.sum(upstream * normal, 0), jnp.sum(upstream, 0)


def tie(*trees):
    leaves, form = jax.tree.flatten(trees)
    return jax.tree.unflatten(form, lax.optimization_barrier(tuple(leaves)))


def project_kernel(*refs, parts):
    x_ref, b_ref, scale_ref, shift_ref = refs[:4]
    o_refs, w_refs = refs[4 : 4 + parts], refs[4 + parts : 4 + 2 * parts]
    resid_ref, n_ref, nt_ref = refs[4 + 2 * parts :]
    resid = x_ref[...].astype(F32) + b_ref[...]
    for o, w in zip(o_refs, w_refs):
        resid += dot_nn(o[...], w[...])
    normed, _, _ = norm_parts(resid, scale_ref[...], shift_ref[...])
    resid_ref[...] = resid
    n_ref[...] = normed.astype(BF)
    nt_ref[...] = normed.T.astype(BF)


def project_rows(x, bias, scale, shift, outs, weights):
    tokens, width = x.shape
    rows = min(256, tokens)
    vector = pl.BlockSpec((1, width), lambda i: (0, 0))
    tile = pl.BlockSpec((rows, width), lambda i: (i, 0))
    deep = sum(o.shape[1] for o in outs)
    return call(
        functools.partial(project_kernel, parts=len(outs)),
        2 * tokens * width * deep,
        2 * (tokens * deep + width * deep + 5 * tokens * width),
        grid=(tokens // rows,),
        in_specs=[tile, vector, vector, vector]
        + [pl.BlockSpec((rows, o.shape[1]), lambda i: (i, 0)) for o in outs]
        + [pl.BlockSpec(w.shape, lambda i: (0, 0)) for w in weights],
        out_specs=[tile, tile, pl.BlockSpec((width, rows), lambda i: (0, i))],
        out_shape=[
            jax.ShapeDtypeStruct((tokens, width), F32),
            jax.ShapeDtypeStruct((tokens, width), BF),
            jax.ShapeDtypeStruct((width, tokens), BF),
        ],
    )(x, bias, scale, shift, *outs, *weights)


def down_kernel(r_ref, b_ref, *refs, parts, skips):
    total = r_ref[...] + b_ref[...]
    for a, w, skip in zip(refs[:parts], refs[parts : 2 * parts], skips):
        total += dot_nn(a[...], w[:, skip:].reshape(a.shape[1], w.shape[2]))
    refs[-1][...] = total.astype(BF)


def down_rows(resid, bias, acts, weights):
    tokens, width = resid.shape
    weights, skips = zip(*weights)
    cols = min(512, width)
    tile = pl.BlockSpec((tokens, cols), lambda i: (0, i))
    deep = sum(a.shape[1] for a in acts)
    return call(
        functools.partial(down_kernel, parts=len(acts), skips=skips),
        2 * tokens * width * deep,
        2 * (tokens * deep + width * deep + 3 * tokens * width),
        grid=(width // cols,),
        in_specs=[tile, pl.BlockSpec((1, cols), lambda i: (0, i))]
        + [pl.BlockSpec(a.shape, lambda i: (0, 0)) for a in acts]
        + [pl.BlockSpec((*w.shape[:2], cols), lambda i: (0, 0, i)) for w in weights],
        out_specs=tile,
        out_shape=jax.ShapeDtypeStruct((tokens, width), BF),
    )(resid, bias, *acts, *weights)


def middle_kernel(r_ref, g_ref, scale_ref, *refs, parts):
    branch_ref, sums_ref = refs[-2:]
    upstream = sum(dot_nt(h[...], w[...]) for h, w in zip(refs[:parts], refs[parts : 2 * parts]))
    grad = g_ref[...].astype(F32)
    _, normal, inv_dev = norm_parts(r_ref[...], 1.0, 0.0)
    back, scale_sum, shift_sum = norm_back(upstream, normal, inv_dev, scale_ref[...])
    branch = (grad + back).astype(BF)
    branch_ref[...] = branch
    total = lambda v: jnp.sum(v, axis=0, keepdims=True)
    sums = [scale_sum[None, :], shift_sum[None, :], total(branch.astype(F32)), total(grad)]
    sums = jnp.concatenate(sums + [jnp.zeros((4, grad.shape[1]), F32)], axis=0)

    @pl.when(pl.program_id(0) == 0)
    def _():
        sums_ref[...] = sums

    @pl.when(pl.program_id(0) > 0)
    def _():
        sums_ref[...] += sums


def middle_rows(resid, grad, scale, hidden_gs, weights):
    tokens, width = resid.shape
    rows = min(256, tokens)
    tile = pl.BlockSpec((rows, width), lambda i: (i, 0))
    deep = sum(h.shape[1] for h in hidden_gs)
    return call(
        functools.partial(middle_kernel, parts=len(hidden_gs)),
        2 * tokens * width * deep,
        2 * (tokens * deep + width * deep + 4 * tokens * width),
        grid=(tokens // rows,),
        in_specs=[tile, tile, pl.BlockSpec((1, width), lambda i: (0, 0))]
        + [pl.BlockSpec((rows, h.shape[1]), lambda i: (i, 0)) for h in hidden_gs]
        + [pl.BlockSpec(w.shape, lambda i: (0, 0)) for w in weights],
        out_specs=[tile, pl.BlockSpec((8, width), lambda i: (0, 0))],
        out_shape=[
            jax.ShapeDtypeStruct((tokens, width), BF),
            jax.ShapeDtypeStruct((8, width), F32),
        ],
    )(resid, grad, scale, *hidden_gs, *weights)


def add_parts(total, w_ref, rows_ref, lo):
    cols = rows_ref.shape[1] // 3
    for kind in range(3):
        weight = w_ref[:, kind, :, lo : lo + cols].reshape(total.shape[1], cols)
        total += dot_nt(rows_ref[:, kind * cols : (kind + 1) * cols], weight)
    return total


def early_kernel(*refs):
    w_ref, rows_ref, out_ref = refs[0], refs[1], refs[-1]
    total = refs[2][...] if len(refs) == 4 else jnp.zeros(out_ref.shape, F32)
    out_ref[...] = add_parts(total, w_ref, rows_ref, 0)


def last_kernel(x_ref, g_ref, scale_ref, part_ref, own_ref, rows_ref, in_grad_ref, sums_ref):
    upstream = add_parts(part_ref[...], own_ref, rows_ref, rows_ref.shape[1] // 3)
    _, normal, inv_dev = norm_parts(x_ref[...].astype(F32), 1.0, 0.0)
    back, scale_sum, shift_sum = norm_back(upstream, normal, inv_dev, scale_ref[...])
    in_grad_ref[...] = (g_ref[...].astype(F32) + back).astype(BF)
    sums = [scale_sum[None, :], shift_sum[None, :], jnp.zeros((6, x_ref.shape[1]), F32)]
    sums = jnp.concatenate(sums, axis=0)

    @pl.when(pl.program_id(0) == 0)
    def _():
        sums_ref[...] = sums

    @pl.when(pl.program_id(0) > 0)
    def _():
        sums_ref[...] += sums


def early_rows(weight, rows_grad, *before):
    tokens, deep = rows_grad.shape
    width = weight.shape[0] * weight.shape[2]
    rows = min(512, tokens)
    block = (weight.shape[0], 3, weight.shape[2], deep // 3)
    tile = pl.BlockSpec((rows, width), lambda i: (i, 0))
    return call(
        early_kernel,
        2 * tokens * width * deep,
        2 * (tokens * deep + width * deep + 2 * tokens * width),
        grid=(tokens // rows,),
        in_specs=[
            pl.BlockSpec(block, lambda i: (0, 0, 0, 0)),
            pl.BlockSpec((rows, deep), lambda i: (i, 0)),
        ]
        + [tile for _ in before],
        out_specs=tile,
        out_shape=jax.ShapeDtypeStruct((tokens, width), F32),
    )(weight, rows_grad, *before)


def last_rows(x, branch_grad, scale, partial, own, own_rows):
    tokens, width = x.shape
    deep = own_rows.shape[1]
    rows = min(256, tokens)
    tile = pl.BlockSpec((rows, width), lambda i: (i, 0))
    return call(
        last_kernel,
        2 * tokens * width * deep,
        2 * (tokens * deep + width * deep + 5 * tokens * width),
        grid=(tokens // rows,),
        in_specs=[tile, tile, pl.BlockSpec((1, width), lambda i: (0, 0)), tile]
        + [pl.BlockSpec(own.shape, lambda i: (0, 0, 0, 0)), pl.BlockSpec((rows, deep), lambda i: (i, 0))],
        out_specs=[tile, pl.BlockSpec((8, width), lambda i: (0, 0))],
        out_shape=[
            jax.ShapeDtypeStruct((tokens, width), BF),
            jax.ShapeDtypeStruct((8, width), F32),
        ],
    )(x, branch_grad, scale, partial, own, own_rows)


def unit_kernel(t_ref, nt_ref, c_ref, sa_ref, sb_ref, *refs, chips, parts):
    dq_refs, own_refs, got_refs = refs[:parts], refs[parts : 2 * parts], refs[2 * parts : 3 * parts]
    keep_ref, send_ref, rows_out, sum_ref, acc_ref = refs[3 * parts :]
    kind = pl.program_id(0)
    cols = dq_refs[0].shape[1]
    added = lambda a, b: a[...].astype(F32) + b[...].astype(F32)

    @pl.when(kind == 0)
    def _():
        for u, dq in enumerate(dq_refs):
            rows_out[:, u * cols : (u + 1) * cols] = dq[...]

    @pl.when(kind == 1)
    def _():
        tables = (c_ref[...], sa_ref[...], sb_ref[...])
        for u, (own, got) in enumerate(zip(own_refs, got_refs)):
            total = added(own, got)
            for at in range(0, cols, LANES):
                turned = turn_back(total[:, at : at + LANES], *tables).astype(BF)
                rows_out[:, u * cols + at : u * cols + at + LANES] = turned

    @pl.when(kind == 2)
    def _():
        for u, (own, got) in enumerate(zip(own_refs, got_refs)):
            rows_out[:, u * cols : (u + 1) * cols] = added(own, got).astype(BF)

    rows = rows_out[...]
    acc_ref[...] = dot_nn(nt_ref[...], rows)
    piece = keep_ref.shape[1]
    for place in range(chips):
        for ref, which in ((keep_ref, place), (send_ref, chips + place)):
            at = pl.multiple_of(t_ref[which] * piece, piece)
            ref[place] = acc_ref[pl.ds(at, piece), :].astype(BF)
    sums = jnp.sum(rows.astype(F32), axis=0, keepdims=True)
    sum_ref[...] = jnp.broadcast_to(sums, sum_ref.shape)


def unit_grads(table, normed_t, tables, dqs, owns, gots):
    width, tokens = normed_t.shape
    parts = len(dqs)
    cols = dqs[0].shape[1]
    wide = parts * cols
    chips = table.shape[0] // 2
    piece = width // (2 * chips)
    rotary = pl.BlockSpec((tokens, LANES), lambda i, t: (0, 0))
    part = pl.BlockSpec((tokens, cols), lambda i, t: (0, 0))
    pair = pl.BlockSpec((None, tokens, cols), lambda i, t: (jnp.maximum(i - 1, 0), 0, 0))
    blocks = pl.BlockSpec((chips, None, piece, wide), lambda i, t: (0, i, 0, 0))
    return pl.pallas_call(
        functools.partial(unit_kernel, chips=chips, parts=parts),
        grid_spec=pltpu.PrefetchScalarGridSpec(
            num_scalar_prefetch=1,
            grid=(3,),
            in_specs=[pl.BlockSpec((width, tokens), lambda i, t: (0, 0))]
            + [rotary] * 3
            + [part] * parts
            + [pair] * (2 * parts),
            out_specs=[
                blocks,
                blocks,
                pl.BlockSpec((tokens, wide), lambda i, t: (0, i)),
                pl.BlockSpec((8, wide), lambda i, t: (0, i)),
            ],
            scratch_shapes=[pltpu.VMEM((width, wide), F32)],
        ),
        out_shape=[jax.ShapeDtypeStruct((chips, 3, piece, wide), BF)] * 2
        + [jax.ShapeDtypeStruct((tokens, 3 * wide), BF), jax.ShapeDtypeStruct((8, 3 * wide), F32)],
        compiler_params=pltpu.CompilerParams(vmem_limit_bytes=VMEM_BYTES),
        cost_estimate=pl.CostEstimate(
            flops=6 * tokens * width * wide,
            bytes_accessed=2 * (tokens * width + 8 * tokens * wide + 3 * width * wide),
            transcendentals=0,
        ),
    )(table, normed_t, *tables, *dqs, *owns, *gots)


def widen_kernel(t_ref, a_ref, b_ref, out_ref):
    count, piece, cols = a_ref.shape
    out_ref[:, :cols] = a_ref[...].reshape(out_ref.shape[0], cols).astype(F32)
    for place in range(count):
        rows = pl.ds(pl.multiple_of(t_ref[place] * piece, piece), piece)
        out_ref[rows, cols:] = b_ref[place].astype(F32)


def widen(table, unit_a, unit_b):
    n, _, piece, cols = unit_a.shape
    spec = pl.BlockSpec((n, None, piece, cols), lambda i, t: (0, i, 0, 0))
    return pl.pallas_call(
        widen_kernel,
        grid_spec=pltpu.PrefetchScalarGridSpec(
            num_scalar_prefetch=1,
            grid=(3,),
            in_specs=[spec, spec],
            out_specs=pl.BlockSpec((None, n * piece, 2 * cols), lambda i, t: (i, 0, 0)),
        ),
        out_shape=jax.ShapeDtypeStruct((3, n * piece, 2 * cols), F32),
        compiler_params=pltpu.CompilerParams(vmem_limit_bytes=VMEM_BYTES),
        cost_estimate=pl.CostEstimate(
            flops=0, bytes_accessed=36 * n * piece * cols, transcendentals=0
        ),
    )(table, unit_a, unit_b)


def split_kernel(t_ref, own_m, own_f, oth_m, oth_f, got_om, got_of, got_tm, got_tf, ka, kb, send, *, last):
    total = lambda a, b: (a[...].astype(F32) + b[...].astype(F32)).astype(BF)
    by_y = t_ref[last] == 0
    own_far, oth_me = total(own_f, got_of), total(oth_m, got_tm)
    ka[...] = total(own_m, got_om)
    kb[...] = jnp.where(by_y, own_far, oth_me)
    send[0] = jnp.where(by_y, oth_me, own_far)
    send[1] = total(oth_f, got_tf)


def first_split(table, own, oth, got_own, got_oth):
    chips, piece, cols = got_own.shape
    count = chips // 2
    own, oth = (g.reshape(chips, 2, piece, cols) for g in (own, oth))
    whole = lambda far: pl.BlockSpec(
        (None, None, piece, cols), lambda i, t: (t[far * count + i], t[2 * count], 0, 0)
    )
    part = lambda far: pl.BlockSpec((None, piece, cols), lambda i, t: (t[far * count + i], 0, 0))
    out = pl.BlockSpec((None, piece, cols), lambda i, t: (i, 0, 0))
    return pl.pallas_call(
        functools.partial(split_kernel, last=2 * count),
        grid_spec=pltpu.PrefetchScalarGridSpec(
            num_scalar_prefetch=1,
            grid=(count,),
            in_specs=[whole(0), whole(1)] * 2 + [part(0), part(1)] * 2,
            out_specs=[out, out, pl.BlockSpec((2, None, piece, cols), lambda i, t: (0, i, 0, 0))],
        ),
        out_shape=[jax.ShapeDtypeStruct((count, piece, cols), BF)] * 2
        + [jax.ShapeDtypeStruct((2, count, piece, cols), BF)],
        compiler_params=pltpu.CompilerParams(vmem_limit_bytes=VMEM_BYTES),
        cost_estimate=pl.CostEstimate(
            flops=4 * count * piece * cols, bytes_accessed=24 * count * piece * cols, transcendentals=0
        ),
    )(table, own, own, oth, oth, got_own, got_own, got_oth, got_oth)


class Paired:
    def __init__(self, n_dp):
        self.n_dp = n_dp
        self.me_dp = lax.axis_index("dp")
        self.me_y = lax.axis_index("tensor")
        self.core = self.me_dp % 2
        self.first = self.core * (SEQ // 2)
        chips = n_dp // 2
        levels = chips.bit_length() - 1
        places = np.arange(chips)
        far = sum(((places >> (levels - 1 - k)) & 1) << k for k in range(levels))
        chip = jnp.asarray(far, jnp.int32) ^ (self.me_dp // 2)
        self.blocks = jnp.concatenate([chip * 2 + self.core, chip * 2 + 1 - self.core]).astype(
            jnp.int32
        )

    def move(self, x, to):
        pairs = []
        for dp in range(self.n_dp):
            for y in range(2):
                a, b = to(dp, y)
                if (a, b) != (dp, y):
                    pairs.append((dp * 2 + y, a * 2 + b))
        return lax.ppermute(x, ("dp", "tensor"), pairs)

    def swap(self, rows):
        return self.move(rows, lambda dp, y: (dp - dp % 2 + y, dp % 2))

    def stays(self, rows, got):
        return jnp.where(self.core == self.me_y, rows, got)

    def over_y(self, x):
        return self.move(x, lambda dp, y: (dp, 1 - y))

    def over_core(self, x):
        return self.move(x, lambda dp, y: (dp ^ 1, y))

    def piece(self, own, axis=0):
        rows = own.shape[axis] // self.n_dp
        return lax.dynamic_slice_in_dim(own, self.me_dp * rows, rows, axis)

    def spread(self, got):
        return lax.all_gather(got, "dp", axis=0, tiled=True)

    def core_send(self, half):
        rows, cols = half.shape
        blocks = half.reshape(self.n_dp // 2, 2, rows // self.n_dp, cols)
        return lax.dynamic_index_in_dim(blocks, 1 - self.core, 1, keepdims=False)

    def over_chip(self, x, level):
        return self.move(x, lambda dp, y: (dp ^ (2 << level), y))

    def over_first(self, x):
        return self.move(x, lambda dp, y: (dp ^ 2, y) if dp % 2 else (dp, 1 - y))

    def over_second(self, x):
        return self.move(x, lambda dp, y: (dp, 1 - y) if dp % 2 else (dp ^ 2, y))

    def over_z(self, x, level):
        return self.move(x, lambda dp, y: (dp ^ (4 << level), y))

    def blocks_of(self, x_bit):
        count = self.n_dp // 4
        levels = count.bit_length() - 1
        z = self.me_dp // 4
        places = np.arange(count)
        far = sum(((places >> (levels - 1 - k)) & 1) << k for k in range(levels))
        return (jnp.asarray(far, jnp.int32) ^ z) * 2 + x_bit

    def table(self):
        x = (self.me_dp // 2) % 2
        me, far = self.blocks_of(x), self.blocks_of(1 - x)
        return jnp.concatenate([me, far, jnp.stack([self.core])]).astype(jnp.int32)

    def gather(self, block):
        return lax.all_gather(block[0], "dp", axis=0, tiled=True)

    def reduce_vectors(self, both, own, other):
        k, width = both.shape
        both = both.reshape(k, 2, width // 2)
        take = lambda b: lax.dynamic_index_in_dim(both, b, 1, keepdims=False).reshape(-1)
        mine = jnp.concatenate([take(self.me_y), own]).reshape(-1, LANES)
        theirs = jnp.concatenate([take(1 - self.me_y), other]).reshape(-1, LANES)
        total = jnp.stack([mine, theirs])
        total = total + self.over_core(total)
        for level in range((self.n_dp // 2).bit_length() - 1):
            total = total + self.over_chip(total, level)
        total = (total[0] + self.over_y(total[1])).reshape(-1)
        return total[: k * width // 2].reshape(k, width // 2), total[k * width // 2 :]


class Spread:
    def __init__(self, tokens):
        self.first = lax.axis_index("tensor") * tokens

    def swap_rows(self, rows):
        return rows

    def keys(self, kv):
        return [lax.all_gather(kv, "tensor", axis=0, tiled=True)]

    def keys_back(self, grads):
        return lax.psum_scatter(grads, "tensor", scatter_dimension=1, tiled=True)


def block_step(
    move,
    block_in,
    ln1_scale,
    ln1_shift,
    qkv_ws,
    qkv_bs,
    out_ws,
    out_bias,
    ln2_scale,
    ln2_shift,
    up_ws,
    up_bs,
    down_ws,
    down_bias,
    out_grad,
):
    f32 = lambda v: v.astype(F32)
    tokens = block_in.shape[0]
    tables = rotary_tables(move.first, tokens)
    ln1_gain, ln2_gain = f32(ln1_scale), f32(ln2_scale)
    block_in = move.swap_rows(block_in)
    x_rows = f32(block_in)
    normed1, normal1, inv_one = norm_parts(x_rows, ln1_gain, f32(ln1_shift))
    normed1 = normed1.astype(BF)
    queries, keys, outs, logs = [], [], [], []
    for weight, bias in zip(qkv_ws, qkv_bs):
        split = weight.reshape(1, weight.shape[0], 3, -1).transpose(0, 2, 1, 3)
        q, kv = qkv_rows(normed1, split, f32(bias)[None, :], tables)
        queries.append(q)
        keys.append(move.keys(kv))
    for q, kvs in zip(queries, keys):
        out, log = attend(q, kvs)
        outs.append(out)
        logs.append(log)
    grad_low = move.swap_rows(out_grad)
    grad_rows = f32(grad_low)
    branch_one = sum(dot_nn(o, w) for o, w in zip(outs, out_ws)) + f32(out_bias)
    resid = x_rows + branch_one
    normed2, normal2, inv_two = norm_parts(resid, ln2_gain, f32(ln2_shift))
    normed2 = normed2.astype(BF)
    acts, slopes = [], []
    for weight, bias in zip(up_ws, up_bs):
        acted, slope = up_rows(normed2, weight, f32(bias)[None, :])
        acts.append(acted)
        slopes.append(slope)
    branch_two = sum(dot_nn(a, w) for a, w in zip(acts, down_ws)) + f32(down_bias)
    block_out = move.swap_rows((resid + branch_two).astype(BF))
    down_bias_grad = jnp.sum(grad_rows, 0)
    down_grads = [dot_tn(a, grad_low).astype(BF) for a in acts]
    hidden_gs, up_b_grads = [], []
    for down, slope in zip(down_ws, slopes):
        hg, total = hidden_grads(grad_low, (down[None], 0), slope)
        hidden_gs.append(hg)
        up_b_grads.append(total[0])
    up_grads = [dot_tn(normed2, hg).astype(BF) for hg in hidden_gs]
    normed2_grad = sum(dot_nt(hg, w) for hg, w in zip(hidden_gs, up_ws))
    resid_part, ln2_scale_grad, ln2_shift_grad = norm_back(normed2_grad, normal2, inv_two, ln2_gain)
    resid_grad = grad_rows + resid_part
    branch_grad = resid_grad.astype(BF)
    out_bias_grad = jnp.sum(branch_grad, 0, dtype=F32)
    out_w_grads = [dot_tn(o, branch_grad).astype(BF) for o in outs]
    qkv_w_grads, qkv_b_grads = [], []
    normed1_grad = 0.0
    for q, kvs, out, log, out_w, qkv_w in zip(queries, keys, outs, logs, out_ws, qkv_ws):
        out_g = dot_nt(branch_grad, out_w).astype(BF)
        dq, (dkv,) = attend_back(q, out_g, out, log, kvs, tables)
        dk, dv = move.keys_back(dkv)
        dk = key_sum(dk, jnp.zeros_like(dk), tables)
        qkv_g = jnp.concatenate([dq, dk, dv], axis=1)
        qkv_w_grads.append(dot_tn(normed1, qkv_g).astype(BF))
        qkv_b_grads.append(jnp.sum(qkv_g, 0, dtype=F32))
        normed1_grad = normed1_grad + dot_nt(qkv_g, qkv_w)
    input_part, ln1_scale_grad, ln1_shift_grad = norm_back(normed1_grad, normal1, inv_one, ln1_gain)
    in_grad = move.swap_rows((resid_grad + input_part).astype(BF))
    vectors = [
        ln1_scale_grad,
        ln1_shift_grad,
        out_bias_grad,
        ln2_scale_grad,
        ln2_shift_grad,
        down_bias_grad,
    ]
    return (
        block_out,
        in_grad,
        vectors,
        (qkv_w_grads, out_w_grads, up_grads, down_grads),
        (qkv_b_grads, up_b_grads),
    )


class Reduction:
    def __init__(self, move, table, own, oth):
        self.move, self.table = move, table
        self.grads = own, oth
        self.sends = [move.core_send(g) for g in (own, oth)]
        self.at = 0

    def start(self):
        at = self.at
        if at == 0:
            go = self.move.over_core
        elif at == 1:
            go = self.move.over_first
        elif at == 2:
            go = self.move.over_second
        else:
            go = functools.partial(self.move.over_z, level=at - 3)
        return [go(x) for x in self.sends]

    def take(self, got):
        at, self.at = self.at, self.at + 1
        if at == 0:
            ka, kb, send = first_split(self.table, *self.grads, *got)
            self.keep, self.sends = (ka, kb), [send]
        elif at == 1:
            self.sends = [self.keep[1] + got[0][1]]
            self.keep = self.keep[0] + got[0][0]
        else:
            total = self.keep + got[0]
            half = total.shape[0] // 2
            if half:
                self.keep, self.sends = total[:half], [total[half:]]
            else:
                self.done = total

    @property
    def last(self):
        return 2 + (self.move.n_dp // 4).bit_length() - 1


def beside(compute, inputs, *steps, late=()):
    sends = [s.sends if isinstance(s, Reduction) else s[1] for s in steps]
    inputs, sends, late_sends = tie(inputs, sends, [s[1] for s in late])
    got = []
    for s, x in zip(steps, sends):
        if isinstance(s, Reduction):
            s.sends = x
            got.append(s.start())
        else:
            got.append(s[0](x))
    later = [s[0](x) for s, x in zip(late, late_sends)]
    out = compute(*inputs)
    out, got = tie(out, got)
    moved = []
    for s, x in zip(steps, got):
        if isinstance(s, Reduction):
            s.take(x)
        else:
            moved.append(x)
    return out, moved + later


def paired_device(n_dp, *args):
    (block_in, ln1_scale, ln1_shift, qkv_weight, qkv_bias, out_weight, out_bias) = args[:7]
    (ln2_scale, ln2_shift, up_weight, up_bias, down_weight, down_bias, out_grad) = args[7:]
    move = Paired(n_dp)
    row = lambda v: v.astype(F32)[None, :]
    width, _, part = qkv_weight.shape
    tokens = block_in.shape[0]
    pairs = part // LANES
    half = pairs // 2
    cols = half * LANES
    table = move.table()
    low_product = lambda a, b: dot_tn(a, b).astype(BF)

    block_got = move.swap(block_in)
    qkv_own = jnp.transpose(qkv_weight, (1, 0, 2))
    small = jnp.concatenate([qkv_bias.reshape(3 * part), up_bias])
    out_piece = move.piece(out_weight)
    out_piece = jnp.concatenate([out_piece[:, at : at + part] for at in range(0, width, part)])
    first_piece = jnp.concatenate([move.piece(qkv_own, 1), out_piece[None]])
    first_got = move.over_y(first_piece)
    small_got = move.over_y(small)
    qkv_bs = [row(v[: 3 * part]) for v in (small, small_got)]
    up_bs = [row(v[3 * part :]) for v in (small, small_got)]
    tables = rotary_tables(move.first, tokens)
    qkv_own = qkv_own[None]
    qkv_oth = lax.all_gather(first_got, "dp")
    rest = [move.piece(w) for w in (up_weight, down_weight)]
    stay = jnp.stack([(move.core == move.me_y).astype(jnp.int32)])
    block_in, normed1, normed1_t = norm_rows(
        stay, block_in, block_got, row(ln1_scale), row(ln1_shift)
    )
    (q_own, kv_own), (rest,) = beside(
        lambda n: qkv_rows(n, qkv_own, qkv_bs[0], tables),
        (normed1,),
        (lambda ws: [move.over_y(w) for w in ws], rest),
    )
    kvs_own = [kv_own, move.over_core(kv_own)]
    up_got, down_got = (move.gather(got[None]) for got in rest)
    (out_a, log_a), _ = beside(lambda q, kvs: attend(q, kvs, 0, half), (q_own, kvs_own))
    qkv_oth, out_a, out_grad = tie(qkv_oth, out_a, out_grad)
    q_oth, kv_oth = qkv_rows(normed1, qkv_oth, qkv_bs[1], tables)
    (out_b, log_b), (kv_got, grad_got) = beside(
        lambda q, kvs: attend(q, kvs, half, half),
        (q_own, kvs_own),
        (move.over_core, kv_oth),
        late=[(move.swap, out_grad)],
    )
    kvs_oth = [kv_oth, kv_got]
    (out_oth, log_oth), _ = beside(attend, (q_oth, kvs_oth))
    grad_low = move.stays(out_grad, grad_got)
    out_got = qkv_oth[:, 3].reshape(n_dp, width // part, part // n_dp, part)
    out_got = out_got.transpose(0, 2, 1, 3).reshape(part, width)
    up_ws = [up_weight, up_got]
    down_ws = [(w[None], 0) for w in (down_weight, down_got)]
    outs = [out_a, out_b, out_oth]
    out_ws = [out_weight[:cols], out_weight[cols:], out_got]

    resid, normed2, normed2_t = project_rows(
        block_in, row(out_bias), row(ln2_scale), row(ln2_shift), outs, out_ws
    )
    acts, slopes = zip(*[up_rows(normed2, w, b) for w, b in zip(up_ws, up_bs)])
    block_out = down_rows(resid, row(down_bias), acts, down_ws)
    down_grads, (block_got,) = beside(
        lambda xs, g: [low_product(a, g) for a in xs],
        (acts, grad_low),
        late=[(move.swap, block_out)],
    )
    down = Reduction(move, table, *down_grads)
    (hg_own, up_b_own), _ = beside(
        lambda g, slope: hidden_grads(g, down_ws[0], slope), (grad_low, slopes[0]), down
    )

    def others(g, hg_own):
        hg_oth, up_b_oth = hidden_grads(g, down_ws[1], slopes[1])
        return hg_oth, up_b_oth, [dot_nn(normed2_t, h).astype(BF) for h in (hg_own, hg_oth)]

    (hg_oth, up_b_oth, up_grads), _ = beside(others, (grad_low, hg_own), down)
    up = Reduction(move, table, *up_grads)
    (branch_grad, sums_two), _ = beside(
        lambda *hs: middle_rows(resid, grad_low, row(ln2_scale), hs, up_ws), (hg_own, hg_oth), up, down
    )

    def projected(outs, g):
        own = jnp.concatenate([low_product(o, g) for o in outs[:2]])
        out_w_grads = own, low_product(outs[2], g)
        return out_w_grads, [dot_nt(g, w).astype(BF) for w in out_ws]

    (out_w_grads, out_gs), _ = beside(projected, (outs, branch_grad), down)
    out_gs, block_got = tie(out_gs, block_got)
    proj = Reduction(move, table, *out_w_grads)

    def back(which):
        own = which >= 2
        lo = (which % 2) * half
        q, kvs = (q_own, kvs_own) if own else (q_oth, kvs_oth)
        out, log, grad = (
            (outs[which - 2], (log_a, log_b)[which - 2], out_gs[which - 2])
            if own
            else (out_oth, log_oth, out_gs[2])
        )
        inputs = q, grad, out, log, kvs
        at = 0 if own else lo
        return lambda *xs: attend_back(*xs, tables, lo, half, at), inputs

    def keys_of(x):
        return move.over_core, x[1][1]

    def unit(xs, gots):
        return unit_grads(
            move.blocks, normed1_t, tables, [x[0] for x in xs], [x[1][0] for x in xs], gots
        )

    over_x = functools.partial(move.over_chip, level=0)
    others_z = (8, 4, 12)

    def over_z(parts):
        return [
            move.move(p, lambda dp, y, far=far: (dp ^ far, y)) for p, far in zip(parts, others_z)
        ]

    def z_parts(total):
        return total[:1], [total[n : n + 1] for n in range(1, 4)]

    def halves(total):
        return total[: total.shape[0] // 2], total[total.shape[0] // 2 :]

    oth_a, _ = beside(*back(0), up, down, proj)
    down_block, oth_a = tie(down.done, oth_a)
    down_all = move.gather(down_block)
    oth_b, (got_a,) = beside(*back(1), keys_of(oth_a), up, proj)
    own_a, (got_b,) = beside(*back(2), keys_of(oth_b), up, proj)
    (keep_oth, send, rows_oth, bias_oth), (key_got,) = beside(
        unit, ((oth_a, oth_b), (got_a, got_b)), keys_of(own_a), up, proj
    )
    (keep_a, send_a, rows_a, bias_a), (core_got,) = beside(
        unit, ((own_a,), (key_got,)), (move.over_core, send), proj
    )
    up_block, keep_a, down_all = tie(up.done, keep_a, down_all)
    up_all = move.gather(up_block)
    y_sends = [keep_oth[..., at : at + cols] + core_got[..., at : at + cols] for at in (0, cols)]
    own_b, (core_got_a, y_got_a, y_got_b) = beside(
        *back(3), (move.over_core, send_a), late=[(move.over_y, y) for y in y_sends]
    )
    y_got_a, own_b = tie(y_got_a, own_b)
    keep_a, send_a = halves(keep_a + core_got_a + y_got_a)
    partial, (key_got, a_got) = beside(
        early_rows, (qkv_oth, rows_oth), keys_of(own_b), late=[(over_x, send_a)]
    )
    (keep_b, send_b, rows_b, bias_b), _ = beside(unit, ((own_b,), (key_got,)))
    keep_b, a_got, y_got_b = tie(keep_b, a_got, y_got_b)
    keep_a, send_a = z_parts(keep_a + a_got)
    partial, (core_got, a_got) = beside(
        early_rows, (qkv_own, rows_a, partial), (move.over_core, send_b), (over_z, send_a)
    )
    total_a = keep_a + sum(a_got)
    keep_b, send_b = halves(keep_b + core_got + y_got_b)
    up_all, partial, total_a = tie(up_all, partial, total_a)
    unit_a = lax.all_gather(
        jnp.concatenate([total_a[0], proj.done.reshape(-1, *total_a.shape[2:])]), "dp"
    )
    f32 = lambda v: v.astype(F32)
    (in_grad, sums_one), (b_got,) = beside(
        lambda *xs: last_rows(block_in, branch_grad, row(ln1_scale), *xs),
        (partial, qkv_own, rows_b),
        (over_x, send_b),
    )
    in_grad, block_got, down_all, up_all = tie(in_grad, block_got, down_all, up_all)
    in_grad_got = move.swap(in_grad)
    keep_b, send_b = z_parts(keep_b + b_got)
    b_got = over_z(send_b)
    total_b = keep_b + sum(b_got)
    b_got = over_z([total_b] * 3)
    b_got[0], down_all, up_all = tie(b_got[0], down_all, up_all)
    down_g, up_g = f32(down_all), f32(up_all)
    b_got, down_g, up_g = tie(b_got, down_g, up_g)
    total_b = jnp.concatenate([total_b] + b_got)
    b_got = over_x(total_b)
    block_out = move.stays(block_out, block_got)
    b_got, block_out = tie(b_got, block_out)
    total_b = jnp.concatenate([total_b, b_got])
    total_b = jnp.concatenate([total_b, move.over_core(total_b)])
    out_g = f32(unit_a[:, 3:].reshape(part, width))
    qkv_g = jnp.transpose(widen(move.blocks, unit_a, total_b), (1, 0, 2))
    side = lambda a, b: jnp.concatenate([a.reshape(3, cols), b.reshape(3, cols)], axis=1).reshape(-1)
    vec, flat = move.reduce_vectors(
        jnp.concatenate([sums_one[:2], sums_two[:4]]),
        jnp.concatenate([side(bias_a[0], bias_b[0]), up_b_own[0]]),
        jnp.concatenate([bias_oth[0], up_b_oth[0]]),
    )
    return (
        block_out,
        move.stays(in_grad, in_grad_got),
        vec[0],
        vec[1],
        qkv_g,
        flat[: 3 * part].reshape(3, part),
        out_g,
        vec[4],
        vec[2],
        vec[3],
        up_g,
        flat[3 * part :],
        down_g,
        vec[5],
    )


def spread_device(*args):
    (block_in, ln1_scale, ln1_shift, qkv_weight, qkv_bias, out_weight, out_bias) = args[:7]
    (ln2_scale, ln2_shift, up_weight, up_bias, down_weight, down_bias, out_grad) = args[7:]
    gather = lambda w, axis: lax.all_gather(w, "tensor", axis=axis, tiled=True)
    scatter = lambda g, axis: lax.psum(
        lax.psum_scatter(g, "tensor", scatter_dimension=axis, tiled=True), "dp"
    ).astype(F32)
    width = qkv_weight.shape[0]
    qkv_all = gather(qkv_weight, 2)
    full = qkv_all.shape[2]
    out = block_step(
        Spread(block_in.shape[0]),
        block_in,
        ln1_scale,
        ln1_shift,
        [qkv_all.reshape(width, 3 * full)],
        [gather(qkv_bias, 1).reshape(3 * full)],
        [gather(out_weight, 0)],
        out_bias,
        ln2_scale,
        ln2_shift,
        [gather(up_weight, 1)],
        [gather(up_bias, 0)],
        [gather(down_weight, 0)],
        down_bias,
        out_grad,
    )
    block_out, in_grad, vectors, weight_grads, (qkv_b, up_b) = out
    ((qkv_g,), (out_g,), (up_g,), (down_g,)) = weight_grads
    vec = scatter(jnp.stack(vectors), 1)
    return (
        block_out,
        in_grad,
        vec[0],
        vec[1],
        scatter(qkv_g.reshape(width, 3, full), 2),
        scatter(qkv_b[0].reshape(3, full), 1),
        scatter(out_g, 0),
        vec[2],
        vec[3],
        vec[4],
        scatter(up_g, 1),
        scatter(up_b[0], 0),
        scatter(down_g, 0),
        vec[5],
    )


def solution(mesh):
    n_dp, n_tensor = mesh.shape["dp"], mesh.shape["tensor"]
    rows = P(("dp", "tensor"), None)
    vector = P("tensor")
    placed = (
        rows,
        P(),
        P(),
        P(None, None, "tensor"),
        P(None, "tensor"),
        P("tensor", None),
        P(),
        P(),
        P(),
        P(None, "tensor"),
        vector,
        P("tensor", None),
        P(),
        rows,
    )
    paired = n_tensor == 2 and n_dp == 16
    return jax.shard_map(
        functools.partial(paired_device, n_dp) if paired else spread_device,
        mesh=mesh,
        in_specs=placed,
        out_specs=(
            rows,
            rows,
            vector,
            vector,
            P(None, None, "tensor"),
            P(None, "tensor"),
            P("tensor", None),
            vector,
            vector,
            vector,
            P(None, "tensor"),
            vector,
            P("tensor", None),
            vector,
        ),
        check_vma=False,
    )
```

```python
import functools
import math

import jax
import jax.numpy as jnp
import numpy as np
from jax import lax
from jax.experimental import pallas as pl
from jax.experimental.pallas import tpu as pltpu
from jax.sharding import PartitionSpec as P

HD = 64
GH = 16
GW = 16
SEQ = 2048
EPS = 1e-06
LANES = 128
ROT = 2 * (HD // 3 // 2)
HALF_ROT = ROT // 2
LOG2E = math.log2(math.e)
SCALE = 1.0 / math.sqrt(HD)
BF = jnp.bfloat16
F32 = jnp.float32
VMEM_BYTES = 56 << 20


def dot_nt(left, right):
    return lax.dot_general(left, right, (((1,), (1,)), ((), ())), preferred_element_type=F32)


def dot_nn(left, right):
    return lax.dot_general(left, right, (((1,), (0,)), ((), ())), preferred_element_type=F32)


def dot_tn(left, right):
    return lax.dot_general(left, right, (((0,), (0,)), ((), ())), preferred_element_type=F32)


def call(kernel, flops, moved, exps=0, **kw):
    return pl.pallas_call(
        kernel,
        compiler_params=pltpu.CompilerParams(vmem_limit_bytes=VMEM_BYTES),
        cost_estimate=pl.CostEstimate(flops=flops, bytes_accessed=moved, transcendentals=exps),
        **kw,
    )


def rotary_tables(first, count):
    lane = np.arange(LANES) % HD
    axis = lane // ROT
    inside = lane % ROT
    freq = np.float32(10000.0) ** (
        -(inside % HALF_ROT).astype(np.float32) / np.float32(HALF_ROT)
    )
    turned = axis < 3
    early = turned & (inside < HALF_ROT)
    late = turned & (inside >= HALF_ROT)
    index = first + jnp.arange(count, dtype=jnp.int32)[:, None]
    places = (index // (GH * GW), index // GW % GH, index % GW)
    place = jnp.where(axis == 0, places[0], jnp.where(axis == 1, places[1], places[2]))
    angle = place.astype(F32) * freq.astype(np.float32)[None, :]
    cos = jnp.where(turned, jnp.cos(angle), 1.0)
    sin = jnp.sin(angle)
    return cos, jnp.where(early, -sin, 0.0), jnp.where(late, sin, 0.0)


def turn(x, cos, sin_a, sin_b):
    return (
        x * cos
        + pltpu.roll(x, LANES - HALF_ROT, 1) * sin_a
        + pltpu.roll(x, HALF_ROT, 1) * sin_b
    )


def turn_back(g, cos, sin_a, sin_b):
    return (
        g * cos
        + pltpu.roll(g * sin_b, LANES - HALF_ROT, 1)
        + pltpu.roll(g * sin_a, HALF_ROT, 1)
    )


def norm_kernel(stay_ref, x_ref, got_ref, scale_ref, shift_ref, rows_ref, n_ref, nt_ref):
    rows = jnp.where(stay_ref[0] == 1, x_ref[...].astype(F32), got_ref[...].astype(F32))
    rows_ref[...] = rows.astype(BF)
    normed, _, _ = norm_parts(rows, scale_ref[...], shift_ref[...])
    n_ref[...] = normed.astype(BF)
    nt_ref[...] = normed.T.astype(BF)


def norm_rows(stay, x, got, scale, shift):
    tokens, width = x.shape
    rows = min(256, tokens)
    vector = pl.BlockSpec((1, width), lambda i, t: (0, 0))
    tile = pl.BlockSpec((rows, width), lambda i, t: (i, 0))
    return pl.pallas_call(
        norm_kernel,
        grid_spec=pltpu.PrefetchScalarGridSpec(
            num_scalar_prefetch=1,
            grid=(tokens // rows,),
            in_specs=[tile, tile, vector, vector],
            out_specs=[tile, tile, pl.BlockSpec((width, rows), lambda i, t: (0, i))],
        ),
        out_shape=[jax.ShapeDtypeStruct((tokens, width), BF)] * 2
        + [jax.ShapeDtypeStruct((width, tokens), BF)],
        compiler_params=pltpu.CompilerParams(vmem_limit_bytes=VMEM_BYTES),
        cost_estimate=pl.CostEstimate(
            flops=10 * tokens * width, bytes_accessed=10 * tokens * width, transcendentals=0
        ),
    )(stay, x, got, scale, shift)


def qkv_kernel(n_ref, w_ref, b_ref, c_ref, sa_ref, sb_ref, q_ref, kv_ref, *, q_steps):
    step = pl.program_id(0)
    weight = w_ref[...].reshape(n_ref.shape[1], w_ref.shape[-1])
    rows = dot_nn(n_ref[...], weight) + b_ref[...]
    wide = rows.shape[1]

    def turned():
        tables = (c_ref[...], sa_ref[...], sb_ref[...])
        parts = [
            turn(rows[:, at : at + LANES], *tables).astype(BF) for at in range(0, wide, LANES)
        ]
        return jnp.concatenate(parts, axis=1)

    @pl.when(step < q_steps)
    def _():
        q_ref[...] = turned()

    @pl.when((step >= q_steps) & (step < 2 * q_steps))
    def _():
        kv_ref[...] = turned()

    @pl.when(step >= 2 * q_steps)
    def _():
        kv_ref[...] = rows.astype(BF)


def qkv_rows(normed, weight, bias, tables):
    tokens, width = normed.shape
    groups, _, deep, cols = weight.shape
    tile = next(t for t in (512, 256, LANES) if cols % t == 0)
    q_steps = cols // tile
    whole = lambda n: (0, 0)
    return call(
        functools.partial(qkv_kernel, q_steps=q_steps),
        2 * tokens * width * 3 * cols,
        2 * (tokens * width + width * 3 * cols + tokens * 3 * cols),
        grid=(3 * q_steps,),
        in_specs=[
            pl.BlockSpec((tokens, width), whole),
            pl.BlockSpec((groups, None, deep, tile), lambda n: (0, n // q_steps, 0, n % q_steps)),
            pl.BlockSpec((1, tile), lambda n: (0, n)),
        ]
        + [pl.BlockSpec((tokens, LANES), whole)] * 3,
        out_specs=[
            pl.BlockSpec((tokens, tile), lambda n: (0, jnp.minimum(n, q_steps - 1))),
            pl.BlockSpec((tokens, tile), lambda n: (0, jnp.maximum(n - q_steps, 0))),
        ],
        out_shape=[
            jax.ShapeDtypeStruct((tokens, cols), BF),
            jax.ShapeDtypeStruct((tokens, 2 * cols), BF),
        ],
    )(normed, weight, bias, *tables)


def attend_kernel(*refs, sources, rows_at):
    q_ref = refs[0]
    k_refs = refs[1 : 1 + sources]
    v_refs = refs[1 + sources : 1 + 2 * sources]
    o_ref, lse_ref = refs[1 + 2 * sources : 3 + 2 * sources]
    wide_refs = refs[3 + 2 * sources :]
    lane = lax.broadcasted_iota(jnp.int32, (1, LANES), 1)
    for v, wide in zip(v_refs, wide_refs):
        wide[:, :LANES] = v[...]
        wide[:, LANES:] = jnp.ones_like(v)

    def scores_of(q, head):
        q_head = jnp.where((lane // HD) == head, q, jnp.zeros_like(q))
        return [dot_nt(q_head, k[...]) for k in k_refs]

    def result(scores):
        peak = functools.reduce(
            jnp.maximum, [jnp.max(s, axis=1, keepdims=True) for s in scores]
        )
        weights = [jnp.exp2((s - peak) * (SCALE * LOG2E)).astype(BF) for s in scores]
        both = sum(dot_nn(w, v[...]) for w, v in zip(weights, wide_refs))
        total = both[:, LANES : LANES + 1]
        return both[:, :LANES] / both[:, LANES:], peak * (SCALE * LOG2E) + jnp.log2(total)

    for first in range(0, q_ref.shape[0], rows_at):
        rows = slice(first, first + rows_at)
        q = q_ref[rows, :]
        (out_0, log_0), (out_1, log_1) = [result(s) for s in [scores_of(q, h) for h in range(2)]]
        early = lane < HD
        o_ref[rows, :] = jnp.where(early, out_0, out_1).astype(BF)
        logs = jnp.where(early, log_0, log_1).T
        lse_ref[0, 0:1, rows] = logs[0:1]
        lse_ref[0, 1:2, rows] = logs[HD : HD + 1]


def attend(q, kvs, skip=0, pairs=None):
    tokens, cols = q.shape
    all_pairs = cols // LANES
    pairs = pairs or all_pairs
    cols = pairs * LANES
    keys = sum(kv.shape[0] for kv in kvs)
    q_spec = pl.BlockSpec((tokens, LANES), lambda i: (0, skip + i))
    k_specs = [pl.BlockSpec((kv.shape[0], LANES), lambda i: (0, skip + i)) for kv in kvs]
    v_specs = [
        pl.BlockSpec((kv.shape[0], LANES), lambda i: (0, all_pairs + skip + i)) for kv in kvs
    ]
    return call(
        functools.partial(attend_kernel, sources=len(kvs), rows_at=min(512, tokens)),
        4 * 4 * tokens * keys * cols,
        2 * (2 * tokens * cols + 2 * keys * cols),
        tokens * keys * 2 * pairs,
        grid=(pairs,),
        in_specs=[q_spec] + k_specs + v_specs,
        out_specs=[
            pl.BlockSpec((tokens, LANES), lambda i: (0, i)),
            pl.BlockSpec((1, 2, tokens), lambda i: (i, 0, 0)),
        ],
        out_shape=[
            jax.ShapeDtypeStruct((tokens, cols), BF),
            jax.ShapeDtypeStruct((pairs, 2, tokens), F32),
        ],
        scratch_shapes=[pltpu.VMEM((kv.shape[0], 2 * LANES), BF) for kv in kvs],
    )(q, *kvs, *kvs)


def attend_back_kernel(*refs, sources, keys_at, queries_at):
    q_ref, do_ref, o_ref, lse_ref, c_ref, sa_ref, sb_ref = refs[:7]
    at = 7
    k_refs = refs[at : at + sources]
    v_refs = refs[at + sources : at + 2 * sources]
    at += 2 * sources
    dq_ref = refs[at]
    dkv_refs = refs[at + 1 : at + 1 + sources]
    dq_acc, centre = refs[at + 1 + sources :]
    lane = lax.broadcasted_iota(jnp.int32, (1, LANES), 1)
    tokens = q_ref.shape[0]
    product = (do_ref[...].astype(F32) * o_ref[...].astype(F32)).T
    for head in range(2):
        centre[head : head + 1, :] = jnp.sum(
            product[head * HD : head * HD + HD], axis=0, keepdims=True
        )
    dq_acc[...] = jnp.zeros_like(dq_acc)
    for k_ref, v_ref, dkv_ref in zip(k_refs, v_refs, dkv_refs):

        def body(j, carry):
            rows = pl.ds(pl.multiple_of(j * keys_at, keys_at), keys_at)
            k, v = k_ref[rows, :], v_ref[rows, :]
            k_t = k.astype(F32).T.astype(BF)
            dv = jnp.zeros((keys_at, LANES), F32)
            dk = jnp.zeros((keys_at, LANES), F32)

            def products(cut, head):
                mine = (lane // HD) == head
                q, do = q_ref[cut, :], do_ref[cut, :]
                q_head = jnp.where(mine, q, jnp.zeros_like(q))
                do_head = jnp.where(mine, do, jnp.zeros_like(do))
                return q_head, do_head, dot_nt(k, q_head), dot_nt(v, do_head)

            steps = [
                (slice(first, first + queries_at), head)
                for first in range(0, tokens, queries_at)
                for head in range(2)
            ]
            later = products(*steps[0])
            for at, (cut, head) in enumerate(steps):
                q_head, do_head, scores, share_grad = later
                if at + 1 < len(steps):
                    later = products(*steps[at + 1])
                shares = jnp.exp2(scores * (SCALE * LOG2E) - lse_ref[0, head : head + 1, cut])
                score_grad = (shares * (share_grad - centre[head : head + 1, cut])).astype(BF)
                dv += dot_nn(shares.astype(BF), do_head)
                dk += dot_nn(score_grad, q_head)
                part = slice(head * HD, head * HD + HD)
                dq_acc[part, cut] += dot_nn(k_t[part], score_grad)
            dkv_ref[0, rows, :] = (dk * SCALE).astype(BF)
            dkv_ref[1, rows, :] = dv.astype(BF)
            return carry

        lax.fori_loop(0, k_ref.shape[0] // keys_at, body, 0)
    dq = (dq_acc[...] * SCALE).T
    dq_ref[...] = turn_back(dq, c_ref[...], sa_ref[...], sb_ref[...]).astype(BF)


def attend_back(q, out_grad, out, lse, kvs, tables, skip=0, pairs=None, at=0):
    tokens, cols = q.shape
    all_pairs = cols // LANES
    pairs = pairs or all_pairs
    cols = pairs * LANES
    keys = sum(kv.shape[0] for kv in kvs)
    q_spec = pl.BlockSpec((tokens, LANES), lambda i: (0, skip + i))
    o_spec = pl.BlockSpec((tokens, LANES), lambda i: (0, at + i))
    k_specs = [pl.BlockSpec((kv.shape[0], LANES), lambda i: (0, skip + i)) for kv in kvs]
    v_specs = [
        pl.BlockSpec((kv.shape[0], LANES), lambda i: (0, all_pairs + skip + i)) for kv in kvs
    ]
    dq_spec = pl.BlockSpec((tokens, LANES), lambda i: (0, i))
    dkv_specs = [pl.BlockSpec((2, kv.shape[0], LANES), lambda i: (0, 0, i)) for kv in kvs]
    table = pl.BlockSpec((tokens, LANES), lambda i: (0, 0))
    outs = call(
        functools.partial(
            attend_back_kernel, sources=len(kvs), keys_at=1024, queries_at=min(256, tokens)
        ),
        10 * 4 * tokens * keys * cols,
        2 * (4 * tokens * cols + 4 * keys * cols),
        tokens * keys * 2 * pairs,
        grid=(pairs,),
        in_specs=[q_spec, o_spec, o_spec]
        + [pl.BlockSpec((1, 2, tokens), lambda i: (at + i, 0, 0))]
        + [table] * 3
        + k_specs
        + v_specs,
        out_specs=[dq_spec] + dkv_specs,
        out_shape=[jax.ShapeDtypeStruct((tokens, cols), BF)]
        + [jax.ShapeDtypeStruct((2, kv.shape[0], cols), BF) for kv in kvs],
        scratch_shapes=[pltpu.VMEM((LANES, tokens), F32), pltpu.VMEM((2, tokens), F32)],
    )(q, out_grad, out, lse, *tables, *kvs, *kvs)
    return outs[0], outs[1:]


def key_sum_kernel(own_ref, got_ref, c_ref, sa_ref, sb_ref, dk_ref):
    total = own_ref[...].astype(F32) + got_ref[...].astype(F32)
    dk_ref[...] = turn_back(total, c_ref[...], sa_ref[...], sb_ref[...]).astype(BF)


def key_sum(own, got, tables):
    tokens, cols = own.shape
    spec = pl.BlockSpec((tokens, LANES), lambda i: (0, i))
    table = pl.BlockSpec((tokens, LANES), lambda i: (0, 0))
    return call(
        key_sum_kernel,
        12 * tokens * cols,
        6 * tokens * cols,
        grid=(cols // LANES,),
        in_specs=[spec, spec] + [table] * 3,
        out_specs=spec,
        out_shape=jax.ShapeDtypeStruct((tokens, cols), BF),
    )(own, got, *tables)


def gelu_parts(hidden):
    cdf = 0.5 + 0.5 * lax.erf(hidden * (1.0 / math.sqrt(2.0)))
    bell = jnp.exp2(hidden * hidden * (-0.5 * LOG2E))
    return hidden * cdf, cdf + hidden * (1.0 / math.sqrt(2.0 * math.pi)) * bell


def up_kernel(n_ref, w_ref, b_ref, acted_ref, slope_ref):
    hidden = dot_nn(n_ref[...], w_ref[...]) + b_ref[...]
    acted, slope = gelu_parts(hidden)
    acted_ref[...] = acted.astype(BF)
    slope_ref[...] = slope.astype(BF)


def up_rows(normed, weight, bias):
    tokens, width = normed.shape
    cols = weight.shape[1]
    tile = 512
    out = pl.BlockSpec((tokens, tile), lambda n: (0, n))
    return call(
        up_kernel,
        2 * tokens * width * cols,
        2 * (tokens * width + width * cols + 2 * tokens * cols),
        tokens * cols,
        grid=(cols // tile,),
        in_specs=[
            pl.BlockSpec((tokens, width), lambda n: (0, 0)),
            pl.BlockSpec((width, tile), lambda n: (0, n)),
            pl.BlockSpec((1, tile), lambda n: (0, n)),
        ],
        out_specs=[out, out],
        out_shape=[jax.ShapeDtypeStruct((tokens, cols), BF)] * 2,
    )(normed, weight, bias)


def hidden_grad_kernel(g_ref, w_ref, slope_ref, hg_ref, sum_ref, *, skip):
    weight = w_ref[:, skip:].reshape(hg_ref.shape[1], g_ref.shape[1])
    grad = dot_nt(g_ref[...], weight) * slope_ref[...].astype(F32)
    low = grad.astype(BF)
    hg_ref[...] = low
    sum_ref[...] = jnp.sum(low.astype(F32), axis=0, keepdims=True)


def hidden_grads(grad, down, slope):
    tokens, width = grad.shape
    down, skip = down
    groups, deep, _ = down.shape
    cols = slope.shape[1]
    tile = 512
    out = pl.BlockSpec((tokens, tile), lambda n: (0, n))
    if groups == 1:
        weight = pl.BlockSpec((1, tile, width), lambda n: (0, n, 0))
    else:
        weight = pl.BlockSpec((tile // (deep - skip), deep, width), lambda n: (n, 0, 0))
    return call(
        functools.partial(hidden_grad_kernel, skip=skip),
        2 * tokens * width * cols,
        2 * (tokens * width + width * cols + 2 * tokens * cols),
        grid=(cols // tile,),
        in_specs=[pl.BlockSpec((tokens, width), lambda n: (0, 0)), weight, out],
        out_specs=[out, pl.BlockSpec((1, tile), lambda n: (0, n))],
        out_shape=[
            jax.ShapeDtypeStruct((tokens, cols), BF),
            jax.ShapeDtypeStruct((1, cols), F32),
        ],
    )(grad, down, slope)


def norm_parts(values, gain, shift):
    centred = values - jnp.mean(values, axis=-1, keepdims=True)
    inv_dev = lax.rsqrt(jnp.mean(centred * centred, axis=-1, keepdims=True) + EPS)
    normal = centred * inv_dev
    return normal * gain + shift, normal, inv_dev


def norm_back(upstream, normal, inv_dev, gain):
    scaled = upstream * gain
    mean_first = jnp.mean(scaled, axis=-1, keepdims=True)
    mean_second = jnp.mean(scaled * normal, axis=-1, keepdims=True)
    back = inv_dev * (scaled - mean_first - normal * mean_second)
    return back, jnp.sum(upstream * normal, 0), jnp.sum(upstream, 0)


def tie(*trees):
    leaves, form = jax.tree.flatten(trees)
    return jax.tree.unflatten(form, lax.optimization_barrier(tuple(leaves)))


def project_kernel(*refs, parts):
    x_ref, b_ref, scale_ref, shift_ref = refs[:4]
    o_refs, w_refs = refs[4 : 4 + parts], refs[4 + parts : 4 + 2 * parts]
    resid_ref, n_ref, nt_ref = refs[4 + 2 * parts :]
    resid = x_ref[...].astype(F32) + b_ref[...]
    for o, w in zip(o_refs, w_refs):
        resid += dot_nn(o[...], w[...])
    normed, _, _ = norm_parts(resid, scale_ref[...], shift_ref[...])
    resid_ref[...] = resid
    n_ref[...] = normed.astype(BF)
    nt_ref[...] = normed.T.astype(BF)


def project_rows(x, bias, scale, shift, outs, weights):
    tokens, width = x.shape
    rows = min(256, tokens)
    vector = pl.BlockSpec((1, width), lambda i: (0, 0))
    tile = pl.BlockSpec((rows, width), lambda i: (i, 0))
    deep = sum(o.shape[1] for o in outs)
    return call(
        functools.partial(project_kernel, parts=len(outs)),
        2 * tokens * width * deep,
        2 * (tokens * deep + width * deep + 5 * tokens * width),
        grid=(tokens // rows,),
        in_specs=[tile, vector, vector, vector]
        + [pl.BlockSpec((rows, o.shape[1]), lambda i: (i, 0)) for o in outs]
        + [pl.BlockSpec(w.shape, lambda i: (0, 0)) for w in weights],
        out_specs=[tile, tile, pl.BlockSpec((width, rows), lambda i: (0, i))],
        out_shape=[
            jax.ShapeDtypeStruct((tokens, width), F32),
            jax.ShapeDtypeStruct((tokens, width), BF),
            jax.ShapeDtypeStruct((width, tokens), BF),
        ],
    )(x, bias, scale, shift, *outs, *weights)


def down_kernel(r_ref, b_ref, *refs, parts, skips):
    total = r_ref[...] + b_ref[...]
    for a, w, skip in zip(refs[:parts], refs[parts : 2 * parts], skips):
        total += dot_nn(a[...], w[:, skip:].reshape(a.shape[1], w.shape[2]))
    refs[-1][...] = total.astype(BF)


def down_rows(resid, bias, acts, weights):
    tokens, width = resid.shape
    weights, skips = zip(*weights)
    cols = min(512, width)
    tile = pl.BlockSpec((tokens, cols), lambda i: (0, i))
    deep = sum(a.shape[1] for a in acts)
    return call(
        functools.partial(down_kernel, parts=len(acts), skips=skips),
        2 * tokens * width * deep,
        2 * (tokens * deep + width * deep + 3 * tokens * width),
        grid=(width // cols,),
        in_specs=[tile, pl.BlockSpec((1, cols), lambda i: (0, i))]
        + [pl.BlockSpec(a.shape, lambda i: (0, 0)) for a in acts]
        + [pl.BlockSpec((*w.shape[:2], cols), lambda i: (0, 0, i)) for w in weights],
        out_specs=tile,
        out_shape=jax.ShapeDtypeStruct((tokens, width), BF),
    )(resid, bias, *acts, *weights)


def middle_kernel(r_ref, g_ref, scale_ref, *refs, parts):
    branch_ref, sums_ref = refs[-2:]
    upstream = sum(dot_nt(h[...], w[...]) for h, w in zip(refs[:parts], refs[parts : 2 * parts]))
    grad = g_ref[...].astype(F32)
    _, normal, inv_dev = norm_parts(r_ref[...], 1.0, 0.0)
    back, scale_sum, shift_sum = norm_back(upstream, normal, inv_dev, scale_ref[...])
    branch = (grad + back).astype(BF)
    branch_ref[...] = branch
    total = lambda v: jnp.sum(v, axis=0, keepdims=True)
    sums = [scale_sum[None, :], shift_sum[None, :], total(branch.astype(F32)), total(grad)]
    sums = jnp.concatenate(sums + [jnp.zeros((4, grad.shape[1]), F32)], axis=0)

    @pl.when(pl.program_id(0) == 0)
    def _():
        sums_ref[...] = sums

    @pl.when(pl.program_id(0) > 0)
    def _():
        sums_ref[...] += sums


def middle_rows(resid, grad, scale, hidden_gs, weights):
    tokens, width = resid.shape
    rows = min(256, tokens)
    tile = pl.BlockSpec((rows, width), lambda i: (i, 0))
    deep = sum(h.shape[1] for h in hidden_gs)
    return call(
        functools.partial(middle_kernel, parts=len(hidden_gs)),
        2 * tokens * width * deep,
        2 * (tokens * deep + width * deep + 4 * tokens * width),
        grid=(tokens // rows,),
        in_specs=[tile, tile, pl.BlockSpec((1, width), lambda i: (0, 0))]
        + [pl.BlockSpec((rows, h.shape[1]), lambda i: (i, 0)) for h in hidden_gs]
        + [pl.BlockSpec(w.shape, lambda i: (0, 0)) for w in weights],
        out_specs=[tile, pl.BlockSpec((8, width), lambda i: (0, 0))],
        out_shape=[
            jax.ShapeDtypeStruct((tokens, width), BF),
            jax.ShapeDtypeStruct((8, width), F32),
        ],
    )(resid, grad, scale, *hidden_gs, *weights)


def add_parts(total, w_ref, rows_ref, lo):
    cols = rows_ref.shape[1] // 3
    for kind in range(3):
        weight = w_ref[:, kind, :, lo : lo + cols].reshape(total.shape[1], cols)
        total += dot_nt(rows_ref[:, kind * cols : (kind + 1) * cols], weight)
    return total


def early_kernel(*refs):
    w_ref, rows_ref, out_ref = refs[0], refs[1], refs[-1]
    total = refs[2][...] if len(refs) == 4 else jnp.zeros(out_ref.shape, F32)
    out_ref[...] = add_parts(total, w_ref, rows_ref, 0)


def last_kernel(x_ref, g_ref, scale_ref, part_ref, own_ref, rows_ref, in_grad_ref, sums_ref):
    upstream = add_parts(part_ref[...], own_ref, rows_ref, rows_ref.shape[1] // 3)
    _, normal, inv_dev = norm_parts(x_ref[...].astype(F32), 1.0, 0.0)
    back, scale_sum, shift_sum = norm_back(upstream, normal, inv_dev, scale_ref[...])
    in_grad_ref[...] = (g_ref[...].astype(F32) + back).astype(BF)
    sums = [scale_sum[None, :], shift_sum[None, :], jnp.zeros((6, x_ref.shape[1]), F32)]
    sums = jnp.concatenate(sums, axis=0)

    @pl.when(pl.program_id(0) == 0)
    def _():
        sums_ref[...] = sums

    @pl.when(pl.program_id(0) > 0)
    def _():
        sums_ref[...] += sums


def early_rows(weight, rows_grad, *before):
    tokens, deep = rows_grad.shape
    width = weight.shape[0] * weight.shape[2]
    rows = min(512, tokens)
    block = (weight.shape[0], 3, weight.shape[2], deep // 3)
    tile = pl.BlockSpec((rows, width), lambda i: (i, 0))
    return call(
        early_kernel,
        2 * tokens * width * deep,
        2 * (tokens * deep + width * deep + 2 * tokens * width),
        grid=(tokens // rows,),
        in_specs=[
            pl.BlockSpec(block, lambda i: (0, 0, 0, 0)),
            pl.BlockSpec((rows, deep), lambda i: (i, 0)),
        ]
        + [tile for _ in before],
        out_specs=tile,
        out_shape=jax.ShapeDtypeStruct((tokens, width), F32),
    )(weight, rows_grad, *before)


def last_rows(x, branch_grad, scale, partial, own, own_rows):
    tokens, width = x.shape
    deep = own_rows.shape[1]
    rows = min(256, tokens)
    tile = pl.BlockSpec((rows, width), lambda i: (i, 0))
    return call(
        last_kernel,
        2 * tokens * width * deep,
        2 * (tokens * deep + width * deep + 5 * tokens * width),
        grid=(tokens // rows,),
        in_specs=[tile, tile, pl.BlockSpec((1, width), lambda i: (0, 0)), tile]
        + [pl.BlockSpec(own.shape, lambda i: (0, 0, 0, 0)), pl.BlockSpec((rows, deep), lambda i: (i, 0))],
        out_specs=[tile, pl.BlockSpec((8, width), lambda i: (0, 0))],
        out_shape=[
            jax.ShapeDtypeStruct((tokens, width), BF),
            jax.ShapeDtypeStruct((8, width), F32),
        ],
    )(x, branch_grad, scale, partial, own, own_rows)


def unit_kernel(t_ref, nt_ref, c_ref, sa_ref, sb_ref, *refs, chips, parts):
    dq_refs, own_refs, got_refs = refs[:parts], refs[parts : 2 * parts], refs[2 * parts : 3 * parts]
    keep_ref, send_ref, rows_out, sum_ref, acc_ref = refs[3 * parts :]
    kind = pl.program_id(0)
    cols = dq_refs[0].shape[1]
    added = lambda a, b: a[...].astype(F32) + b[...].astype(F32)

    @pl.when(kind == 0)
    def _():
        for u, dq in enumerate(dq_refs):
            rows_out[:, u * cols : (u + 1) * cols] = dq[...]

    @pl.when(kind == 1)
    def _():
        tables = (c_ref[...], sa_ref[...], sb_ref[...])
        for u, (own, got) in enumerate(zip(own_refs, got_refs)):
            total = added(own, got)
            for at in range(0, cols, LANES):
                turned = turn_back(total[:, at : at + LANES], *tables).astype(BF)
                rows_out[:, u * cols + at : u * cols + at + LANES] = turned

    @pl.when(kind == 2)
    def _():
        for u, (own, got) in enumerate(zip(own_refs, got_refs)):
            rows_out[:, u * cols : (u + 1) * cols] = added(own, got).astype(BF)

    rows = rows_out[...]
    acc_ref[...] = dot_nn(nt_ref[...], rows)
    piece = keep_ref.shape[1]
    for place in range(chips):
        for ref, which in ((keep_ref, place), (send_ref, chips + place)):
            at = pl.multiple_of(t_ref[which] * piece, piece)
            ref[place] = acc_ref[pl.ds(at, piece), :].astype(BF)
    sums = jnp.sum(rows.astype(F32), axis=0, keepdims=True)
    sum_ref[...] = jnp.broadcast_to(sums, sum_ref.shape)


def unit_grads(table, normed_t, tables, dqs, owns, gots):
    width, tokens = normed_t.shape
    parts = len(dqs)
    cols = dqs[0].shape[1]
    wide = parts * cols
    chips = table.shape[0] // 2
    piece = width // (2 * chips)
    rotary = pl.BlockSpec((tokens, LANES), lambda i, t: (0, 0))
    part = pl.BlockSpec((tokens, cols), lambda i, t: (0, 0))
    pair = pl.BlockSpec((None, tokens, cols), lambda i, t: (jnp.maximum(i - 1, 0), 0, 0))
    blocks = pl.BlockSpec((chips, None, piece, wide), lambda i, t: (0, i, 0, 0))
    return pl.pallas_call(
        functools.partial(unit_kernel, chips=chips, parts=parts),
        grid_spec=pltpu.PrefetchScalarGridSpec(
            num_scalar_prefetch=1,
            grid=(3,),
            in_specs=[pl.BlockSpec((width, tokens), lambda i, t: (0, 0))]
            + [rotary] * 3
            + [part] * parts
            + [pair] * (2 * parts),
            out_specs=[
                blocks,
                blocks,
                pl.BlockSpec((tokens, wide), lambda i, t: (0, i)),
                pl.BlockSpec((8, wide), lambda i, t: (0, i)),
            ],
            scratch_shapes=[pltpu.VMEM((width, wide), F32)],
        ),
        out_shape=[jax.ShapeDtypeStruct((chips, 3, piece, wide), BF)] * 2
        + [jax.ShapeDtypeStruct((tokens, 3 * wide), BF), jax.ShapeDtypeStruct((8, 3 * wide), F32)],
        compiler_params=pltpu.CompilerParams(vmem_limit_bytes=VMEM_BYTES),
        cost_estimate=pl.CostEstimate(
            flops=6 * tokens * width * wide,
            bytes_accessed=2 * (tokens * width + 8 * tokens * wide + 3 * width * wide),
            transcendentals=0,
        ),
    )(table, normed_t, *tables, *dqs, *owns, *gots)


def widen_kernel(t_ref, a_ref, b_ref, out_ref):
    count, piece, cols = a_ref.shape
    out_ref[:, :cols] = a_ref[...].reshape(out_ref.shape[0], cols).astype(F32)
    for place in range(count):
        rows = pl.ds(pl.multiple_of(t_ref[place] * piece, piece), piece)
        out_ref[rows, cols:] = b_ref[place].astype(F32)


def widen(table, unit_a, unit_b):
    n, _, piece, cols = unit_a.shape
    spec = pl.BlockSpec((n, None, piece, cols), lambda i, t: (0, i, 0, 0))
    return pl.pallas_call(
        widen_kernel,
        grid_spec=pltpu.PrefetchScalarGridSpec(
            num_scalar_prefetch=1,
            grid=(3,),
            in_specs=[spec, spec],
            out_specs=pl.BlockSpec((None, n * piece, 2 * cols), lambda i, t: (i, 0, 0)),
        ),
        out_shape=jax.ShapeDtypeStruct((3, n * piece, 2 * cols), F32),
        compiler_params=pltpu.CompilerParams(vmem_limit_bytes=VMEM_BYTES),
        cost_estimate=pl.CostEstimate(
            flops=0, bytes_accessed=36 * n * piece * cols, transcendentals=0
        ),
    )(table, unit_a, unit_b)


def split_kernel(t_ref, own_m, own_f, oth_m, oth_f, got_om, got_of, got_tm, got_tf, ka, kb, send, *, last):
    total = lambda a, b: (a[...].astype(F32) + b[...].astype(F32)).astype(BF)
    by_y = t_ref[last] == 0
    own_far, oth_me = total(own_f, got_of), total(oth_m, got_tm)
    ka[...] = total(own_m, got_om)
    kb[...] = jnp.where(by_y, own_far, oth_me)
    send[0] = jnp.where(by_y, oth_me, own_far)
    send[1] = total(oth_f, got_tf)


def first_split(table, own, oth, got_own, got_oth):
    chips, piece, cols = got_own.shape
    count = chips // 2
    own, oth = (g.reshape(chips, 2, piece, cols) for g in (own, oth))
    whole = lambda far: pl.BlockSpec(
        (None, None, piece, cols), lambda i, t: (t[far * count + i], t[2 * count], 0, 0)
    )
    part = lambda far: pl.BlockSpec((None, piece, cols), lambda i, t: (t[far * count + i], 0, 0))
    out = pl.BlockSpec((None, piece, cols), lambda i, t: (i, 0, 0))
    return pl.pallas_call(
        functools.partial(split_kernel, last=2 * count),
        grid_spec=pltpu.PrefetchScalarGridSpec(
            num_scalar_prefetch=1,
            grid=(count,),
            in_specs=[whole(0), whole(1)] * 2 + [part(0), part(1)] * 2,
            out_specs=[out, out, pl.BlockSpec((2, None, piece, cols), lambda i, t: (0, i, 0, 0))],
        ),
        out_shape=[jax.ShapeDtypeStruct((count, piece, cols), BF)] * 2
        + [jax.ShapeDtypeStruct((2, count, piece, cols), BF)],
        compiler_params=pltpu.CompilerParams(vmem_limit_bytes=VMEM_BYTES),
        cost_estimate=pl.CostEstimate(
            flops=4 * count * piece * cols, bytes_accessed=24 * count * piece * cols, transcendentals=0
        ),
    )(table, own, own, oth, oth, got_own, got_own, got_oth, got_oth)


class Paired:
    def __init__(self, n_dp):
        self.n_dp = n_dp
        self.me_dp = lax.axis_index("dp")
        self.me_y = lax.axis_index("tensor")
        self.core = self.me_dp % 2
        self.first = self.core * (SEQ // 2)
        chips = n_dp // 2
        levels = chips.bit_length() - 1
        places = np.arange(chips)
        far = sum(((places >> (levels - 1 - k)) & 1) << k for k in range(levels))
        chip = jnp.asarray(far, jnp.int32) ^ (self.me_dp // 2)
        self.blocks = jnp.concatenate([chip * 2 + self.core, chip * 2 + 1 - self.core]).astype(
            jnp.int32
        )

    def move(self, x, to):
        pairs = []
        for dp in range(self.n_dp):
            for y in range(2):
                a, b = to(dp, y)
                if (a, b) != (dp, y):
                    pairs.append((dp * 2 + y, a * 2 + b))
        return lax.ppermute(x, ("dp", "tensor"), pairs)

    def swap(self, rows):
        return self.move(rows, lambda dp, y: (dp - dp % 2 + y, dp % 2))

    def stays(self, rows, got):
        return jnp.where(self.core == self.me_y, rows, got)

    def over_y(self, x):
        return self.move(x, lambda dp, y: (dp, 1 - y))

    def over_core(self, x):
        return self.move(x, lambda dp, y: (dp ^ 1, y))

    def piece(self, own, axis=0):
        rows = own.shape[axis] // self.n_dp
        return lax.dynamic_slice_in_dim(own, self.me_dp * rows, rows, axis)

    def spread(self, got):
        return lax.all_gather(got, "dp", axis=0, tiled=True)

    def core_send(self, half):
        rows, cols = half.shape
        blocks = half.reshape(self.n_dp // 2, 2, rows // self.n_dp, cols)
        return lax.dynamic_index_in_dim(blocks, 1 - self.core, 1, keepdims=False)

    def over_chip(self, x, level):
        return self.move(x, lambda dp, y: (dp ^ (2 << level), y))

    def over_first(self, x):
        return self.move(x, lambda dp, y: (dp ^ 2, y) if dp % 2 else (dp, 1 - y))

    def over_second(self, x):
        return self.move(x, lambda dp, y: (dp, 1 - y) if dp % 2 else (dp ^ 2, y))

    def over_z(self, x, level):
        return self.move(x, lambda dp, y: (dp ^ (4 << level), y))

    def blocks_of(self, x_bit):
        count = self.n_dp // 4
        levels = count.bit_length() - 1
        z = self.me_dp // 4
        places = np.arange(count)
        far = sum(((places >> (levels - 1 - k)) & 1) << k for k in range(levels))
        return (jnp.asarray(far, jnp.int32) ^ z) * 2 + x_bit

    def table(self):
        x = (self.me_dp // 2) % 2
        me, far = self.blocks_of(x), self.blocks_of(1 - x)
        return jnp.concatenate([me, far, jnp.stack([self.core])]).astype(jnp.int32)

    def gather(self, block):
        return lax.all_gather(block[0], "dp", axis=0, tiled=True)

    def reduce_vectors(self, both, own, other):
        k, width = both.shape
        both = both.reshape(k, 2, width // 2)
        take = lambda b: lax.dynamic_index_in_dim(both, b, 1, keepdims=False).reshape(-1)
        mine = jnp.concatenate([take(self.me_y), own]).reshape(-1, LANES)
        theirs = jnp.concatenate([take(1 - self.me_y), other]).reshape(-1, LANES)
        total = jnp.stack([mine, theirs])
        total = total + self.over_core(total)
        for level in range((self.n_dp // 2).bit_length() - 1):
            total = total + self.over_chip(total, level)
        total = (total[0] + self.over_y(total[1])).reshape(-1)
        return total[: k * width // 2].reshape(k, width // 2), total[k * width // 2 :]


class Spread:
    def __init__(self, tokens):
        self.first = lax.axis_index("tensor") * tokens

    def swap_rows(self, rows):
        return rows

    def keys(self, kv):
        return [lax.all_gather(kv, "tensor", axis=0, tiled=True)]

    def keys_back(self, grads):
        return lax.psum_scatter(grads, "tensor", scatter_dimension=1, tiled=True)


def block_step(
    move,
    block_in,
    ln1_scale,
    ln1_shift,
    qkv_ws,
    qkv_bs,
    out_ws,
    out_bias,
    ln2_scale,
    ln2_shift,
    up_ws,
    up_bs,
    down_ws,
    down_bias,
    out_grad,
):
    f32 = lambda v: v.astype(F32)
    tokens = block_in.shape[0]
    tables = rotary_tables(move.first, tokens)
    ln1_gain, ln2_gain = f32(ln1_scale), f32(ln2_scale)
    block_in = move.swap_rows(block_in)
    x_rows = f32(block_in)
    normed1, normal1, inv_one = norm_parts(x_rows, ln1_gain, f32(ln1_shift))
    normed1 = normed1.astype(BF)
    queries, keys, outs, logs = [], [], [], []
    for weight, bias in zip(qkv_ws, qkv_bs):
        split = weight.reshape(1, weight.shape[0], 3, -1).transpose(0, 2, 1, 3)
        q, kv = qkv_rows(normed1, split, f32(bias)[None, :], tables)
        queries.append(q)
        keys.append(move.keys(kv))
    for q, kvs in zip(queries, keys):
        out, log = attend(q, kvs)
        outs.append(out)
        logs.append(log)
    grad_low = move.swap_rows(out_grad)
    grad_rows = f32(grad_low)
    branch_one = sum(dot_nn(o, w) for o, w in zip(outs, out_ws)) + f32(out_bias)
    resid = x_rows + branch_one
    normed2, normal2, inv_two = norm_parts(resid, ln2_gain, f32(ln2_shift))
    normed2 = normed2.astype(BF)
    acts, slopes = [], []
    for weight, bias in zip(up_ws, up_bs):
        acted, slope = up_rows(normed2, weight, f32(bias)[None, :])
        acts.append(acted)
        slopes.append(slope)
    branch_two = sum(dot_nn(a, w) for a, w in zip(acts, down_ws)) + f32(down_bias)
    block_out = move.swap_rows((resid + branch_two).astype(BF))
    down_bias_grad = jnp.sum(grad_rows, 0)
    down_grads = [dot_tn(a, grad_low).astype(BF) for a in acts]
    hidden_gs, up_b_grads = [], []
    for down, slope in zip(down_ws, slopes):
        hg, total = hidden_grads(grad_low, (down[None], 0), slope)
        hidden_gs.append(hg)
        up_b_grads.append(total[0])
    up_grads = [dot_tn(normed2, hg).astype(BF) for hg in hidden_gs]
    normed2_grad = sum(dot_nt(hg, w) for hg, w in zip(hidden_gs, up_ws))
    resid_part, ln2_scale_grad, ln2_shift_grad = norm_back(normed2_grad, normal2, inv_two, ln2_gain)
    resid_grad = grad_rows + resid_part
    branch_grad = resid_grad.astype(BF)
    out_bias_grad = jnp.sum(branch_grad, 0, dtype=F32)
    out_w_grads = [dot_tn(o, branch_grad).astype(BF) for o in outs]
    qkv_w_grads, qkv_b_grads = [], []
    normed1_grad = 0.0
    for q, kvs, out, log, out_w, qkv_w in zip(queries, keys, outs, logs, out_ws, qkv_ws):
        out_g = dot_nt(branch_grad, out_w).astype(BF)
        dq, (dkv,) = attend_back(q, out_g, out, log, kvs, tables)
        dk, dv = move.keys_back(dkv)
        dk = key_sum(dk, jnp.zeros_like(dk), tables)
        qkv_g = jnp.concatenate([dq, dk, dv], axis=1)
        qkv_w_grads.append(dot_tn(normed1, qkv_g).astype(BF))
        qkv_b_grads.append(jnp.sum(qkv_g, 0, dtype=F32))
        normed1_grad = normed1_grad + dot_nt(qkv_g, qkv_w)
    input_part, ln1_scale_grad, ln1_shift_grad = norm_back(normed1_grad, normal1, inv_one, ln1_gain)
    in_grad = move.swap_rows((resid_grad + input_part).astype(BF))
    vectors = [
        ln1_scale_grad,
        ln1_shift_grad,
        out_bias_grad,
        ln2_scale_grad,
        ln2_shift_grad,
        down_bias_grad,
    ]
    return (
        block_out,
        in_grad,
        vectors,
        (qkv_w_grads, out_w_grads, up_grads, down_grads),
        (qkv_b_grads, up_b_grads),
    )


class Reduction:
    def __init__(self, move, table, own, oth):
        self.move, self.table = move, table
        self.grads = own, oth
        self.sends = [move.core_send(g) for g in (own, oth)]
        self.at = 0

    def start(self):
        at = self.at
        if at == 0:
            go = self.move.over_core
        elif at == 1:
            go = self.move.over_first
        elif at == 2:
            go = self.move.over_second
        else:
            go = functools.partial(self.move.over_z, level=at - 3)
        return [go(x) for x in self.sends]

    def take(self, got):
        at, self.at = self.at, self.at + 1
        if at == 0:
            ka, kb, send = first_split(self.table, *self.grads, *got)
            self.keep, self.sends = (ka, kb), [send]
        elif at == 1:
            self.sends = [self.keep[1] + got[0][1]]
            self.keep = self.keep[0] + got[0][0]
        else:
            total = self.keep + got[0]
            half = total.shape[0] // 2
            if half:
                self.keep, self.sends = total[:half], [total[half:]]
            else:
                self.done = total

    @property
    def last(self):
        return 2 + (self.move.n_dp // 4).bit_length() - 1


def beside(compute, inputs, *steps, late=()):
    sends = [s.sends if isinstance(s, Reduction) else s[1] for s in steps]
    inputs, sends, late_sends = tie(inputs, sends, [s[1] for s in late])
    got = []
    for s, x in zip(steps, sends):
        if isinstance(s, Reduction):
            s.sends = x
            got.append(s.start())
        else:
            got.append(s[0](x))
    later = [s[0](x) for s, x in zip(late, late_sends)]
    out = compute(*inputs)
    out, got = tie(out, got)
    moved = []
    for s, x in zip(steps, got):
        if isinstance(s, Reduction):
            s.take(x)
        else:
            moved.append(x)
    return out, moved + later


def paired_device(n_dp, *args):
    (block_in, ln1_scale, ln1_shift, qkv_weight, qkv_bias, out_weight, out_bias) = args[:7]
    (ln2_scale, ln2_shift, up_weight, up_bias, down_weight, down_bias, out_grad) = args[7:]
    move = Paired(n_dp)
    row = lambda v: v.astype(F32)[None, :]
    width, _, part = qkv_weight.shape
    tokens = block_in.shape[0]
    pairs = part // LANES
    half = pairs // 2
    cols = half * LANES
    table = move.table()
    low_product = lambda a, b: dot_tn(a, b).astype(BF)

    block_got = move.swap(block_in)
    qkv_own = jnp.transpose(qkv_weight, (1, 0, 2))
    small = jnp.concatenate([qkv_bias.reshape(3 * part), up_bias])
    out_piece = move.piece(out_weight)
    out_piece = jnp.concatenate([out_piece[:, at : at + part] for at in range(0, width, part)])
    first_piece = jnp.concatenate([move.piece(qkv_own, 1), out_piece[None]])
    first_got = move.over_y(first_piece)
    small_got = move.over_y(small)
    qkv_bs = [row(v[: 3 * part]) for v in (small, small_got)]
    up_bs = [row(v[3 * part :]) for v in (small, small_got)]
    tables = rotary_tables(move.first, tokens)
    qkv_own = qkv_own[None]
    qkv_oth = lax.all_gather(first_got, "dp")
    rest = [move.piece(w) for w in (up_weight, down_weight)]
    stay = jnp.stack([(move.core == move.me_y).astype(jnp.int32)])
    block_in, normed1, normed1_t = norm_rows(
        stay, block_in, block_got, row(ln1_scale), row(ln1_shift)
    )
    (q_own, kv_own), (rest,) = beside(
        lambda n: qkv_rows(n, qkv_own, qkv_bs[0], tables),
        (normed1,),
        (lambda ws: [move.over_y(w) for w in ws], rest),
    )
    kvs_own = [kv_own, move.over_core(kv_own)]
    up_got, down_got = (move.gather(got[None]) for got in rest)
    (out_a, log_a), _ = beside(lambda q, kvs: attend(q, kvs, 0, half), (q_own, kvs_own))
    qkv_oth, out_a, out_grad = tie(qkv_oth, out_a, out_grad)
    q_oth, kv_oth = qkv_rows(normed1, qkv_oth, qkv_bs[1], tables)
    (out_b, log_b), (kv_got, grad_got) = beside(
        lambda q, kvs: attend(q, kvs, half, half),
        (q_own, kvs_own),
        (move.over_core, kv_oth),
        late=[(move.swap, out_grad)],
    )
    kvs_oth = [kv_oth, kv_got]
    (out_oth, log_oth), _ = beside(attend, (q_oth, kvs_oth))
    grad_low = move.stays(out_grad, grad_got)
    out_got = qkv_oth[:, 3].reshape(n_dp, width // part, part // n_dp, part)
    out_got = out_got.transpose(0, 2, 1, 3).reshape(part, width)
    up_ws = [up_weight, up_got]
    down_ws = [(w[None], 0) for w in (down_weight, down_got)]
    outs = [out_a, out_b, out_oth]
    out_ws = [out_weight[:cols], out_weight[cols:], out_got]

    resid, normed2, normed2_t = project_rows(
        block_in, row(out_bias), row(ln2_scale), row(ln2_shift), outs, out_ws
    )
    acts, slopes = zip(*[up_rows(normed2, w, b) for w, b in zip(up_ws, up_bs)])
    block_out = down_rows(resid, row(down_bias), acts, down_ws)
    down_grads, (block_got,) = beside(
        lambda xs, g: [low_product(a, g) for a in xs],
        (acts, grad_low),
        late=[(move.swap, block_out)],
    )
    down = Reduction(move, table, *down_grads)
    (hg_own, up_b_own), _ = beside(
        lambda g, slope: hidden_grads(g, down_ws[0], slope), (grad_low, slopes[0]), down
    )

    def others(g, hg_own):
        hg_oth, up_b_oth = hidden_grads(g, down_ws[1], slopes[1])
        return hg_oth, up_b_oth, [dot_nn(normed2_t, h).astype(BF) for h in (hg_own, hg_oth)]

    (hg_oth, up_b_oth, up_grads), _ = beside(others, (grad_low, hg_own), down)
    up = Reduction(move, table, *up_grads)
    (branch_grad, sums_two), _ = beside(
        lambda *hs: middle_rows(resid, grad_low, row(ln2_scale), hs, up_ws), (hg_own, hg_oth), up, down
    )

    def projected(outs, g):
        own = jnp.concatenate([low_product(o, g) for o in outs[:2]])
        out_w_grads = own, low_product(outs[2], g)
        return out_w_grads, [dot_nt(g, w).astype(BF) for w in out_ws]

    (out_w_grads, out_gs), _ = beside(projected, (outs, branch_grad), down)
    out_gs, block_got = tie(out_gs, block_got)
    proj = Reduction(move, table, *out_w_grads)

    def back(which):
        own = which >= 2
        lo = (which % 2) * half
        q, kvs = (q_own, kvs_own) if own else (q_oth, kvs_oth)
        out, log, grad = (
            (outs[which - 2], (log_a, log_b)[which - 2], out_gs[which - 2])
            if own
            else (out_oth, log_oth, out_gs[2])
        )
        inputs = q, grad, out, log, kvs
        at = 0 if own else lo
        return lambda *xs: attend_back(*xs, tables, lo, half, at), inputs

    def keys_of(x):
        return move.over_core, x[1][1]

    def unit(xs, gots):
        return unit_grads(
            move.blocks, normed1_t, tables, [x[0] for x in xs], [x[1][0] for x in xs], gots
        )

    over_x = functools.partial(move.over_chip, level=0)
    others_z = (8, 4, 12)

    def over_z(parts):
        return [
            move.move(p, lambda dp, y, far=far: (dp ^ far, y)) for p, far in zip(parts, others_z)
        ]

    def z_parts(total):
        return total[:1], [total[n : n + 1] for n in range(1, 4)]

    def halves(total):
        return total[: total.shape[0] // 2], total[total.shape[0] // 2 :]

    oth_a, _ = beside(*back(0), up, down, proj)
    down_block, oth_a = tie(down.done, oth_a)
    down_all = move.gather(down_block)
    oth_b, (got_a,) = beside(*back(1), keys_of(oth_a), up, proj)
    own_a, (got_b,) = beside(*back(2), keys_of(oth_b), up, proj)
    (keep_oth, send, rows_oth, bias_oth), (key_got,) = beside(
        unit, ((oth_a, oth_b), (got_a, got_b)), keys_of(own_a), up, proj
    )
    (keep_a, send_a, rows_a, bias_a), (core_got,) = beside(
        unit, ((own_a,), (key_got,)), (move.over_core, send), proj
    )
    up_block, keep_a, down_all = tie(up.done, keep_a, down_all)
    up_all = move.gather(up_block)
    y_sends = [keep_oth[..., at : at + cols] + core_got[..., at : at + cols] for at in (0, cols)]
    own_b, (core_got_a, y_got_a, y_got_b) = beside(
        *back(3), (move.over_core, send_a), late=[(move.over_y, y) for y in y_sends]
    )
    y_got_a, own_b = tie(y_got_a, own_b)
    keep_a, send_a = halves(keep_a + core_got_a + y_got_a)
    partial, (key_got, a_got) = beside(
        early_rows, (qkv_oth, rows_oth), keys_of(own_b), late=[(over_x, send_a)]
    )
    (keep_b, send_b, rows_b, bias_b), _ = beside(unit, ((own_b,), (key_got,)))
    keep_b, a_got, y_got_b = tie(keep_b, a_got, y_got_b)
    keep_a, send_a = z_parts(keep_a + a_got)
    partial, (core_got, a_got) = beside(
        early_rows, (qkv_own, rows_a, partial), (move.over_core, send_b), (over_z, send_a)
    )
    total_a = keep_a + sum(a_got)
    keep_b, send_b = halves(keep_b + core_got + y_got_b)
    up_all, partial, total_a = tie(up_all, partial, total_a)
    unit_a = lax.all_gather(
        jnp.concatenate([total_a[0], proj.done.reshape(-1, *total_a.shape[2:])]), "dp"
    )
    f32 = lambda v: v.astype(F32)
    (in_grad, sums_one), (b_got,) = beside(
        lambda *xs: last_rows(block_in, branch_grad, row(ln1_scale), *xs),
        (partial, qkv_own, rows_b),
        (over_x, send_b),
    )
    in_grad, block_got, down_all, up_all = tie(in_grad, block_got, down_all, up_all)
    in_grad_got = move.swap(in_grad)
    keep_b, send_b = z_parts(keep_b + b_got)
    b_got = over_z(send_b)
    total_b = keep_b + sum(b_got)
    b_got = over_z([total_b] * 3)
    b_got[0], down_all, up_all = tie(b_got[0], down_all, up_all)
    down_g, up_g = f32(down_all), f32(up_all)
    b_got, down_g, up_g = tie(b_got, down_g, up_g)
    total_b = jnp.concatenate([total_b] + b_got)
    b_got = over_x(total_b)
    block_out = move.stays(block_out, block_got)
    b_got, block_out = tie(b_got, block_out)
    total_b = jnp.concatenate([total_b, b_got])
    (out_g, in_grad), (b_got,) = beside(
        lambda u, rows, got: (f32(u[:, 3:].reshape(part, width)), move.stays(rows, got)),
        (unit_a, in_grad, in_grad_got),
        (move.over_core, total_b),
    )
    total_b = jnp.concatenate([total_b, b_got])
    qkv_g = jnp.transpose(widen(move.blocks, unit_a, total_b), (1, 0, 2))
    side = lambda a, b: jnp.concatenate([a.reshape(3, cols), b.reshape(3, cols)], axis=1).reshape(-1)
    vec, flat = move.reduce_vectors(
        jnp.concatenate([sums_one[:2], sums_two[:4]]),
        jnp.concatenate([side(bias_a[0], bias_b[0]), up_b_own[0]]),
        jnp.concatenate([bias_oth[0], up_b_oth[0]]),
    )
    return (
        block_out,
        in_grad,
        vec[0],
        vec[1],
        qkv_g,
        flat[: 3 * part].reshape(3, part),
        out_g,
        vec[4],
        vec[2],
        vec[3],
        up_g,
        flat[3 * part :],
        down_g,
        vec[5],
    )


def spread_device(*args):
    (block_in, ln1_scale, ln1_shift, qkv_weight, qkv_bias, out_weight, out_bias) = args[:7]
    (ln2_scale, ln2_shift, up_weight, up_bias, down_weight, down_bias, out_grad) = args[7:]
    gather = lambda w, axis: lax.all_gather(w, "tensor", axis=axis, tiled=True)
    scatter = lambda g, axis: lax.psum(
        lax.psum_scatter(g, "tensor", scatter_dimension=axis, tiled=True), "dp"
    ).astype(F32)
    width = qkv_weight.shape[0]
    qkv_all = gather(qkv_weight, 2)
    full = qkv_all.shape[2]
    out = block_step(
        Spread(block_in.shape[0]),
        block_in,
        ln1_scale,
        ln1_shift,
        [qkv_all.reshape(width, 3 * full)],
        [gather(qkv_bias, 1).reshape(3 * full)],
        [gather(out_weight, 0)],
        out_bias,
        ln2_scale,
        ln2_shift,
        [gather(up_weight, 1)],
        [gather(up_bias, 0)],
        [gather(down_weight, 0)],
        down_bias,
        out_grad,
    )
    block_out, in_grad, vectors, weight_grads, (qkv_b, up_b) = out
    ((qkv_g,), (out_g,), (up_g,), (down_g,)) = weight_grads
    vec = scatter(jnp.stack(vectors), 1)
    return (
        block_out,
        in_grad,
        vec[0],
        vec[1],
        scatter(qkv_g.reshape(width, 3, full), 2),
        scatter(qkv_b[0].reshape(3, full), 1),
        scatter(out_g, 0),
        vec[2],
        vec[3],
        vec[4],
        scatter(up_g, 1),
        scatter(up_b[0], 0),
        scatter(down_g, 0),
        vec[5],
    )


def solution(mesh):
    n_dp, n_tensor = mesh.shape["dp"], mesh.shape["tensor"]
    rows = P(("dp", "tensor"), None)
    vector = P("tensor")
    placed = (
        rows,
        P(),
        P(),
        P(None, None, "tensor"),
        P(None, "tensor"),
        P("tensor", None),
        P(),
        P(),
        P(),
        P(None, "tensor"),
        vector,
        P("tensor", None),
        P(),
        rows,
    )
    paired = n_tensor == 2 and n_dp == 16
    return jax.shard_map(
        functools.partial(paired_device, n_dp) if paired else spread_device,
        mesh=mesh,
        in_specs=placed,
        out_specs=(
            rows,
            rows,
            vector,
            vector,
            P(None, None, "tensor"),
            P(None, "tensor"),
            P("tensor", None),
            vector,
            vector,
            vector,
            P(None, "tensor"),
            vector,
            P("tensor", None),
            vector,
        ),
        check_vma=False,
    )
```
